256 devices in a mesh: modes: 16 (over x, y_hi, core), axial: 16 (over z, y_lo).
Axes of the slice: x: 4, y: 4 (y_hi: 2, y_lo: 2; y = y_hi * 2 + y_lo), z: 8, core: 2. Of those that a mesh axis runs over, the one named last changes fastest.
Arguments:
- potential_dual: float32 [512, 512, 128], P('modes', 'axial'), may hold values from -6 to 6
- velocity_dual: float32 [512, 512, 128], P('modes', 'axial'), may hold values from -6 to 6
- diffusivity: float32 [512, 128], P('axial'), may hold values from 0.3 to 1.4
- induct_self: float32 [512, 512, 128], P(None, ('axial', 'modes')), may hold values from -4 to 4
- induct_cross: float32 [512, 512, 128], P(None, ('axial', 'modes')), may hold values from -4 to 4
- lorentz_cross: float32 [512, 512, 128], P(None, ('axial', 'modes')), may hold values from -4 to 4
- advect_self: float32 [512, 512, 128], P(None, ('axial', 'modes')), may hold values from -4 to 4
Outputs:
- potential_grad: float32 [512, 512, 128], P('modes', 'axial')
- velocity_grad: float32 [512, 512, 128], P('modes', 'axial')
The draws below stay inside these ranges and needn't reach their ends.
All inputs are finite; a program needn't handle non-finite values.
Results may differ from the reference program's by a relative error of at most 0.0001.
Values sent between devices are 32-bit elements; how exact they have to be, the bound alone decides.
No kernel may reach another device: no remote copies, remote signals or barrier semaphores. Data moves between devices by JAX's collectives and lax.ppermute only.
A program may use at most 64 MiB of HBM per device.

```python
import math
import jax
import jax.numpy as jnp
from jax import lax

K = 512
NR = 128
STEPS = 4
NZ = 512


def levels(stream_key, shape, cuts, smallest, high):
    def one(dim, parts):
        draws = jax.random.uniform(jax.random.fold_in(jax.random.fold_in(stream_key, 6), dim), (parts,), jnp.float32, smallest / len(cuts), high / len(cuts))
        return jnp.repeat(jnp.exp(draws), shape[dim] // parts).reshape((-1,) + (1,) * (len(shape) - dim - 1))

    gain = one(*cuts[0])
    for cut in cuts[1:]:
        gain = gain * one(*cut)
    return gain


def bell_draw(rng, extent, deviation, reach, split=(), kind=jnp.bfloat16):
    array = jax.random.normal(rng, extent, jnp.float32) * deviation
    if len(split) > 0:
        array = levels(rng, extent, split, -0.22, 0.18) * array
    return jnp.clip(array, min=-reach, max=reach).astype(kind)


def setup_inputs(seed: int = 0) -> dict:
    keys = jax.random.split(jax.random.key(seed), 8)
    return {
        "potential_dual": bell_draw(keys[0], (K, NZ, NR), 1.0, 6.0, ((0, 16), (1, 16)), jnp.float32),
        "velocity_dual": bell_draw(keys[1], (K, NZ, NR), 1.0, 6.0, ((0, 16), (1, 16)), jnp.float32),
        "diffusivity": jnp.clip(jnp.exp(math.log(1.4) - 1.540445 * jax.random.uniform(keys[2], (NZ, NR), jnp.float32) ** levels(keys[2], (NZ, NR), ((0, 16),), -0.2, 0.2)), 0.3, 1.4),
        "induct_self": bell_draw(keys[3], (K, NZ, NR), 1.0, 4.0, ((1, 256),), jnp.float32),
        "induct_cross": bell_draw(keys[4], (K, NZ, NR), 1.0, 4.0, ((1, 256),), jnp.float32),
        "lorentz_cross": bell_draw(keys[5], (K, NZ, NR), 1.0, 4.0, ((1, 256),), jnp.float32),
        "advect_self": bell_draw(keys[6], (K, NZ, NR), 1.0, 4.0, ((1, 256),), jnp.float32),
    }


DT = 0.1

def hartley(count):
    idx = jnp.arange(count, dtype=jnp.int32)
    product = idx[:, None] * idx[None, :] % count
    angle = 2.0 * math.pi / count * product.astype(jnp.float32)
    return (jnp.cos(angle) + jnp.sin(angle)) / math.sqrt(count)

def transform(table, field):
    return jnp.einsum('pk,kzr->pzr', table, field, precision=lax.Precision.HIGHEST)

def apply_op(padded, faces, coeff, mode_sq, radius, radius_face):
    diffs = padded[..., 1:, :] - padded[..., :-1, :]
    flux = faces * diffs
    axial_part = flux[..., 1:, :] - flux[..., :-1, :]
    inner = padded[..., 1:-1, :]
    scaled = inner / radius
    radial_diff = scaled[..., 1:] - scaled[..., :-1]
    face_coeff = 0.5 * (coeff[..., 1:] + coeff[..., :-1]) * radius_face
    radial_flux = face_coeff * radial_diff
    widths = [(0, 0)] * (radial_flux.ndim - 1) + [(1, 1)]
    radial_flux = jnp.pad(radial_flux, widths)
    radial_part = radial_flux[..., 1:] - radial_flux[..., :-1]
    mode_part = coeff * mode_sq / (radius * radius) * inner
    return axial_part + radial_part - mode_part

def reference(potential_dual, velocity_dual, diffusivity, induct_self, induct_cross, lorentz_cross, advect_self):
    table = hartley(K)
    modes = jnp.arange(K, dtype=jnp.int32)
    mode_num = jnp.minimum(modes, K - modes).astype(jnp.float32)
    mode_sq = (mode_num * mode_num).reshape(K, 1, 1)
    radius = NR + jnp.arange(NR, dtype=jnp.int32).astype(jnp.float32) + 0.5
    radius_face = NR + jnp.arange(1, NR, dtype=jnp.int32).astype(jnp.float32)
    ones = jnp.ones_like(diffusivity)
    coeff_pad = jnp.pad(diffusivity, ((1, 1), (0, 0)))
    faces_pot = 0.5 * (coeff_pad[1:] + coeff_pad[:-1])
    ones_pad = jnp.pad(ones, ((1, 1), (0, 0)))
    faces_vel = 0.5 * (ones_pad[1:] + ones_pad[:-1])
    potential = potential_dual
    velocity = velocity_dual
    for step in range(STEPS):
        spatial_pot = transform(table, potential)
        spatial_vel = transform(table, velocity)
        term_pot = induct_self * spatial_pot + induct_cross * spatial_vel
        term_vel = lorentz_cross * spatial_pot + advect_self * spatial_vel
        back_pot = transform(table, term_pot)
        back_vel = transform(table, term_vel)
        padded_pot = jnp.pad(potential, ((0, 0), (1, 1), (0, 0)))
        padded_vel = jnp.pad(velocity, ((0, 0), (1, 1), (0, 0)))
        potential = potential + DT * (apply_op(padded_pot, faces_pot, diffusivity, mode_sq, radius, radius_face) + back_pot)
        velocity = velocity + DT * (apply_op(padded_vel, faces_vel, ones, mode_sq, radius, radius_face) + back_vel)
    return (potential, velocity)
```

```python
import math

import jax
import jax.numpy as jnp
import numpy as np
from jax import lax
from jax.experimental import pallas as pl
from jax.experimental.pallas import tpu as pltpu
from jax.sharding import PartitionSpec as P

K = 512
HALF = K // 2
NR = 128
STEPS = 4
DT = 0.1
PEERS = 16
PER = K // PEERS
AXES = ("modes", "axial")
VMEM_BYTES = 24 * 1024 * 1024
F32 = jnp.float32
BF16 = jnp.bfloat16


def tables():
    idx = np.arange(HALF)

    def cas(rows):
        angle = 2.0 * np.pi / K * ((rows[:, None] * idx[None, :]) % K)
        return ((np.cos(angle) + np.sin(angle)) / math.sqrt(K)).astype(np.float32)

    def split(matrix):
        high = matrix.astype(jnp.bfloat16)
        low = (matrix - high.astype(np.float32)).astype(jnp.bfloat16)
        return np.concatenate([high, high, low], axis=1)

    even, odd = cas(2 * idx), cas(2 * idx + 1)
    return np.stack([split(even), split(odd), split(np.ascontiguousarray(odd.T))])


def call(body, out_shapes, args, flops, scratch=(), smem=0):
    space = [pl.BlockSpec(memory_space=pltpu.SMEM)] * smem
    space += [pl.BlockSpec(memory_space=pltpu.VMEM)] * (len(args) - smem)
    size = sum(math.prod(a.shape) * a.dtype.itemsize for a in list(args) + list(out_shapes))
    return pl.pallas_call(
        body,
        out_shape=out_shapes,
        in_specs=space,
        out_specs=[pl.BlockSpec(memory_space=pltpu.VMEM)] * len(out_shapes),
        scratch_shapes=scratch,
        compiler_params=pltpu.CompilerParams(vmem_limit_bytes=VMEM_BYTES),
        cost_estimate=pl.CostEstimate(flops=flops, bytes_accessed=size, transcendentals=0),
    )(*args)


def pack_kernel(pot_ref, vel_ref, out_ref):
    for dest in range(PEERS):
        for side in range(2):
            plane = 2 * dest + (side if dest % 2 == 0 else 1 - side)
            for field, ref in enumerate((pot_ref, vel_ref)):
                out_ref[dest, side, field] = ref[pl.ds(plane, PER, stride=32), :]


def unpack_kernel(in_ref, pot_ref, vel_ref):
    for src in range(PEERS):
        for side in range(2):
            plane = 2 * src + (side if src % 2 == 0 else 1 - side)
            for field, ref in enumerate((pot_ref, vel_ref)):
                ref[pl.ds(plane, PER, stride=32), :] = in_ref[src, side, field]


def factor_kernel(core_ref, *refs):
    ins, out_ref = refs[:4], refs[4]
    first = jnp.full((HALF, NR), core_ref[0], jnp.int32) == 0
    for which, ref in enumerate(ins):
        for parity in range(2):
            lower = ref[pl.ds(2 * parity, HALF, stride=4), :] * DT
            upper = ref[pl.ds(2 * parity + 1, HALF, stride=4), :] * DT
            rows = pl.ds(parity * HALF, HALF)
            out_ref[which, 0, rows, :] = jnp.where(first, lower, upper)
            out_ref[which, 1, rows, :] = jnp.where(first, upper, lower)


def stacked(value):
    high = value.astype(BF16)
    low = (value - high.astype(F32)).astype(BF16)
    return jnp.concatenate([high, low, high], axis=0)


def product(table, value):
    return jnp.dot(table, stacked(value), preferred_element_type=F32)


def step_kernel(outer_ref, inner_ref, factor_ref, table_ref, coef_ref, out_outer, out_inner):
    sides = (outer_ref, inner_ref)
    lo, hi = pl.ds(0, HALF), pl.ds(HALF, HALF)
    for side, (ref, out_ref) in enumerate(zip(sides, (out_outer, out_inner))):
        low = jnp.concatenate([ref[0, lo, :], ref[1, lo, :]], axis=1)
        high = jnp.concatenate([ref[0, hi, :], ref[1, hi, :]], axis=1)
        terms = []
        for parity, (mixed, rows) in enumerate(((low + high, lo), (low - high, hi))):
            spatial = product(table_ref[parity], mixed)
            pot, vel = spatial[:, :NR], spatial[:, NR:]
            terms.append(
                jnp.concatenate(
                    [
                        factor_ref[0, side, rows, :] * pot + factor_ref[1, side, rows, :] * vel,
                        factor_ref[2, side, rows, :] * pot + factor_ref[3, side, rows, :] * vel,
                    ],
                    axis=1,
                )
            )
        even = product(table_ref[0], terms[0])
        odd = product(table_ref[2], terms[1])
        back = (even + odd, even - odd)
        other = sides[1 - side]
        for half, rows in enumerate((lo, hi)):
            k = lax.broadcasted_iota(jnp.int32, (HALF, NR), 0) + half * HALF
            mode = jnp.minimum(k, K - k).astype(F32)
            mode_sq = mode * mode
            for field in range(2):
                value = ref[field, rows, :]
                coef = lambda row: coef_ref[side, field, pl.ds(row, 1), :]
                out_ref[field, rows, :] = (
                    (coef(0) - coef(1) * mode_sq) * value
                    + coef(2) * pltpu.roll(value, NR - 1, 1)
                    + coef(3) * pltpu.roll(value, 1, 1)
                    + coef(4) * other[field, rows, :]
                    + back[half][:, field * NR : (field + 1) * NR]
                )


def join_kernel(part_outer, part_inner, rim_outer, rim_inner, coef_ref, out_outer, out_inner):
    pairs = ((part_outer, rim_outer, out_outer), (part_inner, rim_inner, out_inner))
    for side, (part, rim, out) in enumerate(pairs):
        for field in range(2):
            out[field] = part[field] + coef_ref[side, field, pl.ds(5, 1), :] * rim[field]


def last_kernel(part_outer, part_inner, rim_outer, rim_inner, coef_ref, out_ref):
    for side, (part, rim) in enumerate(((part_outer, rim_outer), (part_inner, rim_inner))):
        for field in range(2):
            coef = coef_ref[side, field, pl.ds(5, 1), :]
            for dest in range(PEERS):
                rows = pl.ds(dest * PER, PER)
                out_ref[dest, side, field] = part[field, rows, :] + coef * rim[field, rows, :]


def coefficients(diffusivity, core):
    count = lax.axis_size("axial")
    up = [(i, i + 1) for i in range(count - 1)]
    down = [(i + 1, i) for i in range(count - 1)]
    modes, axial = lax.axis_index("modes"), lax.axis_index("axial")
    below = lax.ppermute(diffusivity[-1:], "axial", up)
    above = lax.ppermute(diffusivity[:1], "axial", down)
    rims = jnp.concatenate([below, diffusivity, above], axis=0)
    four = lax.dynamic_slice_in_dim(rims, 2 * modes, 4, axis=0)
    plane = axial * 32 + 2 * modes - 1 + jnp.arange(4)
    ones = jnp.where((plane >= 0) & (plane < 512), 1.0, 0.0).astype(F32)
    ones = jnp.broadcast_to(ones[:, None], (4, NR))
    four = jnp.stack([four, ones], axis=1)
    four = jnp.where(core == 0, four, four[::-1])
    near = four[1:3]
    beyond = 0.5 * (near + jnp.stack([four[0], four[3]]))
    middle = jnp.broadcast_to(0.5 * (four[1:2] + four[2:3]), near.shape)
    radius = NR + jnp.arange(NR, dtype=jnp.int32).astype(F32) + 0.5
    radius_face = NR + jnp.arange(1, NR, dtype=jnp.int32).astype(F32)
    face = 0.5 * (near[..., 1:] + near[..., :-1]) * radius_face
    face = jnp.pad(face, ((0, 0), (0, 0), (1, 1)))
    right = jnp.pad(face[..., 1:-1] / radius[1:], ((0, 0), (0, 0), (0, 1)))
    left = jnp.pad(face[..., 1:-1] / radius[:-1], ((0, 0), (0, 0), (1, 0)))
    own = -(face[..., 1:] + face[..., :-1]) / radius - (beyond + middle)
    rows = [
        1.0 + DT * own,
        DT * near / (radius * radius),
        DT * right,
        DT * left,
        DT * middle,
        DT * beyond,
    ]
    rows += [jnp.zeros_like(near)] * 2
    return jnp.stack(rows, axis=2)


def swaps():
    spot = lambda g: (g % 16) * 16 + g // 16
    inner, outer = [], []
    for g in range(255):
        (inner if g % 2 == 0 else outer).extend([(spot(g), spot(g + 1)), (spot(g + 1), spot(g))])
    return inner, outer


def on_device(pot, vel, diffusivity, *factors):
    shape = jax.ShapeDtypeStruct
    core = lax.rem(lax.axis_index("modes"), 2)
    inner_pairs, outer_pairs = swaps()
    table = jnp.asarray(tables())
    block = shape((PEERS, 2, 2, PER, NR), F32)
    plane = shape((2, K, NR), F32)
    flat = [a.reshape(-1, NR) for a in (pot, vel)]
    (sent,) = call(pack_kernel, [block], flat, 0)
    got = lax.all_to_all(sent, "modes", split_axis=0, concat_axis=0, tiled=True)
    (factor,) = call(
        factor_kernel,
        [shape((4, 2, K, NR), F32)],
        [core.reshape(1).astype(jnp.int32)] + [f.reshape(-1, NR) for f in factors],
        0,
        smem=1,
    )
    coef = coefficients(diffusivity, core)
    outer, inner = (got[:, side].transpose(1, 0, 2, 3).reshape(2, K, NR) for side in range(2))
    for step in range(STEPS):
        rim_outer = lax.ppermute(outer, AXES, outer_pairs)
        rim_inner = lax.ppermute(inner, AXES, inner_pairs)
        parts = call(
            step_kernel, [plane, plane], [outer, inner, factor, table, coef], 8 * 2 * 768 * 256 * 256
        )
        rims = [*parts, rim_outer, rim_inner, coef]
        if step < STEPS - 1:
            outer, inner = call(join_kernel, [plane, plane], rims, 0)
    (sent,) = call(last_kernel, [block], rims, 0)
    got = lax.all_to_all(sent, "modes", split_axis=0, concat_axis=0, tiled=True)
    outs = call(unpack_kernel, [shape((1024, NR), F32)] * 2, [got], 0)
    return tuple(a.reshape(32, 32, NR) for a in outs)


def solution(mesh):
    whole = P(None, ("axial", "modes"), None)
    modal = P("modes", "axial", None)
    return jax.shard_map(
        on_device,
        mesh=mesh,
        in_specs=(modal, modal, P("axial", None), whole, whole, whole, whole),
        out_specs=(modal, modal),
        check_vma=False,
    )
```

```python
import functools
import math

import jax
import jax.numpy as jnp
import numpy as np
from jax import lax
from jax.experimental import pallas as pl
from jax.experimental.pallas import tpu as pltpu
from jax.sharding import PartitionSpec as P

K = 512
HALF = K // 2
NR = 128
STEPS = 4
DT = 0.1
PEERS = 16
PER = K // PEERS
CHUNK = 8
AXES = ("modes", "axial")
VMEM_BYTES = 24 * 1024 * 1024
F32 = jnp.float32
BF16 = jnp.bfloat16


def tables():
    idx = np.arange(HALF)

    def cas(rows):
        angle = 2.0 * np.pi / K * ((rows[:, None] * idx[None, :]) % K)
        return ((np.cos(angle) + np.sin(angle)) / math.sqrt(K)).astype(np.float32)

    def split(matrix):
        high = matrix.astype(jnp.bfloat16)
        low = (matrix - high.astype(np.float32)).astype(jnp.bfloat16)
        return np.concatenate([high, high, low], axis=1)

    even, odd = cas(2 * idx), cas(2 * idx + 1)
    return np.stack([split(even), split(odd), split(np.ascontiguousarray(odd.T))])


def call(body, out_shapes, args, flops, scratch=(), smem=0):
    space = [pl.BlockSpec(memory_space=pltpu.SMEM)] * smem
    space += [pl.BlockSpec(memory_space=pltpu.VMEM)] * (len(args) - smem)
    size = sum(math.prod(a.shape) * a.dtype.itemsize for a in list(args) + list(out_shapes))
    return pl.pallas_call(
        body,
        out_shape=out_shapes,
        in_specs=space,
        out_specs=[pl.BlockSpec(memory_space=pltpu.VMEM)] * len(out_shapes),
        scratch_shapes=scratch,
        compiler_params=pltpu.CompilerParams(vmem_limit_bytes=VMEM_BYTES),
        cost_estimate=pl.CostEstimate(flops=flops, bytes_accessed=size, transcendentals=0),
    )(*args)


def pack_kernel(pot_ref, vel_ref, out_ref):
    for dest in range(PEERS):
        for side in range(2):
            plane = 2 * dest + (side if dest % 2 == 0 else 1 - side)
            for field, ref in enumerate((pot_ref, vel_ref)):
                out_ref[dest, side, field] = ref[pl.ds(plane, CHUNK, stride=32), :]


def unpack_kernel(in_ref, pot_ref, vel_ref):
    for src in range(PEERS):
        for side in range(2):
            plane = 2 * src + (side if src % 2 == 0 else 1 - side)
            for field, ref in enumerate((pot_ref, vel_ref)):
                ref[pl.ds(plane, CHUNK, stride=32), :] = in_ref[src, side, field]


def by_mode(body, out_shapes, args):
    def spec(shape):
        if len(shape) == 2:
            return pl.BlockSpec((CHUNK * 32, NR), lambda i: (i, 0))
        return pl.BlockSpec((PEERS, 2, 2, CHUNK, NR), lambda i: (0, 0, 0, i, 0))

    args = [pltpu.with_memory_space_constraint(a, pltpu.HBM) for a in args]
    return pl.pallas_call(
        body,
        grid=(PER // CHUNK,),
        out_shape=[pltpu.HBM(a.shape, a.dtype) for a in out_shapes],
        in_specs=[spec(a.shape) for a in args],
        out_specs=[spec(a.shape) for a in out_shapes],
        compiler_params=pltpu.CompilerParams(vmem_limit_bytes=VMEM_BYTES),
        cost_estimate=pl.CostEstimate(flops=0, bytes_accessed=1 << 21, transcendentals=0),
    )(*args)


def split_kernel(core_ref, in_ref, diff_ref, out_outer, out_inner):
    for side, out in enumerate((out_outer, out_inner)):
        for src in range(PEERS):
            for field in range(2):
                out[pl.ds(field * K + src * PER, PER), :] = in_ref[src, side, field]
        own = near(core_ref, diff_ref, side)
        row = lax.broadcasted_iota(jnp.int32, (8, NR), 0)
        out[pl.ds(2 * K, 8), :] = jnp.where(row == 0, jnp.broadcast_to(own, (8, NR)), 1.0)


def near(core_ref, diff_ref, side):
    plane = core_ref[1] + (core_ref[0] if side == 0 else 1 - core_ref[0])
    return diff_ref[pl.ds(plane, 1), :]


def factor_kernel(core_ref, diff_ref, *refs):
    ins, out_ref, coef_ref = refs[:4], refs[4], refs[5]
    first = jnp.full((HALF, NR), core_ref[0], jnp.int32) == 0
    for which, ref in enumerate(ins):
        for parity in range(2):
            lower = ref[pl.ds(2 * parity, HALF, stride=4), :] * DT
            upper = ref[pl.ds(2 * parity + 1, HALF, stride=4), :] * DT
            rows = pl.ds(parity * HALF, HALF)
            out_ref[which, 0, rows, :] = jnp.where(first, lower, upper)
            out_ref[which, 1, rows, :] = jnp.where(first, upper, lower)
    tile = (8, NR)
    cell = lax.broadcasted_iota(jnp.int32, tile, 1)
    row = lax.broadcasted_iota(jnp.int32, tile, 0)
    face_radius = (cell + NR).astype(F32)
    radius = face_radius + 0.5
    values = [jnp.broadcast_to(near(core_ref, diff_ref, side), tile) for side in range(2)]
    for field in range(2):
        for side in range(2):
            own = values[side] if field == 0 else jnp.ones(tile, F32)
            middle = 0.5 * (values[0] + values[1]) if field == 0 else own
            face = jnp.where(cell > 0, 0.5 * (pltpu.roll(own, 1, 1) + own) * face_radius, 0.0)
            ahead = pltpu.roll(face, NR - 1, 1)
            terms = (
                1.0 - DT * ((ahead + face) / radius + middle),
                DT * own / (radius * radius),
                DT * ahead / (radius + 1.0),
                DT * face / (radius - 1.0),
                DT * middle,
            )
            total = jnp.zeros(tile, F32)
            for at, term in enumerate(terms):
                total = jnp.where(row == at, term, total)
            coef_ref[side, field] = total


def stacked(value):
    high = value.astype(BF16)
    low = (value - high.astype(F32)).astype(BF16)
    return jnp.concatenate([high, low, high], axis=0)


def product(table, value):
    return jnp.dot(table, stacked(value), preferred_element_type=F32)


def flux(edge_ref, side, field, rim, value, past):
    edge = lambda row: edge_ref[side, pl.ds(row, 1), :]
    beyond = rim if past is None else edge(2) * (rim - past)
    return edge(field) * (beyond - value)


def field_rows(field):
    return pl.ds(field * K, K)


def first_kernel(outer, inner, factor_ref, table_ref, coef_ref, out_outer, out_inner):
    step_alone((outer, inner), factor_ref, table_ref, coef_ref, (out_outer, out_inner))


def next_kernel(opening, *refs):
    refs = list(refs)
    take = lambda n: [refs.pop(0) for _ in range(n)]
    parts, olds, rims = take(2), take(2), take(2)
    pasts, edge_ref = ((None, None), None) if opening else (take(2), take(1)[0])
    factor_ref, table_ref, coef_ref = take(3)
    outs, fulls, fluxes = take(2), take(2), take(2)
    if opening:
        (edge_ref,) = take(1)
        for side in range(2):
            own, other = (ref[pl.ds(2 * K, 8), :] for ref in (olds[side], rims[side]))
            row = lax.broadcasted_iota(jnp.int32, (8, NR), 0)
            edge_ref[side] = jnp.where(row < 2, DT * 0.5 * (own + other), other)
    for side in range(2):
        for field in range(2):
            rows = field_rows(field)
            past = None if opening else pasts[side][rows, :]
            flow = flux(edge_ref, side, field, rims[side][rows, :], olds[side][rows, :], past)
            fluxes[side][rows, :] = flow
            fulls[side][rows, :] = parts[side][rows, :] + flow
    step_alone(fulls, factor_ref, table_ref, coef_ref, outs)


def step_alone(sides, factor_ref, table_ref, coef_ref, outs):
    spans = [[pl.ds(field * K + half * HALF, HALF) for half in range(2)] for field in range(2)]
    for side, (ref, out_ref) in enumerate(zip(sides, outs)):
        low, high = (
            jnp.concatenate([ref[spans[0][half], :], ref[spans[1][half], :]], axis=1)
            for half in range(2)
        )
        terms = []
        for parity, mixed in enumerate((low + high, low - high)):
            spatial = product(table_ref[parity], mixed)
            pot, vel = spatial[:, :NR], spatial[:, NR:]
            rows = pl.ds(parity * HALF, HALF)
            terms.append(
                jnp.concatenate(
                    [
                        factor_ref[0, side, rows, :] * pot + factor_ref[1, side, rows, :] * vel,
                        factor_ref[2, side, rows, :] * pot + factor_ref[3, side, rows, :] * vel,
                    ],
                    axis=1,
                )
            )
        even = product(table_ref[0], terms[0])
        odd = product(table_ref[2], terms[1])
        back = (even + odd, even - odd)
        other = sides[1 - side]
        for half in range(2):
            k = lax.broadcasted_iota(jnp.int32, (HALF, NR), 0) + half * HALF
            mode = jnp.minimum(k, K - k).astype(F32)
            mode_sq = mode * mode
            for field in range(2):
                rows = spans[field][half]
                value = ref[rows, :]
                coef = lambda row: coef_ref[side, field, pl.ds(row, 1), :]
                out_ref[rows, :] = (
                    (coef(0) - coef(1) * mode_sq) * value
                    + coef(2) * pltpu.roll(value, NR - 1, 1)
                    + coef(3) * pltpu.roll(value, 1, 1)
                    + coef(4) * other[rows, :]
                    + back[half][:, field * NR : (field + 1) * NR]
                )


def last_kernel(*refs):
    parts, olds, rims, pasts = (refs[i : i + 2] for i in range(0, 8, 2))
    edge_ref, out_ref = refs[8:]
    for side in range(2):
        for field in range(2):
            for dest in range(PEERS):
                rows = pl.ds(field * K + dest * PER, PER)
                flow = flux(
                    edge_ref, side, field, rims[side][rows, :], olds[side][rows, :], pasts[side][rows, :]
                )
                out_ref[dest, side, field] = parts[side][rows, :] + flow


def swaps():
    spot = lambda g: (g % 16) * 16 + g // 16
    inner, outer = [], []
    for g in range(255):
        (inner if g % 2 == 0 else outer).extend([(spot(g), spot(g + 1)), (spot(g + 1), spot(g))])
    return inner, outer


def on_device(pot, vel, diffusivity, *factors):
    shape = jax.ShapeDtypeStruct
    modes = lax.axis_index("modes").astype(jnp.int32)
    place = jnp.stack([modes % 2, 2 * modes])
    inner_pairs, outer_pairs = swaps()
    table = jnp.asarray(tables())
    block = shape((PEERS, 2, 2, PER, NR), F32)
    plane = shape((2 * K, NR), F32)
    opening = shape((2 * K + 8, NR), F32)
    tiles = shape((2, 2, 8, NR), F32)
    (sent,) = by_mode(pack_kernel, [block], [a.reshape(-1, NR) for a in (pot, vel)])
    sent, factors = lax.optimization_barrier((sent, factors))
    got = lax.all_to_all(sent, "modes", split_axis=0, concat_axis=0, tiled=True)
    factor, coef = call(
        factor_kernel,
        [shape((4, 2, K, NR), F32), tiles],
        [place, diffusivity] + [f.reshape(-1, NR) for f in factors],
        0,
        smem=1,
    )
    got, factor, coef = lax.optimization_barrier((got, factor, coef))
    start = call(split_kernel, [opening] * 2, [place, got, diffusivity], 0, smem=1)
    shared = [factor, table, coef]
    flops = 8 * 2 * 768 * 256 * 256

    def swap(planes):
        return [lax.ppermute(planes[0], AXES, outer_pairs), lax.ppermute(planes[1], AXES, inner_pairs)]

    rims = swap(start)
    parts = call(first_kernel, [plane] * 2, [*start, *shared], flops)
    olds, pasts = start, []
    for step in range(1, STEPS):
        coming = swap(parts)
        outs = call(
            functools.partial(next_kernel, step == 1),
            [plane] * 6 + ([shape((2, 8, NR), F32)] if step == 1 else []),
            [*parts, *olds, *rims, *pasts, *shared],
            flops,
        )
        parts, olds = outs[:2], outs[2:4]
        edge = outs[6] if step == 1 else edge
        pasts, rims = [*outs[4:6], edge], coming
    (sent,) = call(last_kernel, [block], [*parts, *olds, *rims, *pasts], 0)
    got = lax.all_to_all(sent, "modes", split_axis=0, concat_axis=0, tiled=True)
    outs = by_mode(unpack_kernel, [shape((32 * PER, NR), F32)] * 2, [got])
    return tuple(a.reshape(PER, 32, NR) for a in outs)


def solution(mesh):
    whole = P(None, ("axial", "modes"), None)
    modal = P("modes", "axial", None)
    return jax.shard_map(
        on_device,
        mesh=mesh,
        in_specs=(modal, modal, P("axial", None), whole, whole, whole, whole),
        out_specs=(modal, modal),
        check_vma=False,
    )
```

```python
import functools
import math

import jax
import jax.numpy as jnp
import numpy as np
from jax import lax
from jax.experimental import pallas as pl
from jax.experimental.pallas import tpu as pltpu
from jax.sharding import PartitionSpec as P

K = 512
HALF = K // 2
NR = 128
STEPS = 4
DT = 0.1
PEERS = 16
PER = K // PEERS
CHUNK = 8
AXES = ("modes", "axial")
VMEM_BYTES = 24 * 1024 * 1024
F32 = jnp.float32
BF16 = jnp.bfloat16


def tables():
    idx = np.arange(HALF)

    def cas(rows):
        angle = 2.0 * np.pi / K * ((rows[:, None] * idx[None, :]) % K)
        return ((np.cos(angle) + np.sin(angle)) / math.sqrt(K)).astype(np.float32)

    def split(matrix):
        high = matrix.astype(jnp.bfloat16)
        low = (matrix - high.astype(np.float32)).astype(jnp.bfloat16)
        return np.concatenate([high, high, low], axis=1)

    even, odd = cas(2 * idx), cas(2 * idx + 1)
    return np.stack([split(even), split(odd), split(np.ascontiguousarray(odd.T))])


def call(body, out_shapes, args, flops, scratch=(), smem=0):
    space = [pl.BlockSpec(memory_space=pltpu.SMEM)] * smem
    space += [pl.BlockSpec(memory_space=pltpu.VMEM)] * (len(args) - smem)
    size = sum(math.prod(a.shape) * a.dtype.itemsize for a in list(args) + list(out_shapes))
    return pl.pallas_call(
        body,
        out_shape=out_shapes,
        in_specs=space,
        out_specs=[pl.BlockSpec(memory_space=pltpu.VMEM)] * len(out_shapes),
        scratch_shapes=scratch,
        compiler_params=pltpu.CompilerParams(vmem_limit_bytes=VMEM_BYTES),
        cost_estimate=pl.CostEstimate(flops=flops, bytes_accessed=size, transcendentals=0),
    )(*args)


def chunk_rows(chunk):
    return pl.ds(chunk * CHUNK * 32, CHUNK * 32)


def chunk_block(ref, chunk):
    return ref.at[:, :, :, pl.ds(chunk * CHUNK, CHUNK)]


def planes():
    for peer in range(PEERS):
        for side in range(2):
            yield peer, side, 2 * peer + (side if peer % 2 == 0 else 1 - side)


def pack_kernel(pot_ref, vel_ref, out_ref, rows, block, in_sems, out_sems):
    chunks = range(PER // CHUNK)
    arrive = [
        [
            pltpu.make_async_copy(
                ref.at[chunk_rows(chunk)], rows.at[field, chunk_rows(chunk)], in_sems.at[field, chunk]
            )
            for field, ref in enumerate((pot_ref, vel_ref))
        ]
        for chunk in chunks
    ]
    for pair in arrive:
        for copy in pair:
            copy.start()
    leave = []
    for chunk in chunks:
        for field in range(2):
            arrive[chunk][field].wait()
            for peer, side, plane in planes():
                block[peer, side, field, pl.ds(chunk * CHUNK, CHUNK)] = rows[
                    field, pl.ds(chunk * CHUNK * 32 + plane, CHUNK, stride=32), :
                ]
        leave.append(
            pltpu.make_async_copy(chunk_block(block, chunk), chunk_block(out_ref, chunk), out_sems.at[chunk])
        )
        leave[-1].start()
    for copy in leave:
        copy.wait()


def unpack_kernel(in_ref, pot_ref, vel_ref, rows, sems):
    leave = []
    for chunk in range(PER // CHUNK):
        for field, ref in enumerate((pot_ref, vel_ref)):
            for peer, side, plane in planes():
                rows[field, pl.ds(chunk * CHUNK * 32 + plane, CHUNK, stride=32), :] = in_ref[
                    peer, side, field, pl.ds(chunk * CHUNK, CHUNK)
                ]
            leave.append(
                pltpu.make_async_copy(
                    rows.at[field, chunk_rows(chunk)], ref.at[chunk_rows(chunk)], sems.at[field, chunk]
                )
            )
            leave[-1].start()
    for copy in leave:
        copy.wait()


def moved(body, out_shapes, args, in_space, scratch):
    if in_space == pltpu.HBM:
        args = [pltpu.with_memory_space_constraint(a, in_space) for a in args]
    return pl.pallas_call(
        body,
        out_shape=[pltpu.HBM(a.shape, a.dtype) for a in out_shapes],
        in_specs=[pl.BlockSpec(memory_space=in_space)] * len(args),
        out_specs=[pl.BlockSpec(memory_space=pltpu.HBM)] * len(out_shapes),
        scratch_shapes=scratch,
        compiler_params=pltpu.CompilerParams(vmem_limit_bytes=VMEM_BYTES),
        cost_estimate=pl.CostEstimate(flops=0, bytes_accessed=1 << 21, transcendentals=0),
    )(*args)


def split_kernel(core_ref, in_ref, diff_ref, out_outer, out_inner):
    for side, out in enumerate((out_outer, out_inner)):
        for src in range(PEERS):
            for field in range(2):
                out[pl.ds(field * K + src * PER, PER), :] = in_ref[src, side, field]
        own = near(core_ref, diff_ref, side)
        row = lax.broadcasted_iota(jnp.int32, (8, NR), 0)
        out[pl.ds(2 * K, 8), :] = jnp.where(row == 0, jnp.broadcast_to(own, (8, NR)), 1.0)


def near(core_ref, diff_ref, side):
    plane = core_ref[1] + (core_ref[0] if side == 0 else 1 - core_ref[0])
    return diff_ref[pl.ds(plane, 1), :]


def factor_kernel(core_ref, diff_ref, *refs):
    ins, out_ref, coef_ref = refs[:4], refs[4], refs[5]
    first = jnp.full((HALF, NR), core_ref[0], jnp.int32) == 0
    for which, ref in enumerate(ins):
        for parity in range(2):
            lower = ref[pl.ds(2 * parity, HALF, stride=4), :] * DT
            upper = ref[pl.ds(2 * parity + 1, HALF, stride=4), :] * DT
            rows = pl.ds(parity * HALF, HALF)
            out_ref[which, 0, rows, :] = jnp.where(first, lower, upper)
            out_ref[which, 1, rows, :] = jnp.where(first, upper, lower)
    tile = (8, NR)
    cell = lax.broadcasted_iota(jnp.int32, tile, 1)
    row = lax.broadcasted_iota(jnp.int32, tile, 0)
    face_radius = (cell + NR).astype(F32)
    radius = face_radius + 0.5
    values = [jnp.broadcast_to(near(core_ref, diff_ref, side), tile) for side in range(2)]
    for field in range(2):
        for side in range(2):
            own = values[side] if field == 0 else jnp.ones(tile, F32)
            middle = 0.5 * (values[0] + values[1]) if field == 0 else own
            face = jnp.where(cell > 0, 0.5 * (pltpu.roll(own, 1, 1) + own) * face_radius, 0.0)
            ahead = pltpu.roll(face, NR - 1, 1)
            terms = (
                1.0 - DT * ((ahead + face) / radius + middle),
                DT * own / (radius * radius),
                DT * ahead / (radius + 1.0),
                DT * face / (radius - 1.0),
                DT * middle,
            )
            total = jnp.zeros(tile, F32)
            for at, term in enumerate(terms):
                total = jnp.where(row == at, term, total)
            coef_ref[side, field] = total


def stacked(value):
    high = value.astype(BF16)
    low = (value - high.astype(F32)).astype(BF16)
    return jnp.concatenate([high, low, high], axis=0)


def product(table, value):
    return jnp.dot(table, stacked(value), preferred_element_type=F32)


def flux(edge_ref, side, field, rim, value, past):
    edge = lambda row: edge_ref[side, pl.ds(row, 1), :]
    beyond = rim if past is None else edge(2) * (rim - past)
    return edge(field) * (beyond - value)


def field_rows(field):
    return pl.ds(field * K, K)


def first_kernel(outer, inner, factor_ref, table_ref, coef_ref, out_outer, out_inner):
    step_alone((outer, inner), factor_ref, table_ref, coef_ref, (out_outer, out_inner))


def next_kernel(opening, *refs):
    refs = list(refs)
    take = lambda n: [refs.pop(0) for _ in range(n)]
    parts, olds, rims = take(2), take(2), take(2)
    pasts, edge_ref = ((None, None), None) if opening else (take(2), take(1)[0])
    factor_ref, table_ref, coef_ref = take(3)
    outs, fulls, fluxes = take(2), take(2), take(2)
    if opening:
        (edge_ref,) = take(1)
        for side in range(2):
            own, other = (ref[pl.ds(2 * K, 8), :] for ref in (olds[side], rims[side]))
            row = lax.broadcasted_iota(jnp.int32, (8, NR), 0)
            edge_ref[side] = jnp.where(row < 2, DT * 0.5 * (own + other), other)
    for side in range(2):
        for field in range(2):
            rows = field_rows(field)
            past = None if opening else pasts[side][rows, :]
            flow = flux(edge_ref, side, field, rims[side][rows, :], olds[side][rows, :], past)
            fluxes[side][rows, :] = flow
            fulls[side][rows, :] = parts[side][rows, :] + flow
    step_alone(fulls, factor_ref, table_ref, coef_ref, outs)


def step_alone(sides, factor_ref, table_ref, coef_ref, outs):
    spans = [[pl.ds(field * K + half * HALF, HALF) for half in range(2)] for field in range(2)]
    for side, (ref, out_ref) in enumerate(zip(sides, outs)):
        low, high = (
            jnp.concatenate([ref[spans[0][half], :], ref[spans[1][half], :]], axis=1)
            for half in range(2)
        )
        terms = []
        for parity, mixed in enumerate((low + high, low - high)):
            spatial = product(table_ref[parity], mixed)
            pot, vel = spatial[:, :NR], spatial[:, NR:]
            rows = pl.ds(parity * HALF, HALF)
            terms.append(
                jnp.concatenate(
                    [
                        factor_ref[0, side, rows, :] * pot + factor_ref[1, side, rows, :] * vel,
                        factor_ref[2, side, rows, :] * pot + factor_ref[3, side, rows, :] * vel,
                    ],
                    axis=1,
                )
            )
        even = product(table_ref[0], terms[0])
        odd = product(table_ref[2], terms[1])
        back = (even + odd, even - odd)
        other = sides[1 - side]
        for half in range(2):
            k = lax.broadcasted_iota(jnp.int32, (HALF, NR), 0) + half * HALF
            mode = jnp.minimum(k, K - k).astype(F32)
            mode_sq = mode * mode
            for field in range(2):
                rows = spans[field][half]
                value = ref[rows, :]
                coef = lambda row: coef_ref[side, field, pl.ds(row, 1), :]
                out_ref[rows, :] = (
                    (coef(0) - coef(1) * mode_sq) * value
                    + coef(2) * pltpu.roll(value, NR - 1, 1)
                    + coef(3) * pltpu.roll(value, 1, 1)
                    + coef(4) * other[rows, :]
                    + back[half][:, field * NR : (field + 1) * NR]
                )


def last_kernel(*refs):
    parts, olds, rims, pasts = (refs[i : i + 2] for i in range(0, 8, 2))
    edge_ref, out_ref = refs[8:]
    for side in range(2):
        for field in range(2):
            for dest in range(PEERS):
                rows = pl.ds(field * K + dest * PER, PER)
                flow = flux(
                    edge_ref, side, field, rims[side][rows, :], olds[side][rows, :], pasts[side][rows, :]
                )
                out_ref[dest, side, field] = parts[side][rows, :] + flow


def swaps():
    spot = lambda g: (g % 16) * 16 + g // 16
    inner, outer = [], []
    for g in range(255):
        (inner if g % 2 == 0 else outer).extend([(spot(g), spot(g + 1)), (spot(g + 1), spot(g))])
    return inner, outer


def on_device(pot, vel, diffusivity, *factors):
    shape = jax.ShapeDtypeStruct
    modes = lax.axis_index("modes").astype(jnp.int32)
    place = jnp.stack([modes % 2, 2 * modes])
    inner_pairs, outer_pairs = swaps()
    table = jnp.asarray(tables())
    block = shape((PEERS, 2, 2, PER, NR), F32)
    plane = shape((2 * K, NR), F32)
    opening = shape((2 * K + 8, NR), F32)
    tiles = shape((2, 2, 8, NR), F32)
    rows = pltpu.VMEM((2, 32 * PER, NR), F32)
    sems = pltpu.SemaphoreType.DMA((2, PER // CHUNK))
    (sent,) = moved(
        pack_kernel,
        [block],
        [a.reshape(-1, NR) for a in (pot, vel)],
        pltpu.HBM,
        [rows, pltpu.VMEM(block.shape, F32), sems, pltpu.SemaphoreType.DMA((PER // CHUNK,))],
    )
    sent, factors = lax.optimization_barrier((sent, factors))
    got = lax.all_to_all(sent, "modes", split_axis=0, concat_axis=0, tiled=True)
    factor, coef = call(
        factor_kernel,
        [shape((4, 2, K, NR), F32), tiles],
        [place, diffusivity] + [f.reshape(-1, NR) for f in factors],
        0,
        smem=1,
    )
    got, factor, coef = lax.optimization_barrier((got, factor, coef))
    start = call(split_kernel, [opening] * 2, [place, got, diffusivity], 0, smem=1)
    shared = [factor, table, coef]
    flops = 8 * 2 * 768 * 256 * 256

    def swap(planes):
        return [lax.ppermute(planes[0], AXES, outer_pairs), lax.ppermute(planes[1], AXES, inner_pairs)]

    rims = swap(start)
    parts = call(first_kernel, [plane] * 2, [*start, *shared], flops)
    olds, pasts = start, []
    for step in range(1, STEPS):
        coming = swap(parts)
        outs = call(
            functools.partial(next_kernel, step == 1),
            [plane] * 6 + ([shape((2, 8, NR), F32)] if step == 1 else []),
            [*parts, *olds, *rims, *pasts, *shared],
            flops,
        )
        parts, olds = outs[:2], outs[2:4]
        edge = outs[6] if step == 1 else edge
        pasts, rims = [*outs[4:6], edge], coming
    (sent,) = call(last_kernel, [block], [*parts, *olds, *rims, *pasts], 0)
    got = lax.all_to_all(sent, "modes", split_axis=0, concat_axis=0, tiled=True)
    outs = moved(unpack_kernel, [shape((32 * PER, NR), F32)] * 2, [got], pltpu.VMEM, [rows, sems])
    return tuple(a.reshape(PER, 32, NR) for a in outs)


def solution(mesh):
    whole = P(None, ("axial", "modes"), None)
    modal = P("modes", "axial", None)
    return jax.shard_map(
        on_device,
        mesh=mesh,
        in_specs=(modal, modal, P("axial", None), whole, whole, whole, whole),
        out_specs=(modal, modal),
        check_vma=False,
    )
```

```python
import functools
import math

import jax
import jax.numpy as jnp
import numpy as np
from jax import lax
from jax.experimental import pallas as pl
from jax.experimental.pallas import tpu as pltpu
from jax.sharding import PartitionSpec as P

K = 512
HALF = K // 2
NR = 128
STEPS = 4
DT = 0.1
PEERS = 16
PER = K // PEERS
CHUNK = 8
AXES = ("modes", "axial")
VMEM_BYTES = 24 * 1024 * 1024
F32 = jnp.float32
BF16 = jnp.bfloat16


def tables():
    idx = np.arange(HALF)

    def cas(rows):
        angle = 2.0 * np.pi / K * ((rows[:, None] * idx[None, :]) % K)
        return ((np.cos(angle) + np.sin(angle)) / math.sqrt(K)).astype(np.float32)

    def split(matrix):
        high = matrix.astype(jnp.bfloat16)
        low = (matrix - high.astype(np.float32)).astype(jnp.bfloat16)
        return np.concatenate([high, high, low], axis=1)

    even, odd = cas(2 * idx), cas(2 * idx + 1)
    return np.stack([split(even), split(odd), split(np.ascontiguousarray(odd.T))])


def call(body, out_shapes, args, flops, scratch=(), smem=0):
    space = [pl.BlockSpec(memory_space=pltpu.SMEM)] * smem
    space += [pl.BlockSpec(memory_space=pltpu.VMEM)] * (len(args) - smem)
    size = sum(math.prod(a.shape) * a.dtype.itemsize for a in list(args) + list(out_shapes))
    return pl.pallas_call(
        body,
        out_shape=out_shapes,
        in_specs=space,
        out_specs=[pl.BlockSpec(memory_space=pltpu.VMEM)] * len(out_shapes),
        scratch_shapes=scratch,
        compiler_params=pltpu.CompilerParams(vmem_limit_bytes=VMEM_BYTES),
        cost_estimate=pl.CostEstimate(flops=flops, bytes_accessed=size, transcendentals=0),
    )(*args)


def chunk_rows(chunk):
    return pl.ds(chunk * CHUNK * 32, CHUNK * 32)


def planes():
    for peer in range(PEERS):
        for side in range(2):
            yield peer, side, 2 * peer + (side if peer % 2 == 0 else 1 - side)


def pack_kernel(pot_ref, vel_ref, out_ref, rows, sems):
    arrive = [
        [
            pltpu.make_async_copy(
                ref.at[chunk_rows(chunk)], rows.at[field, chunk_rows(chunk)], sems.at[field, chunk]
            )
            for field, ref in enumerate((pot_ref, vel_ref))
        ]
        for chunk in range(PER // CHUNK)
    ]
    for pair in arrive:
        for copy in pair:
            copy.start()
    for chunk, pair in enumerate(arrive):
        for field, copy in enumerate(pair):
            copy.wait()
            for peer, side, plane in planes():
                out_ref[peer, side, field, pl.ds(chunk * CHUNK, CHUNK)] = rows[
                    field, pl.ds(chunk * CHUNK * 32 + plane, CHUNK, stride=32), :
                ]


def unpack_kernel(in_ref, pot_ref, vel_ref, rows, sems):
    leave = []
    for chunk in range(PER // CHUNK):
        for field, ref in enumerate((pot_ref, vel_ref)):
            for peer, side, plane in planes():
                rows[field, pl.ds(chunk * CHUNK * 32 + plane, CHUNK, stride=32), :] = in_ref[
                    peer, side, field, pl.ds(chunk * CHUNK, CHUNK)
                ]
            leave.append(
                pltpu.make_async_copy(
                    rows.at[field, chunk_rows(chunk)], ref.at[chunk_rows(chunk)], sems.at[field, chunk]
                )
            )
            leave[-1].start()
    for copy in leave:
        copy.wait()


def moved(body, out_shapes, args, spaces, scratch):
    if spaces[0] == pltpu.HBM:
        args = [pltpu.with_memory_space_constraint(a, pltpu.HBM) for a in args]
    else:
        out_shapes = [pltpu.HBM(a.shape, a.dtype) for a in out_shapes]
    return pl.pallas_call(
        body,
        out_shape=out_shapes,
        in_specs=[pl.BlockSpec(memory_space=spaces[0])] * len(args),
        out_specs=[pl.BlockSpec(memory_space=spaces[1])] * len(out_shapes),
        scratch_shapes=scratch,
        compiler_params=pltpu.CompilerParams(vmem_limit_bytes=VMEM_BYTES),
        cost_estimate=pl.CostEstimate(flops=0, bytes_accessed=1 << 21, transcendentals=0),
    )(*args)


def split_kernel(core_ref, in_ref, diff_ref, out_outer, out_inner):
    for side, out in enumerate((out_outer, out_inner)):
        for src in range(PEERS):
            for field in range(2):
                out[pl.ds(field * K + src * PER, PER), :] = in_ref[src, side, field]
        own = near(core_ref, diff_ref, side)
        row = lax.broadcasted_iota(jnp.int32, (8, NR), 0)
        out[pl.ds(2 * K, 8), :] = jnp.where(row == 0, jnp.broadcast_to(own, (8, NR)), 1.0)


def near(core_ref, diff_ref, side):
    plane = core_ref[1] + (core_ref[0] if side == 0 else 1 - core_ref[0])
    return diff_ref[pl.ds(plane, 1), :]


def factor_kernel(core_ref, diff_ref, *refs):
    ins, out_ref, coef_ref = refs[:4], refs[4], refs[5]
    first = jnp.full((HALF, NR), core_ref[0], jnp.int32) == 0
    for which, ref in enumerate(ins):
        for parity in range(2):
            lower = ref[pl.ds(2 * parity, HALF, stride=4), :] * DT
            upper = ref[pl.ds(2 * parity + 1, HALF, stride=4), :] * DT
            rows = pl.ds(parity * HALF, HALF)
            out_ref[which, 0, rows, :] = jnp.where(first, lower, upper)
            out_ref[which, 1, rows, :] = jnp.where(first, upper, lower)
    tile = (8, NR)
    cell = lax.broadcasted_iota(jnp.int32, tile, 1)
    row = lax.broadcasted_iota(jnp.int32, tile, 0)
    face_radius = (cell + NR).astype(F32)
    radius = face_radius + 0.5
    values = [jnp.broadcast_to(near(core_ref, diff_ref, side), tile) for side in range(2)]
    for field in range(2):
        for side in range(2):
            own = values[side] if field == 0 else jnp.ones(tile, F32)
            middle = 0.5 * (values[0] + values[1]) if field == 0 else own
            face = jnp.where(cell > 0, 0.5 * (pltpu.roll(own, 1, 1) + own) * face_radius, 0.0)
            ahead = pltpu.roll(face, NR - 1, 1)
            terms = (
                1.0 - DT * ((ahead + face) / radius + middle),
                DT * own / (radius * radius),
                DT * ahead / (radius + 1.0),
                DT * face / (radius - 1.0),
                DT * middle,
            )
            total = jnp.zeros(tile, F32)
            for at, term in enumerate(terms):
                total = jnp.where(row == at, term, total)
            coef_ref[side, field] = total


def stacked(value):
    high = value.astype(BF16)
    low = (value - high.astype(F32)).astype(BF16)
    return jnp.concatenate([high, low, high], axis=0)


def product(table, value):
    return jnp.dot(table, stacked(value), preferred_element_type=F32)


def flux(edge_ref, side, field, rim, value, past):
    edge = lambda row: edge_ref[side, pl.ds(row, 1), :]
    beyond = rim if past is None else edge(2) * (rim - past)
    return edge(field) * (beyond - value)


def field_rows(field):
    return pl.ds(field * K, K)


def first_kernel(outer, inner, factor_ref, table_ref, coef_ref, out_outer, out_inner):
    step_alone((outer, inner), factor_ref, table_ref, coef_ref, (out_outer, out_inner))


def next_kernel(opening, *refs):
    refs = list(refs)
    take = lambda n: [refs.pop(0) for _ in range(n)]
    parts, olds, rims = take(2), take(2), take(2)
    pasts, edge_ref = ((None, None), None) if opening else (take(2), take(1)[0])
    factor_ref, table_ref, coef_ref = take(3)
    outs, fulls, fluxes = take(2), take(2), take(2)
    if opening:
        (edge_ref,) = take(1)
        for side in range(2):
            own, other = (ref[pl.ds(2 * K, 8), :] for ref in (olds[side], rims[side]))
            row = lax.broadcasted_iota(jnp.int32, (8, NR), 0)
            edge_ref[side] = jnp.where(row < 2, DT * 0.5 * (own + other), other)
    for side in range(2):
        for field in range(2):
            rows = field_rows(field)
            past = None if opening else pasts[side][rows, :]
            flow = flux(edge_ref, side, field, rims[side][rows, :], olds[side][rows, :], past)
            fluxes[side][rows, :] = flow
            fulls[side][rows, :] = parts[side][rows, :] + flow
    step_alone(fulls, factor_ref, table_ref, coef_ref, outs)


def step_alone(sides, factor_ref, table_ref, coef_ref, outs):
    spans = [[pl.ds(field * K + half * HALF, HALF) for half in range(2)] for field in range(2)]
    for side, (ref, out_ref) in enumerate(zip(sides, outs)):
        low, high = (
            jnp.concatenate([ref[spans[0][half], :], ref[spans[1][half], :]], axis=1)
            for half in range(2)
        )
        terms = []
        for parity, mixed in enumerate((low + high, low - high)):
            spatial = product(table_ref[parity], mixed)
            pot, vel = spatial[:, :NR], spatial[:, NR:]
            rows = pl.ds(parity * HALF, HALF)
            terms.append(
                jnp.concatenate(
                    [
                        factor_ref[0, side, rows, :] * pot + factor_ref[1, side, rows, :] * vel,
                        factor_ref[2, side, rows, :] * pot + factor_ref[3, side, rows, :] * vel,
                    ],
                    axis=1,
                )
            )
        even = product(table_ref[0], terms[0])
        odd = product(table_ref[2], terms[1])
        back = (even + odd, even - odd)
        other = sides[1 - side]
        for half in range(2):
            k = lax.broadcasted_iota(jnp.int32, (HALF, NR), 0) + half * HALF
            mode = jnp.minimum(k, K - k).astype(F32)
            mode_sq = mode * mode
            for field in range(2):
                rows = spans[field][half]
                value = ref[rows, :]
                coef = lambda row: coef_ref[side, field, pl.ds(row, 1), :]
                out_ref[rows, :] = (
                    (coef(0) - coef(1) * mode_sq) * value
                    + coef(2) * pltpu.roll(value, NR - 1, 1)
                    + coef(3) * pltpu.roll(value, 1, 1)
                    + coef(4) * other[rows, :]
                    + back[half][:, field * NR : (field + 1) * NR]
                )


def last_kernel(*refs):
    parts, olds, rims, pasts = (refs[i : i + 2] for i in range(0, 8, 2))
    edge_ref, out_ref = refs[8:]
    for side in range(2):
        for field in range(2):
            for dest in range(PEERS):
                rows = pl.ds(field * K + dest * PER, PER)
                flow = flux(
                    edge_ref, side, field, rims[side][rows, :], olds[side][rows, :], pasts[side][rows, :]
                )
                out_ref[dest, side, field] = parts[side][rows, :] + flow


def swaps():
    spot = lambda g: (g % 16) * 16 + g // 16
    inner, outer = [], []
    for g in range(255):
        (inner if g % 2 == 0 else outer).extend([(spot(g), spot(g + 1)), (spot(g + 1), spot(g))])
    return inner, outer


def on_device(pot, vel, diffusivity, *factors):
    shape = jax.ShapeDtypeStruct
    modes = lax.axis_index("modes").astype(jnp.int32)
    place = jnp.stack([modes % 2, 2 * modes])
    inner_pairs, outer_pairs = swaps()
    table = jnp.asarray(tables())
    block = shape((PEERS, 2, 2, PER, NR), F32)
    plane = shape((2 * K, NR), F32)
    opening = shape((2 * K + 8, NR), F32)
    tiles = shape((2, 2, 8, NR), F32)
    staging = [pltpu.VMEM((2, 32 * PER, NR), F32), pltpu.SemaphoreType.DMA((2, PER // CHUNK))]

    def swap(planes):
        return [lax.ppermute(planes[0], AXES, outer_pairs), lax.ppermute(planes[1], AXES, inner_pairs)]

    flat = [a.reshape(-1, NR) for a in (pot, vel)]
    (sent,) = moved(pack_kernel, [block], flat, (pltpu.HBM, pltpu.VMEM), staging)
    sent, place = lax.optimization_barrier((sent, place))
    got = lax.all_to_all(sent, "modes", split_axis=0, concat_axis=0, tiled=True)
    got, place, diffusivity, table = lax.optimization_barrier((got, place, diffusivity, table))
    start = call(split_kernel, [opening] * 2, [place, got, diffusivity], 0, smem=1)
    rims = swap(start)
    start, factors = lax.optimization_barrier((start, factors))
    factor, coef = call(
        factor_kernel,
        [shape((4, 2, K, NR), F32), tiles],
        [place, diffusivity] + [f.reshape(-1, NR) for f in factors],
        0,
        smem=1,
    )
    shared = [factor, table, coef]
    flops = 8 * 2 * 768 * 256 * 256
    parts = call(first_kernel, [plane] * 2, [*start, *shared], flops)
    olds, pasts = start, []
    for step in range(1, STEPS):
        coming = swap(parts)
        outs = call(
            functools.partial(next_kernel, step == 1),
            [plane] * 6 + ([shape((2, 8, NR), F32)] if step == 1 else []),
            [*parts, *olds, *rims, *pasts, *shared],
            flops,
        )
        parts, olds = outs[:2], outs[2:4]
        edge = outs[6] if step == 1 else edge
        pasts, rims = [*outs[4:6], edge], coming
    (sent,) = call(last_kernel, [block], [*parts, *olds, *rims, *pasts], 0)
    got = lax.all_to_all(sent, "modes", split_axis=0, concat_axis=0, tiled=True)
    outs = moved(unpack_kernel, [shape((32 * PER, NR), F32)] * 2, [got], (pltpu.VMEM, pltpu.HBM), staging)
    return tuple(a.reshape(PER, 32, NR) for a in outs)


def solution(mesh):
    whole = P(None, ("axial", "modes"), None)
    modal = P("modes", "axial", None)
    return jax.shard_map(
        on_device,
        mesh=mesh,
        in_specs=(modal, modal, P("axial", None), whole, whole, whole, whole),
        out_specs=(modal, modal),
        check_vma=False,
    )
```

```python
import functools
import math

import jax
import jax.numpy as jnp
import numpy as np
from jax import lax
from jax.experimental import pallas as pl
from jax.experimental.pallas import tpu as pltpu
from jax.sharding import PartitionSpec as P

K = 512
HALF = K // 2
NR = 128
STEPS = 4
DT = 0.1
PEERS = 16
PER = K // PEERS
CHUNK = 8
AXES = ("modes", "axial")
VMEM_BYTES = 24 * 1024 * 1024
F32 = jnp.float32
BF16 = jnp.bfloat16


def tables():
    idx = np.arange(HALF)

    def cas(rows):
        angle = 2.0 * np.pi / K * ((rows[:, None] * idx[None, :]) % K)
        return ((np.cos(angle) + np.sin(angle)) / math.sqrt(K)).astype(np.float32)

    def split(matrix):
        high = matrix.astype(jnp.bfloat16)
        low = (matrix - high.astype(np.float32)).astype(jnp.bfloat16)
        return np.concatenate([high, high, low], axis=1)

    even, odd = cas(2 * idx), cas(2 * idx + 1)
    return np.stack([split(even), split(odd), split(np.ascontiguousarray(odd.T))])


def call(body, out_shapes, args, flops, scratch=(), smem=0):
    space = [pl.BlockSpec(memory_space=pltpu.SMEM)] * smem
    space += [pl.BlockSpec(memory_space=pltpu.VMEM)] * (len(args) - smem)
    size = sum(math.prod(a.shape) * a.dtype.itemsize for a in list(args) + list(out_shapes))
    return pl.pallas_call(
        body,
        out_shape=out_shapes,
        in_specs=space,
        out_specs=[pl.BlockSpec(memory_space=pltpu.VMEM)] * len(out_shapes),
        scratch_shapes=scratch,
        compiler_params=pltpu.CompilerParams(vmem_limit_bytes=VMEM_BYTES),
        cost_estimate=pl.CostEstimate(flops=flops, bytes_accessed=size, transcendentals=0),
    )(*args)


def chunk_rows(chunk):
    return pl.ds(chunk * CHUNK * 32, CHUNK * 32)


def planes(sides):
    for peer in range(PEERS):
        order = (0, 1, -1) if peer % 2 == 0 else (1, 0, 2)
        for side in range(sides):
            plane = 2 * peer + order[side]
            yield peer, side, plane if 0 <= plane < 2 * PEERS else None


def pack_kernel(pot_ref, vel_ref, out_ref, rows, sems):
    arrive = [
        [
            pltpu.make_async_copy(
                ref.at[chunk_rows(chunk)], rows.at[field, chunk_rows(chunk)], sems.at[field, chunk]
            )
            for field, ref in enumerate((pot_ref, vel_ref))
        ]
        for chunk in range(PER // CHUNK)
    ]
    for pair in arrive:
        for copy in pair:
            copy.start()
    for chunk, pair in enumerate(arrive):
        for field, copy in enumerate(pair):
            copy.wait()
            for peer, side, plane in planes(3):
                if plane is None:
                    piece = jnp.zeros((CHUNK, NR), F32)
                else:
                    piece = rows[field, pl.ds(chunk * CHUNK * 32 + plane, CHUNK, stride=32), :]
                out_ref[peer, side, field, pl.ds(chunk * CHUNK, CHUNK)] = piece


def unpack_kernel(in_ref, pot_ref, vel_ref, rows, sems):
    leave = []
    for chunk in range(PER // CHUNK):
        for field, ref in enumerate((pot_ref, vel_ref)):
            for peer, side, plane in planes(2):
                rows[field, pl.ds(chunk * CHUNK * 32 + plane, CHUNK, stride=32), :] = in_ref[
                    peer, side, field, pl.ds(chunk * CHUNK, CHUNK)
                ]
            leave.append(
                pltpu.make_async_copy(
                    rows.at[field, chunk_rows(chunk)], ref.at[chunk_rows(chunk)], sems.at[field, chunk]
                )
            )
            leave[-1].start()
    for copy in leave:
        copy.wait()


def moved(body, out_shapes, args, spaces, scratch):
    if spaces[0] == pltpu.HBM:
        args = [pltpu.with_memory_space_constraint(a, pltpu.HBM) for a in args]
    else:
        out_shapes = [pltpu.HBM(a.shape, a.dtype) for a in out_shapes]
    return pl.pallas_call(
        body,
        out_shape=out_shapes,
        in_specs=[pl.BlockSpec(memory_space=spaces[0])] * len(args),
        out_specs=[pl.BlockSpec(memory_space=spaces[1])] * len(out_shapes),
        scratch_shapes=scratch,
        compiler_params=pltpu.CompilerParams(vmem_limit_bytes=VMEM_BYTES),
        cost_estimate=pl.CostEstimate(flops=0, bytes_accessed=1 << 21, transcendentals=0),
    )(*args)


def split_kernel(core_ref, in_ref, diff_ref, *outs):
    row = lax.broadcasted_iota(jnp.int32, (8, NR), 0)
    for side, out in enumerate(outs):
        for src in range(PEERS):
            for field in range(2):
                out[pl.ds(field * K + src * PER, PER), :] = in_ref[src, side, field]
        own = jnp.where(row == 0, jnp.broadcast_to(near(core_ref, diff_ref, side), (8, NR)), 1.0)
        if side == 2:
            own = jnp.where(jnp.full((8, NR), core_ref[2], jnp.int32) == 1, own, 0.0)
        out[pl.ds(2 * K, 8), :] = own


def near(core_ref, diff_ref, side):
    at = (core_ref[0], 1 - core_ref[0], core_ref[3])[side]
    return diff_ref[pl.ds(core_ref[1] + at, 1), :]


def factor_kernel(core_ref, diff_ref, *refs):
    ins, out_ref, coef_ref = refs[:4], refs[4], refs[5]
    first = jnp.full((HALF, NR), core_ref[0], jnp.int32) == 0
    for which, ref in enumerate(ins):
        for parity in range(2):
            lower = ref[pl.ds(2 * parity, HALF, stride=4), :] * DT
            upper = ref[pl.ds(2 * parity + 1, HALF, stride=4), :] * DT
            rows = pl.ds(parity * HALF, HALF)
            out_ref[which, 0, rows, :] = jnp.where(first, lower, upper)
            out_ref[which, 1, rows, :] = jnp.where(first, upper, lower)
    tile = (8, NR)
    cell = lax.broadcasted_iota(jnp.int32, tile, 1)
    row = lax.broadcasted_iota(jnp.int32, tile, 0)
    face_radius = (cell + NR).astype(F32)
    radius = face_radius + 0.5
    values = [jnp.broadcast_to(near(core_ref, diff_ref, side), tile) for side in range(2)]
    for field in range(2):
        for side in range(2):
            own = values[side] if field == 0 else jnp.ones(tile, F32)
            middle = 0.5 * (values[0] + values[1]) if field == 0 else own
            face = jnp.where(cell > 0, 0.5 * (pltpu.roll(own, 1, 1) + own) * face_radius, 0.0)
            ahead = pltpu.roll(face, NR - 1, 1)
            terms = (
                1.0 - DT * ((ahead + face) / radius + middle),
                DT * own / (radius * radius),
                DT * ahead / (radius + 1.0),
                DT * face / (radius - 1.0),
                DT * middle,
            )
            total = jnp.zeros(tile, F32)
            for at, term in enumerate(terms):
                total = jnp.where(row == at, term, total)
            coef_ref[side, field] = total


def stacked(value):
    high = value.astype(BF16)
    low = (value - high.astype(F32)).astype(BF16)
    return jnp.concatenate([high, low, high], axis=0)


def product(table, value):
    return jnp.dot(table, stacked(value), preferred_element_type=F32)


def flux(edge_ref, side, field, rim, value, past):
    edge = lambda row: edge_ref[side, pl.ds(row, 1), :]
    beyond = rim if past is None else edge(2) * (rim - past)
    return edge(field) * (beyond - value)


def field_rows(field):
    return pl.ds(field * K, K)


def first_kernel(outer, inner, factor_ref, table_ref, coef_ref, out_outer, out_inner):
    step_alone((outer, inner), factor_ref, table_ref, coef_ref, (out_outer, out_inner))


def next_kernel(opening, *refs):
    refs = list(refs)
    take = lambda n: [refs.pop(0) for _ in range(n)]
    parts, olds, rims = take(2), take(2), take(2)
    if opening:
        (beyond,) = take(1)
        coming = [lambda rows: rims[0][rows, :] + beyond[rows, :], lambda rows: rims[1][rows, :]]
    else:
        pasts, (edge_ref,) = take(2), take(1)
        coming = [lambda rows, rim=rim: rim[rows, :] for rim in rims]
    factor_ref, table_ref, coef_ref = take(3)
    outs, fulls, fluxes = take(2), take(2), take(2)
    if opening:
        (edge_ref,) = take(1)
        for side in range(2):
            own, other = olds[side][pl.ds(2 * K, 8), :], coming[side](pl.ds(2 * K, 8))
            row = lax.broadcasted_iota(jnp.int32, (8, NR), 0)
            edge_ref[side] = jnp.where(row < 2, DT * 0.5 * (own + other), other)
    for side in range(2):
        for field in range(2):
            rows = field_rows(field)
            past = None if opening else pasts[side][rows, :]
            flow = flux(edge_ref, side, field, coming[side](rows), olds[side][rows, :], past)
            fluxes[side][rows, :] = flow
            fulls[side][rows, :] = parts[side][rows, :] + flow
    step_alone(fulls, factor_ref, table_ref, coef_ref, outs)


def step_alone(sides, factor_ref, table_ref, coef_ref, outs):
    spans = [[pl.ds(field * K + half * HALF, HALF) for half in range(2)] for field in range(2)]
    for side, (ref, out_ref) in enumerate(zip(sides, outs)):
        low, high = (
            jnp.concatenate([ref[spans[0][half], :], ref[spans[1][half], :]], axis=1)
            for half in range(2)
        )
        terms = []
        for parity, mixed in enumerate((low + high, low - high)):
            spatial = product(table_ref[parity], mixed)
            pot, vel = spatial[:, :NR], spatial[:, NR:]
            rows = pl.ds(parity * HALF, HALF)
            terms.append(
                jnp.concatenate(
                    [
                        factor_ref[0, side, rows, :] * pot + factor_ref[1, side, rows, :] * vel,
                        factor_ref[2, side, rows, :] * pot + factor_ref[3, side, rows, :] * vel,
                    ],
                    axis=1,
                )
            )
        even = product(table_ref[0], terms[0])
        odd = product(table_ref[2], terms[1])
        back = (even + odd, even - odd)
        other = sides[1 - side]
        for half in range(2):
            k = lax.broadcasted_iota(jnp.int32, (HALF, NR), 0) + half * HALF
            mode = jnp.minimum(k, K - k).astype(F32)
            mode_sq = mode * mode
            for field in range(2):
                rows = spans[field][half]
                value = ref[rows, :]
                coef = lambda row: coef_ref[side, field, pl.ds(row, 1), :]
                out_ref[rows, :] = (
                    (coef(0) - coef(1) * mode_sq) * value
                    + coef(2) * pltpu.roll(value, NR - 1, 1)
                    + coef(3) * pltpu.roll(value, 1, 1)
                    + coef(4) * other[rows, :]
                    + back[half][:, field * NR : (field + 1) * NR]
                )


def last_kernel(*refs):
    parts, olds, rims, pasts = (refs[i : i + 2] for i in range(0, 8, 2))
    edge_ref, out_ref = refs[8:]
    for side in range(2):
        for field in range(2):
            for dest in range(PEERS):
                rows = pl.ds(field * K + dest * PER, PER)
                flow = flux(
                    edge_ref, side, field, rims[side][rows, :], olds[side][rows, :], pasts[side][rows, :]
                )
                out_ref[dest, side, field] = parts[side][rows, :] + flow


def swaps():
    spot = lambda g: (g % 16) * 16 + g // 16
    inner, outer = [], []
    for g in range(255):
        (inner if g % 2 == 0 else outer).extend([(spot(g), spot(g + 1)), (spot(g + 1), spot(g))])
    slab = [pair for pair in outer if pair[0] % 16 != pair[1] % 16]
    return inner, outer, slab


def on_device(pot, vel, diffusivity, *factors):
    shape = jax.ShapeDtypeStruct
    modes = lax.axis_index("modes").astype(jnp.int32)
    core = modes % 2
    beyond = 2 * modes + 3 * core - 1
    held = (beyond >= 0) & (beyond < 2 * PEERS)
    place = jnp.stack([core, 2 * modes, held.astype(jnp.int32), jnp.where(held, 3 * core - 1, 0)])
    inner_pairs, outer_pairs, slab_pairs = swaps()
    table = jnp.asarray(tables())
    block = shape((PEERS, 2, 2, PER, NR), F32)
    wide = shape((PEERS, 3, 2, PER, NR), F32)
    plane = shape((2 * K, NR), F32)
    opening = shape((2 * K + 8, NR), F32)
    tiles = shape((2, 2, 8, NR), F32)
    staging = [pltpu.VMEM((2, 32 * PER, NR), F32), pltpu.SemaphoreType.DMA((2, PER // CHUNK))]

    def swap(planes):
        return [lax.ppermute(planes[0], AXES, outer_pairs), lax.ppermute(planes[1], AXES, inner_pairs)]

    flat = [a.reshape(-1, NR) for a in (pot, vel)]
    (sent,) = moved(pack_kernel, [wide], flat, (pltpu.HBM, pltpu.VMEM), staging)
    sent, place = lax.optimization_barrier((sent, place))
    got = lax.all_to_all(sent, "modes", split_axis=0, concat_axis=0, tiled=True)
    got, place, diffusivity, table = lax.optimization_barrier((got, place, diffusivity, table))
    *start, beyond = call(split_kernel, [opening] * 3, [place, got, diffusivity], 0, smem=1)
    rims = [lax.ppermute(start[0], AXES, slab_pairs), lax.ppermute(start[1], AXES, inner_pairs)]
    start, factors = lax.optimization_barrier((start, factors))
    factor, coef = call(
        factor_kernel,
        [shape((4, 2, K, NR), F32), tiles],
        [place, diffusivity] + [f.reshape(-1, NR) for f in factors],
        0,
        smem=1,
    )
    shared = [factor, table, coef]
    flops = 8 * 2 * 768 * 256 * 256
    parts = call(first_kernel, [plane] * 2, [*start, *shared], flops)
    olds, pasts = start, [beyond]
    for step in range(1, STEPS):
        coming = swap(parts)
        outs = call(
            functools.partial(next_kernel, step == 1),
            [plane] * 6 + ([shape((2, 8, NR), F32)] if step == 1 else []),
            [*parts, *olds, *rims, *pasts, *shared],
            flops,
        )
        parts, olds = outs[:2], outs[2:4]
        edge = outs[6] if step == 1 else edge
        pasts, rims = [*outs[4:6], edge], coming
    (sent,) = call(last_kernel, [block], [*parts, *olds, *rims, *pasts], 0)
    got = lax.all_to_all(sent, "modes", split_axis=0, concat_axis=0, tiled=True)
    outs = moved(unpack_kernel, [shape((32 * PER, NR), F32)] * 2, [got], (pltpu.VMEM, pltpu.HBM), staging)
    return tuple(a.reshape(PER, 32, NR) for a in outs)


def solution(mesh):
    whole = P(None, ("axial", "modes"), None)
    modal = P("modes", "axial", None)
    return jax.shard_map(
        on_device,
        mesh=mesh,
        in_specs=(modal, modal, P("axial", None), whole, whole, whole, whole),
        out_specs=(modal, modal),
        check_vma=False,
    )
```

```python
import functools
import math

import jax
import jax.numpy as jnp
import numpy as np
from jax import lax
from jax.experimental import pallas as pl
from jax.experimental.pallas import tpu as pltpu
from jax.sharding import PartitionSpec as P

K = 512
HALF = K // 2
NR = 128
STEPS = 4
DT = 0.1
PEERS = 16
PER = K // PEERS
CHUNK = 8
AXES = ("modes", "axial")
VMEM_BYTES = 24 * 1024 * 1024
F32 = jnp.float32
BF16 = jnp.bfloat16


def tables():
    idx = np.arange(HALF)

    def cas(rows):
        angle = 2.0 * np.pi / K * ((rows[:, None] * idx[None, :]) % K)
        return ((np.cos(angle) + np.sin(angle)) / math.sqrt(K)).astype(np.float32)

    def split(matrix):
        high = matrix.astype(jnp.bfloat16)
        low = (matrix - high.astype(np.float32)).astype(jnp.bfloat16)
        return np.concatenate([high, high, low], axis=1)

    even, odd = cas(2 * idx), cas(2 * idx + 1)
    return np.stack([split(even), split(odd), split(np.ascontiguousarray(odd.T))])


def call(body, out_shapes, args, flops, scratch=(), smem=0):
    space = [pl.BlockSpec(memory_space=pltpu.SMEM)] * smem
    space += [pl.BlockSpec(memory_space=pltpu.VMEM)] * (len(args) - smem)
    size = sum(math.prod(a.shape) * a.dtype.itemsize for a in list(args) + list(out_shapes))
    return pl.pallas_call(
        body,
        out_shape=out_shapes,
        in_specs=space,
        out_specs=[pl.BlockSpec(memory_space=pltpu.VMEM)] * len(out_shapes),
        scratch_shapes=scratch,
        compiler_params=pltpu.CompilerParams(vmem_limit_bytes=VMEM_BYTES),
        cost_estimate=pl.CostEstimate(flops=flops, bytes_accessed=size, transcendentals=0),
    )(*args)


def chunk_rows(chunk):
    return pl.ds(chunk * CHUNK * 32, CHUNK * 32)


def planes(sides):
    for peer in range(PEERS):
        order = (0, 1, -1) if peer % 2 == 0 else (1, 0, 2)
        for side in range(sides):
            plane = 2 * peer + order[side]
            yield peer, side, plane if 0 <= plane < 2 * PEERS else None


def pack_kernel(pot_ref, vel_ref, out_ref, rows, sems):
    arrive = [
        [
            pltpu.make_async_copy(
                ref.at[chunk_rows(chunk)], rows.at[field, chunk_rows(chunk)], sems.at[field, chunk]
            )
            for field, ref in enumerate((pot_ref, vel_ref))
        ]
        for chunk in range(PER // CHUNK)
    ]
    for pair in arrive:
        for copy in pair:
            copy.start()
    for chunk, pair in enumerate(arrive):
        for field, copy in enumerate(pair):
            copy.wait()
            for peer, side, plane in planes(2 + field):
                if plane is None:
                    piece = jnp.zeros((CHUNK, NR), F32)
                else:
                    piece = rows[field, pl.ds(chunk * CHUNK * 32 + plane, CHUNK, stride=32), :]
                out_ref[peer, 2 * side + field * (side < 2), pl.ds(chunk * CHUNK, CHUNK)] = piece


def unpack_kernel(in_ref, pot_ref, vel_ref, rows, sems):
    leave = []
    for chunk in range(PER // CHUNK):
        for field, ref in enumerate((pot_ref, vel_ref)):
            for peer, side, plane in planes(2):
                rows[field, pl.ds(chunk * CHUNK * 32 + plane, CHUNK, stride=32), :] = in_ref[
                    peer, side, field, pl.ds(chunk * CHUNK, CHUNK)
                ]
            leave.append(
                pltpu.make_async_copy(
                    rows.at[field, chunk_rows(chunk)], ref.at[chunk_rows(chunk)], sems.at[field, chunk]
                )
            )
            leave[-1].start()
    for copy in leave:
        copy.wait()


def moved(body, out_shapes, args, spaces, scratch):
    if spaces[0] == pltpu.HBM:
        args = [pltpu.with_memory_space_constraint(a, pltpu.HBM) for a in args]
    else:
        out_shapes = [pltpu.HBM(a.shape, a.dtype) for a in out_shapes]
    return pl.pallas_call(
        body,
        out_shape=out_shapes,
        in_specs=[pl.BlockSpec(memory_space=spaces[0])] * len(args),
        out_specs=[pl.BlockSpec(memory_space=spaces[1])] * len(out_shapes),
        scratch_shapes=scratch,
        compiler_params=pltpu.CompilerParams(vmem_limit_bytes=VMEM_BYTES),
        cost_estimate=pl.CostEstimate(flops=0, bytes_accessed=1 << 21, transcendentals=0),
    )(*args)


def split_kernel(core_ref, in_ref, diff_ref, outer, inner, pot_rim, vel_rim, beyond):
    row = lax.broadcasted_iota(jnp.int32, (8, NR), 0)
    for side, out in enumerate((outer, inner)):
        own = jnp.broadcast_to(near(core_ref, diff_ref, side), (8, NR))
        own = jnp.where(row == 0, own, 1.0)
        out[pl.ds(2 * K, 8), :] = own
        if side == 0:
            pot_rim[pl.ds(K, 8), :] = own
        for src in range(PEERS):
            for field in range(2):
                piece = in_ref[src, 2 * side + field]
                out[pl.ds(field * K + src * PER, PER), :] = piece
                if side == 0:
                    (pot_rim, vel_rim)[field][pl.ds(src * PER, PER), :] = piece
    for src in range(PEERS):
        beyond[pl.ds(src * PER, PER), :] = in_ref[src, 4]


def near(core_ref, diff_ref, side):
    plane = core_ref[1] + (core_ref[0] if side == 0 else 1 - core_ref[0])
    return diff_ref[pl.ds(plane, 1), :]


def factor_kernel(core_ref, diff_ref, *refs):
    ins, out_ref, coef_ref = refs[:4], refs[4], refs[5]
    first = jnp.full((HALF, NR), core_ref[0], jnp.int32) == 0
    for which, ref in enumerate(ins):
        for parity in range(2):
            lower = ref[pl.ds(2 * parity, HALF, stride=4), :] * DT
            upper = ref[pl.ds(2 * parity + 1, HALF, stride=4), :] * DT
            rows = pl.ds(parity * HALF, HALF)
            out_ref[which, 0, rows, :] = jnp.where(first, lower, upper)
            out_ref[which, 1, rows, :] = jnp.where(first, upper, lower)
    tile = (8, NR)
    cell = lax.broadcasted_iota(jnp.int32, tile, 1)
    row = lax.broadcasted_iota(jnp.int32, tile, 0)
    face_radius = (cell + NR).astype(F32)
    radius = face_radius + 0.5
    values = [jnp.broadcast_to(near(core_ref, diff_ref, side), tile) for side in range(2)]
    for field in range(2):
        for side in range(2):
            own = values[side] if field == 0 else jnp.ones(tile, F32)
            middle = 0.5 * (values[0] + values[1]) if field == 0 else own
            face = jnp.where(cell > 0, 0.5 * (pltpu.roll(own, 1, 1) + own) * face_radius, 0.0)
            ahead = pltpu.roll(face, NR - 1, 1)
            terms = (
                1.0 - DT * ((ahead + face) / radius + middle),
                DT * own / (radius * radius),
                DT * ahead / (radius + 1.0),
                DT * face / (radius - 1.0),
                DT * middle,
            )
            total = jnp.zeros(tile, F32)
            for at, term in enumerate(terms):
                total = jnp.where(row == at, term, total)
            coef_ref[side, field] = total


def stacked(value):
    high = value.astype(BF16)
    low = (value - high.astype(F32)).astype(BF16)
    return jnp.concatenate([high, low, high], axis=0)


def product(table, value):
    return jnp.dot(table, stacked(value), preferred_element_type=F32)


def flux(edge_ref, side, field, rim, value, past):
    edge = lambda row: edge_ref[side, pl.ds(row, 1), :]
    beyond = rim if past is None else edge(2) * (rim - past)
    return edge(field) * (beyond - value)


def field_rows(field):
    return pl.ds(field * K, K)


def first_kernel(outer, inner, factor_ref, table_ref, coef_ref, out_outer, out_inner):
    step_alone((outer, inner), factor_ref, table_ref, coef_ref, (out_outer, out_inner))


def next_kernel(opening, *refs):
    refs = list(refs)
    take = lambda n: [refs.pop(0) for _ in range(n)]
    parts, olds = take(2), take(2)
    if opening:
        pot_rim, vel_rim, beyond, inner_rim = take(4)
        comings = [
            [pot_rim[pl.ds(0, K), :], vel_rim[...] + beyond[...]],
            [inner_rim[field_rows(field), :] for field in range(2)],
        ]
        others = [pot_rim[pl.ds(K, 8), :], inner_rim[pl.ds(2 * K, 8), :]]
    else:
        rims, pasts, (edge_ref,) = take(2), take(2), take(1)
        comings = [[rim[field_rows(field), :] for field in range(2)] for rim in rims]
    factor_ref, table_ref, coef_ref = take(3)
    outs, fulls, fluxes = take(2), take(2), take(2)
    if opening:
        (edge_ref,) = take(1)
        for side in range(2):
            own, other = olds[side][pl.ds(2 * K, 8), :], others[side]
            row = lax.broadcasted_iota(jnp.int32, (8, NR), 0)
            edge_ref[side] = jnp.where(row < 2, DT * 0.5 * (own + other), other)
    for side in range(2):
        for field in range(2):
            rows = field_rows(field)
            past = None if opening else pasts[side][rows, :]
            flow = flux(edge_ref, side, field, comings[side][field], olds[side][rows, :], past)
            fluxes[side][rows, :] = flow
            fulls[side][rows, :] = parts[side][rows, :] + flow
    step_alone(fulls, factor_ref, table_ref, coef_ref, outs)


def step_alone(sides, factor_ref, table_ref, coef_ref, outs):
    spans = [[pl.ds(field * K + half * HALF, HALF) for half in range(2)] for field in range(2)]
    for side, (ref, out_ref) in enumerate(zip(sides, outs)):
        low, high = (
            jnp.concatenate([ref[spans[0][half], :], ref[spans[1][half], :]], axis=1)
            for half in range(2)
        )
        terms = []
        for parity, mixed in enumerate((low + high, low - high)):
            spatial = product(table_ref[parity], mixed)
            pot, vel = spatial[:, :NR], spatial[:, NR:]
            rows = pl.ds(parity * HALF, HALF)
            terms.append(
                jnp.concatenate(
                    [
                        factor_ref[0, side, rows, :] * pot + factor_ref[1, side, rows, :] * vel,
                        factor_ref[2, side, rows, :] * pot + factor_ref[3, side, rows, :] * vel,
                    ],
                    axis=1,
                )
            )
        even = product(table_ref[0], terms[0])
        odd = product(table_ref[2], terms[1])
        back = (even + odd, even - odd)
        other = sides[1 - side]
        for half in range(2):
            k = lax.broadcasted_iota(jnp.int32, (HALF, NR), 0) + half * HALF
            mode = jnp.minimum(k, K - k).astype(F32)
            mode_sq = mode * mode
            for field in range(2):
                rows = spans[field][half]
                value = ref[rows, :]
                coef = lambda row: coef_ref[side, field, pl.ds(row, 1), :]
                out_ref[rows, :] = (
                    (coef(0) - coef(1) * mode_sq) * value
                    + coef(2) * pltpu.roll(value, NR - 1, 1)
                    + coef(3) * pltpu.roll(value, 1, 1)
                    + coef(4) * other[rows, :]
                    + back[half][:, field * NR : (field + 1) * NR]
                )


def last_kernel(*refs):
    parts, olds, rims, pasts = (refs[i : i + 2] for i in range(0, 8, 2))
    edge_ref, out_ref = refs[8:]
    for side in range(2):
        for field in range(2):
            for dest in range(PEERS):
                rows = pl.ds(field * K + dest * PER, PER)
                flow = flux(
                    edge_ref, side, field, rims[side][rows, :], olds[side][rows, :], pasts[side][rows, :]
                )
                out_ref[dest, side, field] = parts[side][rows, :] + flow


def swaps():
    spot = lambda g: (g % 16) * 16 + g // 16
    inner, outer = [], []
    for g in range(255):
        (inner if g % 2 == 0 else outer).extend([(spot(g), spot(g + 1)), (spot(g + 1), spot(g))])
    slab = [pair for pair in outer if pair[0] % 16 != pair[1] % 16]
    return inner, outer, slab


def on_device(pot, vel, diffusivity, *factors):
    shape = jax.ShapeDtypeStruct
    modes = lax.axis_index("modes").astype(jnp.int32)
    place = jnp.stack([modes % 2, 2 * modes])
    inner_pairs, outer_pairs, slab_pairs = swaps()
    table = jnp.asarray(tables())
    block = shape((PEERS, 2, 2, PER, NR), F32)
    wide = shape((PEERS, 5, PER, NR), F32)
    plane = shape((2 * K, NR), F32)
    opening = shape((2 * K + 8, NR), F32)
    tiles = shape((2, 2, 8, NR), F32)
    staging = [pltpu.VMEM((2, 32 * PER, NR), F32), pltpu.SemaphoreType.DMA((2, PER // CHUNK))]

    def swap(planes):
        return [lax.ppermute(planes[0], AXES, outer_pairs), lax.ppermute(planes[1], AXES, inner_pairs)]

    flat = [a.reshape(-1, NR) for a in (pot, vel)]
    (sent,) = moved(pack_kernel, [wide], flat, (pltpu.HBM, pltpu.VMEM), staging)
    sent, place = lax.optimization_barrier((sent, place))
    got = lax.all_to_all(sent, "modes", split_axis=0, concat_axis=0, tiled=True)
    got, place, diffusivity, table = lax.optimization_barrier((got, place, diffusivity, table))
    *start, pot_rim, vel_rim, beyond = call(
        split_kernel,
        [opening] * 2 + [shape((K + 8, NR), F32)] + [shape((K, NR), F32)] * 2,
        [place, got, diffusivity],
        0,
        smem=1,
    )
    rims = [
        lax.ppermute(pot_rim, AXES, outer_pairs),
        lax.ppermute(vel_rim, AXES, slab_pairs),
        beyond,
        lax.ppermute(start[1], AXES, inner_pairs),
    ]
    start, factors = lax.optimization_barrier((start, factors))
    factor, coef = call(
        factor_kernel,
        [shape((4, 2, K, NR), F32), tiles],
        [place, diffusivity] + [f.reshape(-1, NR) for f in factors],
        0,
        smem=1,
    )
    shared = [factor, table, coef]
    flops = 1 << 34
    parts = call(first_kernel, [plane] * 2, [*start, *shared], flops)
    olds, pasts = start, []
    for step in range(1, STEPS):
        coming = swap(parts)
        outs = call(
            functools.partial(next_kernel, step == 1),
            [plane] * 6 + ([shape((2, 8, NR), F32)] if step == 1 else []),
            [*parts, *olds, *rims, *pasts, *shared],
            flops,
        )
        parts, olds = outs[:2], outs[2:4]
        edge = outs[6] if step == 1 else edge
        pasts, rims = [*outs[4:6], edge], coming
    (sent,) = call(last_kernel, [block], [*parts, *olds, *rims, *pasts], 0)
    got = lax.all_to_all(sent, "modes", split_axis=0, concat_axis=0, tiled=True)
    outs = moved(unpack_kernel, [shape((32 * PER, NR), F32)] * 2, [got], (pltpu.VMEM, pltpu.HBM), staging)
    return tuple(a.reshape(PER, 32, NR) for a in outs)


def solution(mesh):
    whole = P(None, ("axial", "modes"), None)
    modal = P("modes", "axial", None)
    return jax.shard_map(
        on_device,
        mesh=mesh,
        in_specs=(modal, modal, P("axial", None), whole, whole, whole, whole),
        out_specs=(modal, modal),
        check_vma=False,
    )
```

```python
import functools
import math

import jax
import jax.numpy as jnp
import numpy as np
from jax import lax
from jax.experimental import pallas as pl
from jax.experimental.pallas import tpu as pltpu
from jax.sharding import PartitionSpec as P

K = 512
HALF = K // 2
NR = 128
STEPS = 4
DT = 0.1
PEERS = 16
PER = K // PEERS
CHUNK = 8
AXES = ("modes", "axial")
VMEM_BYTES = 24 * 1024 * 1024
F32 = jnp.float32
BF16 = jnp.bfloat16


def tables():
    idx = np.arange(HALF)

    def cas(rows):
        angle = 2.0 * np.pi / K * ((rows[:, None] * idx[None, :]) % K)
        return ((np.cos(angle) + np.sin(angle)) / math.sqrt(K)).astype(np.float32)

    def split(matrix):
        high = matrix.astype(jnp.bfloat16)
        low = (matrix - high.astype(np.float32)).astype(jnp.bfloat16)
        return np.concatenate([high, high, low], axis=1)

    even, odd = cas(2 * idx), cas(2 * idx + 1)
    return np.stack([split(even), split(odd), split(np.ascontiguousarray(odd.T))])


def call(body, out_shapes, args, flops, scratch=(), smem=0):
    space = [pl.BlockSpec(memory_space=pltpu.SMEM)] * smem
    space += [pl.BlockSpec(memory_space=pltpu.VMEM)] * (len(args) - smem)
    size = sum(math.prod(a.shape) * a.dtype.itemsize for a in list(args) + list(out_shapes))
    return pl.pallas_call(
        body,
        out_shape=out_shapes,
        in_specs=space,
        out_specs=[pl.BlockSpec(memory_space=pltpu.VMEM)] * len(out_shapes),
        scratch_shapes=scratch,
        compiler_params=pltpu.CompilerParams(vmem_limit_bytes=VMEM_BYTES),
        cost_estimate=pl.CostEstimate(flops=flops, bytes_accessed=size, transcendentals=0),
    )(*args)


def chunk_rows(chunk):
    return pl.ds(chunk * CHUNK * 32, CHUNK * 32)


def planes(sides):
    for peer in range(PEERS):
        order = (0, 1, -1) if peer % 2 == 0 else (1, 0, 2)
        for side in range(sides):
            plane = 2 * peer + order[side]
            yield peer, side, plane if 0 <= plane < 2 * PEERS else None


def pack_kernel(pot_ref, vel_ref, out_ref, rows, sems):
    arrive = [
        [
            pltpu.make_async_copy(
                ref.at[chunk_rows(chunk)], rows.at[field, chunk_rows(chunk)], sems.at[field, chunk]
            )
            for field, ref in enumerate((pot_ref, vel_ref))
        ]
        for chunk in range(PER // CHUNK)
    ]
    for pair in arrive:
        for copy in pair:
            copy.start()
    for chunk, pair in enumerate(arrive):
        for field, copy in enumerate(pair):
            copy.wait()
            for peer, side, plane in planes(2 + field):
                if plane is None:
                    piece = jnp.zeros((CHUNK, NR), F32)
                else:
                    piece = rows[field, pl.ds(chunk * CHUNK * 32 + plane, CHUNK, stride=32), :]
                out_ref[peer, 2 * side + field * (side < 2), pl.ds(chunk * CHUNK, CHUNK)] = piece


def unpack_kernel(in_ref, pot_ref, vel_ref, rows, sems):
    leave = []
    for chunk in range(PER // CHUNK):
        for field, ref in enumerate((pot_ref, vel_ref)):
            for peer, side, plane in planes(2):
                rows[field, pl.ds(chunk * CHUNK * 32 + plane, CHUNK, stride=32), :] = in_ref[
                    peer, side, field, pl.ds(chunk * CHUNK, CHUNK)
                ]
            leave.append(
                pltpu.make_async_copy(
                    rows.at[field, chunk_rows(chunk)], ref.at[chunk_rows(chunk)], sems.at[field, chunk]
                )
            )
            leave[-1].start()
    for copy in leave:
        copy.wait()


def moved(body, out_shapes, args, spaces, scratch):
    if spaces[0] == pltpu.HBM:
        args = [pltpu.with_memory_space_constraint(a, pltpu.HBM) for a in args]
    else:
        out_shapes = [pltpu.HBM(a.shape, a.dtype) for a in out_shapes]
    return pl.pallas_call(
        body,
        out_shape=out_shapes,
        in_specs=[pl.BlockSpec(memory_space=spaces[0])] * len(args),
        out_specs=[pl.BlockSpec(memory_space=spaces[1])] * len(out_shapes),
        scratch_shapes=scratch,
        compiler_params=pltpu.CompilerParams(vmem_limit_bytes=VMEM_BYTES),
        cost_estimate=pl.CostEstimate(flops=0, bytes_accessed=1 << 21, transcendentals=0),
    )(*args)


def split_kernel(core_ref, in_ref, diff_ref, outer, inner, pot_rim, beyond):
    row = lax.broadcasted_iota(jnp.int32, (8, NR), 0)
    for side, out in enumerate((outer, inner)):
        own = jnp.broadcast_to(near(core_ref, diff_ref, side), (8, NR))
        own = jnp.where(row == 0, own, 1.0)
        out[pl.ds(2 * K, 8), :] = own
        if side == 0:
            pot_rim[pl.ds(K, 8), :] = own
        else:
            out[pl.ds(2 * K + 8, 8), :] = own
        for src in range(PEERS):
            for field in range(2):
                piece = in_ref[src, 2 * side + field]
                out[pl.ds(field * K + src * PER, PER), :] = piece
                if side == 0 and field == 0:
                    pot_rim[pl.ds(src * PER, PER), :] = piece
    for src in range(PEERS):
        beyond[pl.ds(src * PER, PER), :] = in_ref[src, 4]


def near(core_ref, diff_ref, side):
    plane = core_ref[1] + (core_ref[0] if side == 0 else 1 - core_ref[0])
    return diff_ref[pl.ds(plane, 1), :]


def factor_kernel(core_ref, diff_ref, *refs):
    ins, out_ref, coef_ref = refs[:4], refs[4], refs[5]
    first = jnp.full((HALF, NR), core_ref[0], jnp.int32) == 0
    for which, ref in enumerate(ins):
        for parity in range(2):
            lower = ref[pl.ds(2 * parity, HALF, stride=4), :] * DT
            upper = ref[pl.ds(2 * parity + 1, HALF, stride=4), :] * DT
            rows = pl.ds(parity * HALF, HALF)
            out_ref[which, 0, rows, :] = jnp.where(first, lower, upper)
            out_ref[which, 1, rows, :] = jnp.where(first, upper, lower)
    tile = (8, NR)
    cell = lax.broadcasted_iota(jnp.int32, tile, 1)
    row = lax.broadcasted_iota(jnp.int32, tile, 0)
    face_radius = (cell + NR).astype(F32)
    radius = face_radius + 0.5
    values = [jnp.broadcast_to(near(core_ref, diff_ref, side), tile) for side in range(2)]
    for field in range(2):
        for side in range(2):
            own = values[side] if field == 0 else jnp.ones(tile, F32)
            middle = 0.5 * (values[0] + values[1]) if field == 0 else own
            face = jnp.where(cell > 0, 0.5 * (pltpu.roll(own, 1, 1) + own) * face_radius, 0.0)
            ahead = pltpu.roll(face, NR - 1, 1)
            terms = (
                1.0 - DT * ((ahead + face) / radius + middle),
                DT * own / (radius * radius),
                DT * ahead / (radius + 1.0),
                DT * face / (radius - 1.0),
                DT * middle,
            )
            total = jnp.zeros(tile, F32)
            for at, term in enumerate(terms):
                total = jnp.where(row == at, term, total)
            coef_ref[side, field] = total


def stacked(value):
    high = value.astype(BF16)
    low = (value - high.astype(F32)).astype(BF16)
    return jnp.concatenate([high, low, high], axis=0)


def product(table, value):
    return jnp.dot(table, stacked(value), preferred_element_type=F32)


def flux(edge_ref, side, field, rim, value, past):
    edge = lambda row: edge_ref[side, pl.ds(row, 1), :]
    beyond = rim if past is None else edge(2) * (rim - past)
    return edge(field) * (beyond - value)


def field_rows(field):
    return pl.ds(field * K, K)


def first_kernel(outer, inner, factor_ref, table_ref, coef_ref, out_outer, out_inner):
    step_alone((outer, inner), factor_ref, table_ref, coef_ref, (out_outer, out_inner))


def next_kernel(opening, *refs):
    refs = list(refs)
    take = lambda n: [refs.pop(0) for _ in range(n)]
    parts, olds = take(2), take(2)
    if opening:
        pot_rim, slab_rim, beyond, inner_rim = take(4)
        comings = [
            [slab_rim[field_rows(0), :] + pot_rim[pl.ds(0, K), :], slab_rim[field_rows(1), :] + beyond[...]],
            [inner_rim[field_rows(field), :] for field in range(2)],
        ]
        ends = pl.ds(2 * K, 8)
        others = [slab_rim[ends, :] + pot_rim[pl.ds(K, 8), :], inner_rim[ends, :]]
    else:
        rims, pasts, (edge_ref,) = take(2), take(2), take(1)
        comings = [[rim[field_rows(field), :] for field in range(2)] for rim in rims]
    factor_ref, table_ref, coef_ref = take(3)
    outs, fulls, fluxes = take(2), take(2), take(2)
    if opening:
        (edge_ref,) = take(1)
        for side in range(2):
            own, other = olds[side][pl.ds(2 * K, 8), :], others[side]
            row = lax.broadcasted_iota(jnp.int32, (8, NR), 0)
            edge_ref[side] = jnp.where(row < 2, DT * 0.5 * (own + other), other)
    for side in range(2):
        for field in range(2):
            rows = field_rows(field)
            past = None if opening else pasts[side][rows, :]
            flow = flux(edge_ref, side, field, comings[side][field], olds[side][rows, :], past)
            fluxes[side][rows, :] = flow
            fulls[side][rows, :] = parts[side][rows, :] + flow
    step_alone(fulls, factor_ref, table_ref, coef_ref, outs)


def step_alone(sides, factor_ref, table_ref, coef_ref, outs):
    spans = [[pl.ds(field * K + half * HALF, HALF) for half in range(2)] for field in range(2)]
    for side, (ref, out_ref) in enumerate(zip(sides, outs)):
        low, high = (
            jnp.concatenate([ref[spans[0][half], :], ref[spans[1][half], :]], axis=1)
            for half in range(2)
        )
        terms = []
        for parity, mixed in enumerate((low + high, low - high)):
            spatial = product(table_ref[parity], mixed)
            pot, vel = spatial[:, :NR], spatial[:, NR:]
            rows = pl.ds(parity * HALF, HALF)
            terms.append(
                jnp.concatenate(
                    [
                        factor_ref[0, side, rows, :] * pot + factor_ref[1, side, rows, :] * vel,
                        factor_ref[2, side, rows, :] * pot + factor_ref[3, side, rows, :] * vel,
                    ],
                    axis=1,
                )
            )
        even = product(table_ref[0], terms[0])
        odd = product(table_ref[2], terms[1])
        back = (even + odd, even - odd)
        other = sides[1 - side]
        for half in range(2):
            k = lax.broadcasted_iota(jnp.int32, (HALF, NR), 0) + half * HALF
            mode = jnp.minimum(k, K - k).astype(F32)
            mode_sq = mode * mode
            for field in range(2):
                rows = spans[field][half]
                value = ref[rows, :]
                coef = lambda row: coef_ref[side, field, pl.ds(row, 1), :]
                out_ref[rows, :] = (
                    (coef(0) - coef(1) * mode_sq) * value
                    + coef(2) * pltpu.roll(value, NR - 1, 1)
                    + coef(3) * pltpu.roll(value, 1, 1)
                    + coef(4) * other[rows, :]
                    + back[half][:, field * NR : (field + 1) * NR]
                )


def last_kernel(*refs):
    parts, olds, rims, pasts = (refs[i : i + 2] for i in range(0, 8, 2))
    edge_ref, out_ref = refs[8:]
    for side in range(2):
        for field in range(2):
            for dest in range(PEERS):
                rows = pl.ds(field * K + dest * PER, PER)
                flow = flux(
                    edge_ref, side, field, rims[side][rows, :], olds[side][rows, :], pasts[side][rows, :]
                )
                out_ref[dest, side, field] = parts[side][rows, :] + flow


def swaps():
    spot = lambda g: (g % 16) * 16 + g // 16
    inner, outer = [], []
    for g in range(255):
        (inner if g % 2 == 0 else outer).extend([(spot(g), spot(g + 1)), (spot(g + 1), spot(g))])
    slab = [pair for pair in outer if pair[0] % 16 != pair[1] % 16]
    return inner, outer, slab


def on_device(pot, vel, diffusivity, *factors):
    shape = jax.ShapeDtypeStruct
    modes = lax.axis_index("modes").astype(jnp.int32)
    place = jnp.stack([modes % 2, 2 * modes])
    inner_pairs, outer_pairs, slab_pairs = swaps()
    table = jnp.asarray(tables())
    block = shape((PEERS, 2, 2, PER, NR), F32)
    wide = shape((PEERS, 5, PER, NR), F32)
    plane = shape((2 * K, NR), F32)
    tiles = shape((2, 2, 8, NR), F32)
    staging = [pltpu.VMEM((2, 32 * PER, NR), F32), pltpu.SemaphoreType.DMA((2, PER // CHUNK))]

    def swap(planes):
        return [lax.ppermute(planes[0], AXES, outer_pairs), lax.ppermute(planes[1], AXES, inner_pairs)]

    flat = [a.reshape(-1, NR) for a in (pot, vel)]
    (sent,) = moved(pack_kernel, [wide], flat, (pltpu.HBM, pltpu.VMEM), staging)
    sent, place = lax.optimization_barrier((sent, place))
    got = lax.all_to_all(sent, "modes", split_axis=0, concat_axis=0, tiled=True)
    got, place, diffusivity, table = lax.optimization_barrier((got, place, diffusivity, table))
    *start, pot_rim, beyond = call(
        split_kernel,
        [shape((2 * K + rows, NR), F32) for rows in (8, 16)] + [shape((K + 8, NR), F32), shape((K, NR), F32)],
        [place, got, diffusivity],
        0,
        smem=1,
    )
    rims = [
        lax.ppermute(pot_rim, AXES, [pair for pair in outer_pairs if pair not in slab_pairs]),
        lax.ppermute(start[0], AXES, slab_pairs),
        beyond,
        lax.ppermute(start[1], AXES, inner_pairs),
    ]
    start, factors = lax.optimization_barrier((start, factors))
    factor, coef = call(
        factor_kernel,
        [shape((4, 2, K, NR), F32), tiles],
        [place, diffusivity] + [f.reshape(-1, NR) for f in factors],
        0,
        smem=1,
    )
    shared = [factor, table, coef]
    flops = 1 << 34
    parts = call(first_kernel, [plane] * 2, [*start, *shared], flops)
    olds, pasts = start, []
    for step in range(1, STEPS):
        coming = swap(parts)
        outs = call(
            functools.partial(next_kernel, step == 1),
            [plane] * 6 + ([shape((2, 8, NR), F32)] if step == 1 else []),
            [*parts, *olds, *rims, *pasts, *shared],
            flops,
        )
        parts, olds = outs[:2], outs[2:4]
        edge = outs[6] if step == 1 else edge
        pasts, rims = [*outs[4:6], edge], coming
    (sent,) = call(last_kernel, [block], [*parts, *olds, *rims, *pasts], 0)
    got = lax.all_to_all(sent, "modes", split_axis=0, concat_axis=0, tiled=True)
    outs = moved(unpack_kernel, [shape((32 * PER, NR), F32)] * 2, [got], (pltpu.VMEM, pltpu.HBM), staging)
    return tuple(a.reshape(PER, 32, NR) for a in outs)


def solution(mesh):
    whole = P(None, ("axial", "modes"), None)
    modal = P("modes", "axial", None)
    return jax.shard_map(
        on_device,
        mesh=mesh,
        in_specs=(modal, modal, P("axial", None), whole, whole, whole, whole),
        out_specs=(modal, modal),
        check_vma=False,
    )
```

```python
import functools
import math

import jax
import jax.numpy as jnp
import numpy as np
from jax import lax
from jax.experimental import pallas as pl
from jax.experimental.pallas import tpu as pltpu
from jax.sharding import PartitionSpec as P

K = 512
HALF = K // 2
NR = 128
STEPS = 4
DT = 0.1
PEERS = 16
PER = K // PEERS
CHUNK = 8
AXES = ("modes", "axial")
VMEM_BYTES = 24 * 1024 * 1024
F32 = jnp.float32
BF16 = jnp.bfloat16


def tables():
    idx = np.arange(HALF)

    def cas(rows):
        angle = 2.0 * np.pi / K * ((rows[:, None] * idx[None, :]) % K)
        return ((np.cos(angle) + np.sin(angle)) / math.sqrt(K)).astype(np.float32)

    def split(matrix):
        high = matrix.astype(jnp.bfloat16)
        low = (matrix - high.astype(np.float32)).astype(jnp.bfloat16)
        return np.concatenate([high, high, low], axis=1)

    even, odd = cas(2 * idx), cas(2 * idx + 1)
    return np.stack([split(even), split(odd), split(np.ascontiguousarray(odd.T))])


def call(body, out_shapes, args, flops, scratch=(), smem=0):
    space = [pl.BlockSpec(memory_space=pltpu.SMEM)] * smem
    space += [pl.BlockSpec(memory_space=pltpu.VMEM)] * (len(args) - smem)
    size = sum(math.prod(a.shape) * a.dtype.itemsize for a in list(args) + list(out_shapes))
    return pl.pallas_call(
        body,
        out_shape=out_shapes,
        in_specs=space,
        out_specs=[pl.BlockSpec(memory_space=pltpu.VMEM)] * len(out_shapes),
        scratch_shapes=scratch,
        compiler_params=pltpu.CompilerParams(vmem_limit_bytes=VMEM_BYTES),
        cost_estimate=pl.CostEstimate(flops=flops, bytes_accessed=size, transcendentals=0),
    )(*args)


def chunk_rows(chunk):
    return pl.ds(chunk * CHUNK * 32, CHUNK * 32)


def planes():
    for peer in range(PEERS):
        for side in range(2):
            yield peer, side, 2 * peer + (side if peer % 2 == 0 else 1 - side)


def pack_kernel(pot_ref, vel_ref, out_ref, rows, sems):
    arrive = [
        [
            pltpu.make_async_copy(
                ref.at[chunk_rows(chunk)], rows.at[field, chunk_rows(chunk)], sems.at[field, chunk]
            )
            for field, ref in enumerate((pot_ref, vel_ref))
        ]
        for chunk in range(PER // CHUNK)
    ]
    for pair in arrive:
        for copy in pair:
            copy.start()
    for chunk, pair in enumerate(arrive):
        for field, copy in enumerate(pair):
            copy.wait()
            for peer, side, plane in planes():
                out_ref[peer, side, field, pl.ds(chunk * CHUNK, CHUNK)] = rows[
                    field, pl.ds(chunk * CHUNK * 32 + plane, CHUNK, stride=32), :
                ]


def unpack_kernel(in_ref, diff_ref, pot_ref, vel_ref, rows, sems):
    leave = []
    for chunk in range(PER // CHUNK):
        modes = pl.ds(chunk * CHUNK, CHUNK)
        for field, ref in enumerate((pot_ref, vel_ref)):
            flows = {}
            for left in range(1, PEERS - 1, 2):
                pair = diff_ref[pl.ds(2 * left + 1, 1), :] + diff_ref[pl.ds(2 * left + 2, 1), :]
                coef = DT * 0.5 * pair if field == 0 else DT
                flow = coef * (in_ref[left + 1, 4 + field, modes] - in_ref[left, 4 + field, modes])
                flows[left], flows[left + 1] = flow, -flow
            for peer, side, plane in planes():
                value = in_ref[peer, 2 * side + field, modes]
                if side == 0 and peer in flows:
                    value = value + flows[peer]
                rows[field, pl.ds(chunk * CHUNK * 32 + plane, CHUNK, stride=32), :] = value
            leave.append(
                pltpu.make_async_copy(
                    rows.at[field, chunk_rows(chunk)], ref.at[chunk_rows(chunk)], sems.at[field, chunk]
                )
            )
            leave[-1].start()
    for copy in leave:
        copy.wait()


def moved(body, out_shapes, args, spaces, scratch):
    if spaces[0] == pltpu.HBM:
        args = [pltpu.with_memory_space_constraint(a, pltpu.HBM) for a in args]
    else:
        out_shapes = [pltpu.HBM(a.shape, a.dtype) for a in out_shapes]
    return pl.pallas_call(
        body,
        out_shape=out_shapes,
        in_specs=[pl.BlockSpec(memory_space=spaces[0])] * len(args),
        out_specs=[pl.BlockSpec(memory_space=spaces[1])] * len(out_shapes),
        scratch_shapes=scratch,
        compiler_params=pltpu.CompilerParams(vmem_limit_bytes=VMEM_BYTES),
        cost_estimate=pl.CostEstimate(flops=0, bytes_accessed=1 << 21, transcendentals=0),
    )(*args)


def split_kernel(core_ref, in_ref, diff_ref, out_outer, out_inner):
    for side, out in enumerate((out_outer, out_inner)):
        for src in range(PEERS):
            for field in range(2):
                out[pl.ds(field * K + src * PER, PER), :] = in_ref[src, side, field]
        own = near(core_ref, diff_ref, side)
        row = lax.broadcasted_iota(jnp.int32, (8, NR), 0)
        held = jnp.full((8, NR), core_ref[2], jnp.int32).astype(F32)
        ends = jnp.where(row == 3, held, 1.0)
        out[pl.ds(2 * K, 8), :] = jnp.where(row == 0, jnp.broadcast_to(own, (8, NR)), ends)


def near(core_ref, diff_ref, side):
    plane = core_ref[1] + (core_ref[0] if side == 0 else 1 - core_ref[0])
    return diff_ref[pl.ds(plane, 1), :]


def factor_kernel(core_ref, diff_ref, *refs):
    ins, out_ref, coef_ref = refs[:4], refs[4], refs[5]
    first = jnp.full((HALF, NR), core_ref[0], jnp.int32) == 0
    for which, ref in enumerate(ins):
        for parity in range(2):
            lower = ref[pl.ds(2 * parity, HALF, stride=4), :] * DT
            upper = ref[pl.ds(2 * parity + 1, HALF, stride=4), :] * DT
            rows = pl.ds(parity * HALF, HALF)
            out_ref[which, 0, rows, :] = jnp.where(first, lower, upper)
            out_ref[which, 1, rows, :] = jnp.where(first, upper, lower)
    tile = (8, NR)
    cell = lax.broadcasted_iota(jnp.int32, tile, 1)
    row = lax.broadcasted_iota(jnp.int32, tile, 0)
    face_radius = (cell + NR).astype(F32)
    radius = face_radius + 0.5
    values = [jnp.broadcast_to(near(core_ref, diff_ref, side), tile) for side in range(2)]
    for field in range(2):
        for side in range(2):
            own = values[side] if field == 0 else jnp.ones(tile, F32)
            middle = 0.5 * (values[0] + values[1]) if field == 0 else own
            face = jnp.where(cell > 0, 0.5 * (pltpu.roll(own, 1, 1) + own) * face_radius, 0.0)
            ahead = pltpu.roll(face, NR - 1, 1)
            terms = (
                1.0 - DT * ((ahead + face) / radius + middle),
                DT * own / (radius * radius),
                DT * ahead / (radius + 1.0),
                DT * face / (radius - 1.0),
                DT * middle,
            )
            total = jnp.zeros(tile, F32)
            for at, term in enumerate(terms):
                total = jnp.where(row == at, term, total)
            coef_ref[side, field] = total


def stacked(value):
    high = value.astype(BF16)
    low = (value - high.astype(F32)).astype(BF16)
    return jnp.concatenate([high, low, high], axis=0)


def product(table, value):
    return jnp.dot(table, stacked(value), preferred_element_type=F32)


def flux(edge_ref, side, field, rim, value, past):
    edge = lambda row: edge_ref[side, pl.ds(row, 1), :]
    beyond = rim if past is None else edge(2) * (rim - past)
    return edge(field) * (beyond - value)


def field_rows(field):
    return pl.ds(field * K, K)


def first_kernel(outer, inner, factor_ref, table_ref, coef_ref, out_outer, out_inner):
    step_alone((outer, inner), factor_ref, table_ref, coef_ref, (out_outer, out_inner))


def next_kernel(opening, *refs):
    refs = list(refs)
    take = lambda n: [refs.pop(0) for _ in range(n)]
    parts, olds, rims = take(2), take(2), take(2)
    pasts, edge_ref = ((None, None), None) if opening else (take(2), take(1)[0])
    factor_ref, table_ref, coef_ref = take(3)
    outs, fulls, fluxes = take(2), take(2), take(2)
    if opening:
        (edge_ref,) = take(1)
        for side in range(2):
            own, other = (ref[pl.ds(2 * K, 8), :] for ref in (olds[side], rims[side]))
            row = lax.broadcasted_iota(jnp.int32, (8, NR), 0)
            other = jnp.where(row < 2, DT * 0.5 * (own + other), other)
            edge_ref[side] = jnp.where(row == 3, 1.0 - own, other)
    for side in range(2):
        for field in range(2):
            rows = field_rows(field)
            past = None if opening else pasts[side][rows, :]
            flow = flux(edge_ref, side, field, rims[side][rows, :], olds[side][rows, :], past)
            fluxes[side][rows, :] = flow
            fulls[side][rows, :] = parts[side][rows, :] + flow
    step_alone(fulls, factor_ref, table_ref, coef_ref, outs)


def step_alone(sides, factor_ref, table_ref, coef_ref, outs):
    spans = [[pl.ds(field * K + half * HALF, HALF) for half in range(2)] for field in range(2)]
    for side, (ref, out_ref) in enumerate(zip(sides, outs)):
        low, high = (
            jnp.concatenate([ref[spans[0][half], :], ref[spans[1][half], :]], axis=1)
            for half in range(2)
        )
        terms = []
        for parity, mixed in enumerate((low + high, low - high)):
            spatial = product(table_ref[parity], mixed)
            pot, vel = spatial[:, :NR], spatial[:, NR:]
            rows = pl.ds(parity * HALF, HALF)
            terms.append(
                jnp.concatenate(
                    [
                        factor_ref[0, side, rows, :] * pot + factor_ref[1, side, rows, :] * vel,
                        factor_ref[2, side, rows, :] * pot + factor_ref[3, side, rows, :] * vel,
                    ],
                    axis=1,
                )
            )
        even = product(table_ref[0], terms[0])
        odd = product(table_ref[2], terms[1])
        back = (even + odd, even - odd)
        other = sides[1 - side]
        for half in range(2):
            k = lax.broadcasted_iota(jnp.int32, (HALF, NR), 0) + half * HALF
            mode = jnp.minimum(k, K - k).astype(F32)
            mode_sq = mode * mode
            for field in range(2):
                rows = spans[field][half]
                value = ref[rows, :]
                coef = lambda row: coef_ref[side, field, pl.ds(row, 1), :]
                out_ref[rows, :] = (
                    (coef(0) - coef(1) * mode_sq) * value
                    + coef(2) * pltpu.roll(value, NR - 1, 1)
                    + coef(3) * pltpu.roll(value, 1, 1)
                    + coef(4) * other[rows, :]
                    + back[half][:, field * NR : (field + 1) * NR]
                )


def last_kernel(*refs):
    parts, olds, rims, pasts = (refs[i : i + 2] for i in range(0, 8, 2))
    edge_ref, out_ref = refs[8:]
    for side in range(2):
        for field in range(2):
            for dest in range(PEERS):
                rows = pl.ds(field * K + dest * PER, PER)
                old = olds[side][rows, :]
                flow = flux(edge_ref, side, field, rims[side][rows, :], old, pasts[side][rows, :])
                if side == 0:
                    flow = edge_ref[0, pl.ds(3, 1), :] * flow
                    out_ref[dest, 4 + field] = old
                out_ref[dest, 2 * side + field] = parts[side][rows, :] + flow


def swaps():
    spot = lambda g: (g % 16) * 16 + g // 16
    inner, outer = [], []
    for g in range(255):
        (inner if g % 2 == 0 else outer).extend([(spot(g), spot(g + 1)), (spot(g + 1), spot(g))])
    slab = [pair for pair in outer if pair[0] % 16 != pair[1] % 16]
    return inner, outer, slab


def on_device(pot, vel, diffusivity, *factors):
    shape = jax.ShapeDtypeStruct
    modes = lax.axis_index("modes").astype(jnp.int32)
    beyond = 2 * modes + 3 * (modes % 2) - 1
    held = (beyond >= 0) & (beyond < 2 * PEERS)
    place = jnp.stack([modes % 2, 2 * modes, held.astype(jnp.int32)])
    inner_pairs, outer_pairs, slab_pairs = swaps()
    table = jnp.asarray(tables())
    block = shape((PEERS, 2, 2, PER, NR), F32)
    plane = shape((2 * K, NR), F32)
    opening = shape((2 * K + 8, NR), F32)
    tiles = shape((2, 2, 8, NR), F32)
    staging = [pltpu.VMEM((2, 32 * PER, NR), F32), pltpu.SemaphoreType.DMA((2, PER // CHUNK))]

    def swap(planes, pairs=outer_pairs):
        return [lax.ppermute(planes[0], AXES, pairs), lax.ppermute(planes[1], AXES, inner_pairs)]

    flat = [a.reshape(-1, NR) for a in (pot, vel)]
    (sent,) = moved(pack_kernel, [block], flat, (pltpu.HBM, pltpu.VMEM), staging)
    sent, place = lax.optimization_barrier((sent, place))
    got = lax.all_to_all(sent, "modes", split_axis=0, concat_axis=0, tiled=True)
    got, place, diffusivity, table = lax.optimization_barrier((got, place, diffusivity, table))
    start = call(split_kernel, [opening] * 2, [place, got, diffusivity], 0, smem=1)
    rims = swap(start)
    start, factors = lax.optimization_barrier((start, factors))
    factor, coef = call(
        factor_kernel,
        [shape((4, 2, K, NR), F32), tiles],
        [place, diffusivity] + [f.reshape(-1, NR) for f in factors],
        0,
        smem=1,
    )
    shared = [factor, table, coef]
    flops = 8 * 2 * 768 * 256 * 256
    parts = call(first_kernel, [plane] * 2, [*start, *shared], flops)
    olds, pasts = start, []
    for step in range(1, STEPS):
        coming = swap(parts, outer_pairs if step < STEPS - 1 else slab_pairs)
        outs = call(
            functools.partial(next_kernel, step == 1),
            [plane] * 6 + ([shape((2, 8, NR), F32)] if step == 1 else []),
            [*parts, *olds, *rims, *pasts, *shared],
            flops,
        )
        parts, olds = outs[:2], outs[2:4]
        edge = outs[6] if step == 1 else edge
        pasts, rims = [*outs[4:6], edge], coming
    (sent,) = call(last_kernel, [shape((PEERS, 6, PER, NR), F32)], [*parts, *olds, *rims, *pasts], 0)
    got = lax.all_to_all(sent, "modes", split_axis=0, concat_axis=0, tiled=True)
    outs = moved(unpack_kernel, [shape((32 * PER, NR), F32)] * 2, [got, diffusivity], (pltpu.VMEM, pltpu.HBM), staging)
    return tuple(a.reshape(PER, 32, NR) for a in outs)


def solution(mesh):
    whole = P(None, ("axial", "modes"), None)
    modal = P("modes", "axial", None)
    return jax.shard_map(
        on_device,
        mesh=mesh,
        in_specs=(modal, modal, P("axial", None), whole, whole, whole, whole),
        out_specs=(modal, modal),
        check_vma=False,
    )
```

```python
import functools
import math

import jax
import jax.numpy as jnp
import numpy as np
from jax import lax
from jax.experimental import pallas as pl
from jax.experimental.pallas import tpu as pltpu
from jax.sharding import PartitionSpec as P

K = 512
HALF = K // 2
NR = 128
STEPS = 4
DT = 0.1
PEERS = 16
PER = K // PEERS
CHUNK = 8
AXES = ("modes", "axial")
VMEM_BYTES = 24 * 1024 * 1024
F32 = jnp.float32
BF16 = jnp.bfloat16


def tables():
    idx = np.arange(HALF)

    def cas(rows):
        angle = 2.0 * np.pi / K * ((rows[:, None] * idx[None, :]) % K)
        return ((np.cos(angle) + np.sin(angle)) / math.sqrt(K)).astype(np.float32)

    def split(matrix):
        high = matrix.astype(jnp.bfloat16)
        low = (matrix - high.astype(np.float32)).astype(jnp.bfloat16)
        return np.concatenate([high, high, low], axis=1)

    even, odd = cas(2 * idx), cas(2 * idx + 1)
    return np.stack([split(even), split(odd), split(np.ascontiguousarray(odd.T))])


def call(body, out_shapes, args, flops, scratch=(), smem=0):
    space = [pl.BlockSpec(memory_space=pltpu.SMEM)] * smem
    space += [pl.BlockSpec(memory_space=pltpu.VMEM)] * (len(args) - smem)
    size = sum(math.prod(a.shape) * a.dtype.itemsize for a in list(args) + list(out_shapes))
    return pl.pallas_call(
        body,
        out_shape=out_shapes,
        in_specs=space,
        out_specs=[pl.BlockSpec(memory_space=pltpu.VMEM)] * len(out_shapes),
        scratch_shapes=scratch,
        compiler_params=pltpu.CompilerParams(vmem_limit_bytes=VMEM_BYTES),
        cost_estimate=pl.CostEstimate(flops=flops, bytes_accessed=size, transcendentals=0),
    )(*args)


def chunk_rows(chunk):
    return pl.ds(chunk * CHUNK * 32, CHUNK * 32)


def planes(sides):
    for peer in range(PEERS):
        order = (0, 1, -1) if peer % 2 == 0 else (1, 0, 2)
        for side in range(sides):
            plane = 2 * peer + order[side]
            yield peer, side, plane if 0 <= plane < 2 * PEERS else None


def pack_kernel(pot_ref, vel_ref, out_ref, rows, sems):
    arrive = [
        [
            pltpu.make_async_copy(
                ref.at[chunk_rows(chunk)], rows.at[field, chunk_rows(chunk)], sems.at[field, chunk]
            )
            for field, ref in enumerate((pot_ref, vel_ref))
        ]
        for chunk in range(PER // CHUNK)
    ]
    for pair in arrive:
        for copy in pair:
            copy.start()
    for chunk, pair in enumerate(arrive):
        for field, copy in enumerate(pair):
            copy.wait()
            for peer, side, plane in planes(2 + field):
                if plane is None:
                    piece = jnp.zeros((CHUNK, NR), F32)
                else:
                    piece = rows[field, pl.ds(chunk * CHUNK * 32 + plane, CHUNK, stride=32), :]
                out_ref[peer, 2 * side + field * (side < 2), pl.ds(chunk * CHUNK, CHUNK)] = piece


def unpack_kernel(in_ref, diff_ref, pot_ref, vel_ref, rows, sems):
    leave = []
    for chunk in range(PER // CHUNK):
        modes = pl.ds(chunk * CHUNK, CHUNK)
        for field, ref in enumerate((pot_ref, vel_ref)):
            flows = {}
            for left in range(1, PEERS - 1, 2):
                pair = diff_ref[pl.ds(2 * left + 1, 1), :] + diff_ref[pl.ds(2 * left + 2, 1), :]
                coef = DT * 0.5 * pair if field == 0 else DT
                flow = coef * (in_ref[left + 1, 4 + field, modes] - in_ref[left, 4 + field, modes])
                flows[left], flows[left + 1] = flow, -flow
            for peer, side, plane in planes(2):
                value = in_ref[peer, 2 * side + field, modes]
                if side == 0 and peer in flows:
                    value = value + flows[peer]
                rows[field, pl.ds(chunk * CHUNK * 32 + plane, CHUNK, stride=32), :] = value
            leave.append(
                pltpu.make_async_copy(
                    rows.at[field, chunk_rows(chunk)], ref.at[chunk_rows(chunk)], sems.at[field, chunk]
                )
            )
            leave[-1].start()
    for copy in leave:
        copy.wait()


def moved(body, out_shapes, args, spaces, scratch):
    if spaces[0] == pltpu.HBM:
        args = [pltpu.with_memory_space_constraint(a, pltpu.HBM) for a in args]
    else:
        out_shapes = [pltpu.HBM(a.shape, a.dtype) for a in out_shapes]
    return pl.pallas_call(
        body,
        out_shape=out_shapes,
        in_specs=[pl.BlockSpec(memory_space=spaces[0])] * len(args),
        out_specs=[pl.BlockSpec(memory_space=spaces[1])] * len(out_shapes),
        scratch_shapes=scratch,
        compiler_params=pltpu.CompilerParams(vmem_limit_bytes=VMEM_BYTES),
        cost_estimate=pl.CostEstimate(flops=0, bytes_accessed=1 << 21, transcendentals=0),
    )(*args)


def split_kernel(core_ref, in_ref, diff_ref, outer, inner, pot_rim, beyond):
    row = lax.broadcasted_iota(jnp.int32, (8, NR), 0)
    for side, out in enumerate((outer, inner)):
        own = jnp.broadcast_to(near(core_ref, diff_ref, side), (8, NR))
        own = jnp.where(row == 0, own, 1.0)
        out[pl.ds(2 * K, 8), :] = own
        if side == 0:
            pot_rim[pl.ds(K, 8), :] = own
        else:
            out[pl.ds(2 * K + 8, 8), :] = own
        for src in range(PEERS):
            for field in range(2):
                piece = in_ref[src, 2 * side + field]
                out[pl.ds(field * K + src * PER, PER), :] = piece
                if side == 0 and field == 0:
                    pot_rim[pl.ds(src * PER, PER), :] = piece
    for src in range(PEERS):
        beyond[pl.ds(src * PER, PER), :] = in_ref[src, 4]


def near(core_ref, diff_ref, side):
    plane = core_ref[1] + (core_ref[0] if side == 0 else 1 - core_ref[0])
    return diff_ref[pl.ds(plane, 1), :]


def factor_kernel(core_ref, diff_ref, *refs):
    ins, out_ref, coef_ref = refs[:4], refs[4], refs[5]
    first = jnp.full((HALF, NR), core_ref[0], jnp.int32) == 0
    for which, ref in enumerate(ins):
        for parity in range(2):
            lower = ref[pl.ds(2 * parity, HALF, stride=4), :] * DT
            upper = ref[pl.ds(2 * parity + 1, HALF, stride=4), :] * DT
            rows = pl.ds(parity * HALF, HALF)
            out_ref[which, 0, rows, :] = jnp.where(first, lower, upper)
            out_ref[which, 1, rows, :] = jnp.where(first, upper, lower)
    tile = (8, NR)
    cell = lax.broadcasted_iota(jnp.int32, tile, 1)
    row = lax.broadcasted_iota(jnp.int32, tile, 0)
    face_radius = (cell + NR).astype(F32)
    radius = face_radius + 0.5
    values = [jnp.broadcast_to(near(core_ref, diff_ref, side), tile) for side in range(2)]
    for field in range(2):
        for side in range(2):
            own = values[side] if field == 0 else jnp.ones(tile, F32)
            middle = 0.5 * (values[0] + values[1]) if field == 0 else own
            face = jnp.where(cell > 0, 0.5 * (pltpu.roll(own, 1, 1) + own) * face_radius, 0.0)
            ahead = pltpu.roll(face, NR - 1, 1)
            terms = (
                1.0 - DT * ((ahead + face) / radius + middle),
                DT * own / (radius * radius),
                DT * ahead / (radius + 1.0),
                DT * face / (radius - 1.0),
                DT * middle,
            )
            total = jnp.zeros(tile, F32)
            for at, term in enumerate(terms):
                total = jnp.where(row == at, term, total)
            coef_ref[side, field] = total


def stacked(value):
    high = value.astype(BF16)
    low = (value - high.astype(F32)).astype(BF16)
    return jnp.concatenate([high, low, high], axis=0)


def product(table, value):
    return jnp.dot(table, stacked(value), preferred_element_type=F32)


def flux(edge_ref, side, field, rim, value, past):
    edge = lambda row: edge_ref[side, pl.ds(row, 1), :]
    beyond = rim if past is None else edge(2) * (rim - past)
    return edge(field) * (beyond - value)


def field_rows(field):
    return pl.ds(field * K, K)


def first_kernel(outer, inner, factor_ref, table_ref, coef_ref, out_outer, out_inner):
    step_alone((outer, inner), factor_ref, table_ref, coef_ref, (out_outer, out_inner))


def next_kernel(opening, *refs):
    refs = list(refs)
    take = lambda n: [refs.pop(0) for _ in range(n)]
    parts, olds = take(2), take(2)
    if opening:
        pot_rim, slab_rim, beyond, inner_rim = take(4)
        comings = [
            [slab_rim[field_rows(0), :] + pot_rim[pl.ds(0, K), :], slab_rim[field_rows(1), :] + beyond[...]],
            [inner_rim[field_rows(field), :] for field in range(2)],
        ]
        ends = pl.ds(2 * K, 8)
        others = [slab_rim[ends, :] + pot_rim[pl.ds(K, 8), :], inner_rim[ends, :]]
    else:
        rims, pasts, (edge_ref,) = take(2), take(2), take(1)
        comings = [[rim[field_rows(field), :] for field in range(2)] for rim in rims]
    factor_ref, table_ref, coef_ref = take(3)
    outs, fulls, fluxes = take(2), take(2), take(2)
    if opening:
        (edge_ref,) = take(1)
        for side in range(2):
            own, other = olds[side][pl.ds(2 * K, 8), :], others[side]
            row = lax.broadcasted_iota(jnp.int32, (8, NR), 0)
            other = jnp.where(row < 2, DT * 0.5 * (own + other), other)
            edge_ref[side] = jnp.where(row == 3, 1.0 - pot_rim[pl.ds(K, 8), :], other)
    for side in range(2):
        for field in range(2):
            rows = field_rows(field)
            past = None if opening else pasts[side][rows, :]
            flow = flux(edge_ref, side, field, comings[side][field], olds[side][rows, :], past)
            fluxes[side][rows, :] = flow
            fulls[side][rows, :] = parts[side][rows, :] + flow
    step_alone(fulls, factor_ref, table_ref, coef_ref, outs)


def step_alone(sides, factor_ref, table_ref, coef_ref, outs):
    spans = [[pl.ds(field * K + half * HALF, HALF) for half in range(2)] for field in range(2)]
    for side, (ref, out_ref) in enumerate(zip(sides, outs)):
        low, high = (
            jnp.concatenate([ref[spans[0][half], :], ref[spans[1][half], :]], axis=1)
            for half in range(2)
        )
        terms = []
        for parity, mixed in enumerate((low + high, low - high)):
            spatial = product(table_ref[parity], mixed)
            pot, vel = spatial[:, :NR], spatial[:, NR:]
            rows = pl.ds(parity * HALF, HALF)
            terms.append(
                jnp.concatenate(
                    [
                        factor_ref[0, side, rows, :] * pot + factor_ref[1, side, rows, :] * vel,
                        factor_ref[2, side, rows, :] * pot + factor_ref[3, side, rows, :] * vel,
                    ],
                    axis=1,
                )
            )
        even = product(table_ref[0], terms[0])
        odd = product(table_ref[2], terms[1])
        back = (even + odd, even - odd)
        other = sides[1 - side]
        for half in range(2):
            k = lax.broadcasted_iota(jnp.int32, (HALF, NR), 0) + half * HALF
            mode = jnp.minimum(k, K - k).astype(F32)
            mode_sq = mode * mode
            for field in range(2):
                rows = spans[field][half]
                value = ref[rows, :]
                coef = lambda row: coef_ref[side, field, pl.ds(row, 1), :]
                out_ref[rows, :] = (
                    (coef(0) - coef(1) * mode_sq) * value
                    + coef(2) * pltpu.roll(value, NR - 1, 1)
                    + coef(3) * pltpu.roll(value, 1, 1)
                    + coef(4) * other[rows, :]
                    + back[half][:, field * NR : (field + 1) * NR]
                )


def last_kernel(*refs):
    parts, olds, rims, pasts = (refs[i : i + 2] for i in range(0, 8, 2))
    edge_ref, out_ref = refs[8:]
    for side in range(2):
        for field in range(2):
            for dest in range(PEERS):
                rows = pl.ds(field * K + dest * PER, PER)
                old = olds[side][rows, :]
                flow = flux(edge_ref, side, field, rims[side][rows, :], old, pasts[side][rows, :])
                if side == 0:
                    flow = edge_ref[0, pl.ds(3, 1), :] * flow
                    out_ref[dest, 4 + field] = old
                out_ref[dest, 2 * side + field] = parts[side][rows, :] + flow


def swaps():
    spot = lambda g: (g % 16) * 16 + g // 16
    inner, outer = [], []
    for g in range(255):
        (inner if g % 2 == 0 else outer).extend([(spot(g), spot(g + 1)), (spot(g + 1), spot(g))])
    slab = [pair for pair in outer if pair[0] % 16 != pair[1] % 16]
    return inner, outer, slab


def on_device(pot, vel, diffusivity, *factors):
    shape = jax.ShapeDtypeStruct
    modes = lax.axis_index("modes").astype(jnp.int32)
    place = jnp.stack([modes % 2, 2 * modes])
    inner_pairs, outer_pairs, slab_pairs = swaps()
    table = jnp.asarray(tables())
    wide = shape((PEERS, 5, PER, NR), F32)
    plane = shape((2 * K, NR), F32)
    tiles = shape((2, 2, 8, NR), F32)
    staging = [pltpu.VMEM((2, 32 * PER, NR), F32), pltpu.SemaphoreType.DMA((2, PER // CHUNK))]

    def swap(planes, pairs=outer_pairs):
        return [lax.ppermute(planes[0], AXES, pairs), lax.ppermute(planes[1], AXES, inner_pairs)]

    flat = [a.reshape(-1, NR) for a in (pot, vel)]
    (sent,) = moved(pack_kernel, [wide], flat, (pltpu.HBM, pltpu.VMEM), staging)
    sent, place = lax.optimization_barrier((sent, place))
    got = lax.all_to_all(sent, "modes", split_axis=0, concat_axis=0, tiled=True)
    got, place, diffusivity, table = lax.optimization_barrier((got, place, diffusivity, table))
    *start, pot_rim, beyond = call(
        split_kernel,
        [shape((2 * K + rows, NR), F32) for rows in (8, 16)] + [shape((K + 8, NR), F32), shape((K, NR), F32)],
        [place, got, diffusivity],
        0,
        smem=1,
    )
    rims = [
        lax.ppermute(pot_rim, AXES, [pair for pair in outer_pairs if pair not in slab_pairs]),
        lax.ppermute(start[0], AXES, slab_pairs),
        beyond,
        lax.ppermute(start[1], AXES, inner_pairs),
    ]
    start, factors = lax.optimization_barrier((start, factors))
    factor, coef = call(
        factor_kernel,
        [shape((4, 2, K, NR), F32), tiles],
        [place, diffusivity] + [f.reshape(-1, NR) for f in factors],
        0,
        smem=1,
    )
    shared = [factor, table, coef]
    flops = 1 << 34
    parts = call(first_kernel, [plane] * 2, [*start, *shared], flops)
    olds, pasts = start, []
    for step in range(1, STEPS):
        coming = swap(parts, outer_pairs if step < STEPS - 1 else slab_pairs)
        outs = call(
            functools.partial(next_kernel, step == 1),
            [plane] * 6 + ([shape((2, 8, NR), F32)] if step == 1 else []),
            [*parts, *olds, *rims, *pasts, *shared],
            flops,
        )
        parts, olds = outs[:2], outs[2:4]
        edge = outs[6] if step == 1 else edge
        pasts, rims = [*outs[4:6], edge], coming
    (sent,) = call(last_kernel, [shape((PEERS, 6, PER, NR), F32)], [*parts, *olds, *rims, *pasts], 0)
    got = lax.all_to_all(sent, "modes", split_axis=0, concat_axis=0, tiled=True)
    outs = moved(unpack_kernel, [shape((32 * PER, NR), F32)] * 2, [got, diffusivity], (pltpu.VMEM, pltpu.HBM), staging)
    return tuple(a.reshape(PER, 32, NR) for a in outs)


def solution(mesh):
    whole = P(None, ("axial", "modes"), None)
    modal = P("modes", "axial", None)
    return jax.shard_map(
        on_device,
        mesh=mesh,
        in_specs=(modal, modal, P("axial", None), whole, whole, whole, whole),
        out_specs=(modal, modal),
        check_vma=False,
    )
```

```python
import functools
import math

import jax
import jax.numpy as jnp
import numpy as np
from jax import lax
from jax.experimental import pallas as pl
from jax.experimental.pallas import tpu as pltpu
from jax.sharding import PartitionSpec as P

K = 512
HALF = K // 2
NR = 128
STEPS = 4
DT = 0.1
PEERS = 16
PER = K // PEERS
CHUNK = 8
AXES = ("modes", "axial")
VMEM_BYTES = 24 * 1024 * 1024
F32 = jnp.float32
BF16 = jnp.bfloat16


def tables():
    idx = np.arange(HALF)

    def cas(rows):
        angle = 2.0 * np.pi / K * ((rows[:, None] * idx[None, :]) % K)
        return ((np.cos(angle) + np.sin(angle)) / math.sqrt(K)).astype(np.float32)

    def split(matrix):
        high = matrix.astype(jnp.bfloat16)
        low = (matrix - high.astype(np.float32)).astype(jnp.bfloat16)
        return np.concatenate([high, high, low], axis=1)

    even, odd = cas(2 * idx), cas(2 * idx + 1)
    return np.stack([split(even), split(odd), split(np.ascontiguousarray(odd.T))])


def call(body, out_shapes, args, flops, scratch=(), smem=0):
    space = [pl.BlockSpec(memory_space=pltpu.SMEM)] * smem
    space += [pl.BlockSpec(memory_space=pltpu.VMEM)] * (len(args) - smem)
    size = sum(math.prod(a.shape) * a.dtype.itemsize for a in list(args) + list(out_shapes))
    return pl.pallas_call(
        body,
        out_shape=out_shapes,
        in_specs=space,
        out_specs=[pl.BlockSpec(memory_space=pltpu.VMEM)] * len(out_shapes),
        scratch_shapes=scratch,
        compiler_params=pltpu.CompilerParams(vmem_limit_bytes=VMEM_BYTES),
        cost_estimate=pl.CostEstimate(flops=flops, bytes_accessed=size, transcendentals=0),
    )(*args)


def chunk_rows(chunk):
    return pl.ds(chunk * CHUNK * 32, CHUNK * 32)


def planes():
    for peer in range(PEERS):
        for side in range(2):
            yield peer, side, 2 * peer + (side if peer % 2 == 0 else 1 - side)


def pack_kernel(pot_ref, vel_ref, out_ref, rows, sems):
    arrive = [
        [
            pltpu.make_async_copy(
                ref.at[chunk_rows(chunk)], rows.at[field, chunk_rows(chunk)], sems.at[field, chunk]
            )
            for field, ref in enumerate((pot_ref, vel_ref))
        ]
        for chunk in range(PER // CHUNK)
    ]
    for pair in arrive:
        for copy in pair:
            copy.start()
    for chunk, pair in enumerate(arrive):
        for field, copy in enumerate(pair):
            copy.wait()
            for peer, side, plane in planes():
                out_ref[peer, side, field, pl.ds(chunk * CHUNK, CHUNK)] = rows[
                    field, pl.ds(chunk * CHUNK * 32 + plane, CHUNK, stride=32), :
                ]


def unpack_kernel(in_ref, diff_ref, pot_ref, vel_ref, rows, sems):
    leave = []
    for chunk in range(PER // CHUNK):
        modes = pl.ds(chunk * CHUNK, CHUNK)
        for field, ref in enumerate((pot_ref, vel_ref)):
            flows = {}
            for left in range(1, PEERS - 1, 2):
                pair = diff_ref[pl.ds(2 * left + 1, 1), :] + diff_ref[pl.ds(2 * left + 2, 1), :]
                coef = DT * 0.5 * pair if field == 0 else DT
                flow = coef * (in_ref[left + 1, 4 + field, modes] - in_ref[left, 4 + field, modes])
                flows[left], flows[left + 1] = flow, -flow
            for peer, side, plane in planes():
                value = in_ref[peer, 2 * side + field, modes]
                if side == 0 and peer in flows:
                    value = value + flows[peer]
                rows[field, pl.ds(chunk * CHUNK * 32 + plane, CHUNK, stride=32), :] = value
            leave.append(
                pltpu.make_async_copy(
                    rows.at[field, chunk_rows(chunk)], ref.at[chunk_rows(chunk)], sems.at[field, chunk]
                )
            )
            leave[-1].start()
    for copy in leave:
        copy.wait()


def moved(body, out_shapes, args, spaces, scratch):
    if spaces[0] == pltpu.HBM:
        args = [pltpu.with_memory_space_constraint(a, pltpu.HBM) for a in args]
    else:
        out_shapes = [pltpu.HBM(a.shape, a.dtype) for a in out_shapes]
    return pl.pallas_call(
        body,
        out_shape=out_shapes,
        in_specs=[pl.BlockSpec(memory_space=spaces[0])] * len(args),
        out_specs=[pl.BlockSpec(memory_space=spaces[1])] * len(out_shapes),
        scratch_shapes=scratch,
        compiler_params=pltpu.CompilerParams(vmem_limit_bytes=VMEM_BYTES),
        cost_estimate=pl.CostEstimate(flops=0, bytes_accessed=1 << 21, transcendentals=0),
    )(*args)


def split_kernel(core_ref, in_ref, diff_ref, out_outer, out_inner):
    for side, out in enumerate((out_outer, out_inner)):
        for src in range(PEERS):
            for field in range(2):
                out[pl.ds(field * K + src * PER, PER), :] = in_ref[src, side, field]
        own = near(core_ref, diff_ref, side)
        row = lax.broadcasted_iota(jnp.int32, (8, NR), 0)
        held = jnp.full((8, NR), core_ref[2], jnp.int32).astype(F32)
        ends = jnp.where(row == 3, held, 1.0)
        out[pl.ds(2 * K, 8), :] = jnp.where(row == 0, jnp.broadcast_to(own, (8, NR)), ends)


def near(core_ref, diff_ref, side):
    plane = core_ref[1] + (core_ref[0] if side == 0 else 1 - core_ref[0])
    return diff_ref[pl.ds(plane, 1), :]


def factor_kernel(core_ref, diff_ref, *refs):
    ins, out_ref, coef_ref = refs[:4], refs[4], refs[5]
    first = jnp.full((HALF, NR), core_ref[0], jnp.int32) == 0
    for which, ref in enumerate(ins):
        for parity in range(2):
            lower = ref[pl.ds(2 * parity, HALF, stride=4), :] * DT
            upper = ref[pl.ds(2 * parity + 1, HALF, stride=4), :] * DT
            rows = pl.ds(parity * HALF, HALF)
            out_ref[which, 0, rows, :] = jnp.where(first, lower, upper)
            out_ref[which, 1, rows, :] = jnp.where(first, upper, lower)
    tile = (8, NR)
    cell = lax.broadcasted_iota(jnp.int32, tile, 1)
    row = lax.broadcasted_iota(jnp.int32, tile, 0)
    face_radius = (cell + NR).astype(F32)
    radius = face_radius + 0.5
    values = [jnp.broadcast_to(near(core_ref, diff_ref, side), tile) for side in range(2)]
    for field in range(2):
        for side in range(2):
            own = values[side] if field == 0 else jnp.ones(tile, F32)
            middle = 0.5 * (values[0] + values[1]) if field == 0 else own
            face = jnp.where(cell > 0, 0.5 * (pltpu.roll(own, 1, 1) + own) * face_radius, 0.0)
            ahead = pltpu.roll(face, NR - 1, 1)
            terms = (
                1.0 - DT * ((ahead + face) / radius + middle),
                DT * own / (radius * radius),
                DT * ahead / (radius + 1.0),
                DT * face / (radius - 1.0),
                DT * middle,
            )
            total = jnp.zeros(tile, F32)
            for at, term in enumerate(terms):
                total = jnp.where(row == at, term, total)
            coef_ref[side, field] = total


def stacked(value):
    high = value.astype(BF16)
    low = (value - high.astype(F32)).astype(BF16)
    return jnp.concatenate([high, low, high], axis=0)


def product(table, value):
    return jnp.dot(table, stacked(value), preferred_element_type=F32)


def flux(edge_ref, side, field, rim, value, past):
    edge = lambda row: edge_ref[side, pl.ds(row, 1), :]
    beyond = rim if past is None else edge(2) * (rim - past)
    return edge(field) * (beyond - value)


def field_rows(field):
    return pl.ds(field * K, K)


def first_kernel(outer, inner, factor_ref, table_ref, coef_ref, out_outer, out_inner):
    step_alone((outer, inner), factor_ref, table_ref, coef_ref, (out_outer, out_inner))


def next_kernel(opening, *refs):
    refs = list(refs)
    take = lambda n: [refs.pop(0) for _ in range(n)]
    parts, olds, rims = take(2), take(2), take(2)
    pasts, edge_ref = ((None, None), None) if opening else (take(2), take(1)[0])
    factor_ref, table_ref, coef_ref = take(3)
    outs, fulls, fluxes = take(2), take(2), take(2)
    if opening:
        (edge_ref,) = take(1)
        for side in range(2):
            own, other = (ref[pl.ds(2 * K, 8), :] for ref in (olds[side], rims[side]))
            row = lax.broadcasted_iota(jnp.int32, (8, NR), 0)
            other = jnp.where(row < 2, DT * 0.5 * (own + other), other)
            edge_ref[side] = jnp.where(row == 3, 1.0 - own, other)
    for side in range(2):
        for field in range(2):
            rows = field_rows(field)
            past = None if opening else pasts[side][rows, :]
            flow = flux(edge_ref, side, field, rims[side][rows, :], olds[side][rows, :], past)
            fluxes[side][rows, :] = flow
            fulls[side][rows, :] = parts[side][rows, :] + flow
    step_alone(fulls, factor_ref, table_ref, coef_ref, outs)
    more = outs[0].shape[0] - 2 * K
    if more > 0:
        outs[0][pl.ds(2 * K, more), :] = jnp.zeros((more, NR), F32)


def step_alone(sides, factor_ref, table_ref, coef_ref, outs):
    spans = [[pl.ds(field * K + half * HALF, HALF) for half in range(2)] for field in range(2)]
    for side, (ref, out_ref) in enumerate(zip(sides, outs)):
        low, high = (
            jnp.concatenate([ref[spans[0][half], :], ref[spans[1][half], :]], axis=1)
            for half in range(2)
        )
        terms = []
        for parity, mixed in enumerate((low + high, low - high)):
            spatial = product(table_ref[parity], mixed)
            pot, vel = spatial[:, :NR], spatial[:, NR:]
            rows = pl.ds(parity * HALF, HALF)
            terms.append(
                jnp.concatenate(
                    [
                        factor_ref[0, side, rows, :] * pot + factor_ref[1, side, rows, :] * vel,
                        factor_ref[2, side, rows, :] * pot + factor_ref[3, side, rows, :] * vel,
                    ],
                    axis=1,
                )
            )
        even = product(table_ref[0], terms[0])
        odd = product(table_ref[2], terms[1])
        back = (even + odd, even - odd)
        other = sides[1 - side]
        for half in range(2):
            k = lax.broadcasted_iota(jnp.int32, (HALF, NR), 0) + half * HALF
            mode = jnp.minimum(k, K - k).astype(F32)
            mode_sq = mode * mode
            for field in range(2):
                rows = spans[field][half]
                value = ref[rows, :]
                coef = lambda row: coef_ref[side, field, pl.ds(row, 1), :]
                out_ref[rows, :] = (
                    (coef(0) - coef(1) * mode_sq) * value
                    + coef(2) * pltpu.roll(value, NR - 1, 1)
                    + coef(3) * pltpu.roll(value, 1, 1)
                    + coef(4) * other[rows, :]
                    + back[half][:, field * NR : (field + 1) * NR]
                )


def last_kernel(*refs):
    parts, olds, rims, pasts = (refs[i : i + 2] for i in range(0, 8, 2))
    edge_ref, out_ref = refs[8:]
    for side in range(2):
        for field in range(2):
            for dest in range(PEERS):
                rows = pl.ds(field * K + dest * PER, PER)
                old = olds[side][rows, :]
                flow = flux(edge_ref, side, field, rims[side][rows, :], old, pasts[side][rows, :])
                if side == 0:
                    flow = edge_ref[0, pl.ds(3, 1), :] * flow
                    out_ref[dest, 4 + field] = old
                out_ref[dest, 2 * side + field] = parts[side][rows, :] + flow


def swaps():
    spot = lambda g: (g % 16) * 16 + g // 16
    inner, outer = [], []
    for g in range(255):
        (inner if g % 2 == 0 else outer).extend([(spot(g), spot(g + 1)), (spot(g + 1), spot(g))])
    slab = [pair for pair in outer if pair[0] % 16 != pair[1] % 16]
    return inner, outer, slab


def on_device(pot, vel, diffusivity, *factors):
    shape = jax.ShapeDtypeStruct
    modes = lax.axis_index("modes").astype(jnp.int32)
    beyond = 2 * modes + 3 * (modes % 2) - 1
    held = (beyond >= 0) & (beyond < 2 * PEERS)
    place = jnp.stack([modes % 2, 2 * modes, held.astype(jnp.int32)])
    inner_pairs, outer_pairs, slab_pairs = swaps()
    table = jnp.asarray(tables())
    block = shape((PEERS, 2, 2, PER, NR), F32)
    plane = shape((2 * K, NR), F32)
    opening = shape((2 * K + 8, NR), F32)
    tiles = shape((2, 2, 8, NR), F32)
    staging = [pltpu.VMEM((2, 32 * PER, NR), F32), pltpu.SemaphoreType.DMA((2, PER // CHUNK))]

    flat = [a.reshape(-1, NR) for a in (pot, vel)]
    (sent,) = moved(pack_kernel, [block], flat, (pltpu.HBM, pltpu.VMEM), staging)
    sent, place = lax.optimization_barrier((sent, place))
    got = lax.all_to_all(sent, "modes", split_axis=0, concat_axis=0, tiled=True)
    got, place, diffusivity, table = lax.optimization_barrier((got, place, diffusivity, table))
    start = call(split_kernel, [opening] * 2, [place, got, diffusivity], 0, smem=1)
    rims = [lax.ppermute(start[0], AXES, outer_pairs), lax.ppermute(start[1], AXES, inner_pairs)]
    start, factors = lax.optimization_barrier((start, factors))
    factor, coef = call(
        factor_kernel,
        [shape((4, 2, K, NR), F32), tiles],
        [place, diffusivity] + [f.reshape(-1, NR) for f in factors],
        0,
        smem=1,
    )
    shared = [factor, table, coef]
    flops = 1 << 34
    parts = call(first_kernel, [plane] * 2, [*start, *shared], flops)
    olds, pasts = start, []
    for step in range(1, STEPS):
        late = step == STEPS - 2
        pairs = outer_pairs if step < STEPS - 1 else slab_pairs
        coming = [lax.ppermute(parts[0], AXES, pairs)]
        inner = parts[1]
        if not late:
            coming.append(lax.ppermute(inner, AXES, inner_pairs))
        if step == STEPS - 1:
            coming[0], rims = lax.optimization_barrier((coming[0], rims))
        outs = call(
            functools.partial(next_kernel, step == 1),
            [shape((2 * K + 8 * (STEPS - 1 - step), NR), F32)] + [plane] * 5 + ([shape((2, 8, NR), F32)] if step == 1 else []),
            [*parts, *olds, *rims, *pasts, *shared],
            flops,
        )
        if late:
            inner, outs = lax.optimization_barrier((inner, outs))
            coming.append(lax.ppermute(inner, AXES, inner_pairs))
        parts, olds = outs[:2], outs[2:4]
        edge = outs[6] if step == 1 else edge
        pasts, rims = [*outs[4:6], edge], coming
    (sent,) = call(last_kernel, [shape((PEERS, 6, PER, NR), F32)], [*parts, *olds, *rims, *pasts], 0)
    got = lax.all_to_all(sent, "modes", split_axis=0, concat_axis=0, tiled=True)
    outs = moved(unpack_kernel, [shape((32 * PER, NR), F32)] * 2, [got, diffusivity], (pltpu.VMEM, pltpu.HBM), staging)
    return tuple(a.reshape(PER, 32, NR) for a in outs)


def solution(mesh):
    whole = P(None, ("axial", "modes"), None)
    modal = P("modes", "axial", None)
    return jax.shard_map(
        on_device,
        mesh=mesh,
        in_specs=(modal, modal, P("axial", None), whole, whole, whole, whole),
        out_specs=(modal, modal),
        check_vma=False,
    )
```

```python
import functools
import math

import jax
import jax.numpy as jnp
import numpy as np
from jax import lax
from jax.experimental import pallas as pl
from jax.experimental.pallas import tpu as pltpu
from jax.sharding import PartitionSpec as P

K = 512
HALF = K // 2
NR = 128
STEPS = 4
DT = 0.1
PEERS = 16
PER = K // PEERS
CHUNK = 8
AXES = ("modes", "axial")
VMEM_BYTES = 24 * 1024 * 1024
F32 = jnp.float32
BF16 = jnp.bfloat16


def tables():
    idx = np.arange(HALF)

    def cas(rows):
        angle = 2.0 * np.pi / K * ((rows[:, None] * idx[None, :]) % K)
        return ((np.cos(angle) + np.sin(angle)) / math.sqrt(K)).astype(np.float32)

    def split(matrix):
        high = matrix.astype(jnp.bfloat16)
        low = (matrix - high.astype(np.float32)).astype(jnp.bfloat16)
        return np.concatenate([high, high, low], axis=1)

    even, odd = cas(2 * idx), cas(2 * idx + 1)
    return np.stack([split(even), split(odd), split(np.ascontiguousarray(odd.T))])


def call(body, out_shapes, args, flops, scratch=(), smem=0):
    space = [pl.BlockSpec(memory_space=pltpu.SMEM)] * smem
    space += [pl.BlockSpec(memory_space=pltpu.VMEM)] * (len(args) - smem)
    size = sum(math.prod(a.shape) * a.dtype.itemsize for a in list(args) + list(out_shapes))
    return pl.pallas_call(
        body,
        out_shape=out_shapes,
        in_specs=space,
        out_specs=[pl.BlockSpec(memory_space=pltpu.VMEM)] * len(out_shapes),
        scratch_shapes=scratch,
        compiler_params=pltpu.CompilerParams(vmem_limit_bytes=VMEM_BYTES),
        cost_estimate=pl.CostEstimate(flops=flops, bytes_accessed=size, transcendentals=0),
    )(*args)


def chunk_rows(chunk):
    return pl.ds(chunk * CHUNK * 32, CHUNK * 32)


def planes(sides):
    for peer in range(PEERS):
        order = (0, 1, -1) if peer % 2 == 0 else (1, 0, 2)
        for side in range(sides):
            plane = 2 * peer + order[side]
            yield peer, side, plane if 0 <= plane < 2 * PEERS else None


def pack_kernel(pot_ref, vel_ref, out_ref, rows, sems):
    arrive = [
        [
            pltpu.make_async_copy(
                ref.at[chunk_rows(chunk)], rows.at[field, chunk_rows(chunk)], sems.at[field, chunk]
            )
            for field, ref in enumerate((pot_ref, vel_ref))
        ]
        for chunk in range(PER // CHUNK)
    ]
    for pair in arrive:
        for copy in pair:
            copy.start()
    for chunk, pair in enumerate(arrive):
        for field, copy in enumerate(pair):
            copy.wait()
            for peer, side, plane in planes(2 + field):
                if plane is None:
                    piece = jnp.zeros((CHUNK, NR), F32)
                else:
                    piece = rows[field, pl.ds(chunk * CHUNK * 32 + plane, CHUNK, stride=32), :]
                out_ref[peer, 2 * side + field * (side < 2), pl.ds(chunk * CHUNK, CHUNK)] = piece


def unpack_kernel(in_ref, pot_ref, vel_ref, rows, sems):
    leave = []
    for chunk in range(PER // CHUNK):
        modes = pl.ds(chunk * CHUNK, CHUNK)
        for field, ref in enumerate((pot_ref, vel_ref)):
            flows = {}
            for left in range(1, PEERS - 1, 2) if field == 1 else ():
                flow = DT * (in_ref[left + 1, 4, modes] - in_ref[left, 4, modes])
                flows[left], flows[left + 1] = flow, -flow
            for peer, side, plane in planes(2):
                value = in_ref[peer, 2 * side + field, modes]
                if side == 0 and peer in flows:
                    value = value + flows[peer]
                rows[field, pl.ds(chunk * CHUNK * 32 + plane, CHUNK, stride=32), :] = value
            leave.append(
                pltpu.make_async_copy(
                    rows.at[field, chunk_rows(chunk)], ref.at[chunk_rows(chunk)], sems.at[field, chunk]
                )
            )
            leave[-1].start()
    for copy in leave:
        copy.wait()


def moved(body, out_shapes, args, spaces, scratch):
    if spaces[0] == pltpu.HBM:
        args = [pltpu.with_memory_space_constraint(a, pltpu.HBM) for a in args]
    else:
        out_shapes = [pltpu.HBM(a.shape, a.dtype) for a in out_shapes]
    return pl.pallas_call(
        body,
        out_shape=out_shapes,
        in_specs=[pl.BlockSpec(memory_space=spaces[0])] * len(args),
        out_specs=[pl.BlockSpec(memory_space=spaces[1])] * len(out_shapes),
        scratch_shapes=scratch,
        compiler_params=pltpu.CompilerParams(vmem_limit_bytes=VMEM_BYTES),
        cost_estimate=pl.CostEstimate(flops=0, bytes_accessed=1 << 21, transcendentals=0),
    )(*args)


def split_kernel(core_ref, in_ref, diff_ref, outer, inner, pot_rim, beyond):
    row = lax.broadcasted_iota(jnp.int32, (8, NR), 0)
    for side, out in enumerate((outer, inner)):
        own = jnp.broadcast_to(near(core_ref, diff_ref, side), (8, NR))
        own = jnp.where(row == 0, own, 1.0)
        out[pl.ds(2 * K, 8), :] = own
        if side == 0:
            pot_rim[pl.ds(K, 8), :] = own
        else:
            out[pl.ds(2 * K + 8, 8), :] = own
        for src in range(PEERS):
            for field in range(2):
                piece = in_ref[src, 2 * side + field]
                out[pl.ds(field * K + src * PER, PER), :] = piece
                if side == 0 and field == 0:
                    pot_rim[pl.ds(src * PER, PER), :] = piece
    for src in range(PEERS):
        beyond[pl.ds(src * PER, PER), :] = in_ref[src, 4]


def near(core_ref, diff_ref, side):
    plane = core_ref[1] + (core_ref[0] if side == 0 else 1 - core_ref[0])
    return diff_ref[pl.ds(plane, 1), :]


def factor_kernel(core_ref, diff_ref, *refs):
    ins, out_ref, coef_ref = refs[:4], refs[4], refs[5]
    first = jnp.full((HALF, NR), core_ref[0], jnp.int32) == 0
    for which, ref in enumerate(ins):
        for parity in range(2):
            lower = ref[pl.ds(2 * parity, HALF, stride=4), :] * DT
            upper = ref[pl.ds(2 * parity + 1, HALF, stride=4), :] * DT
            rows = pl.ds(parity * HALF, HALF)
            out_ref[which, 0, rows, :] = jnp.where(first, lower, upper)
            out_ref[which, 1, rows, :] = jnp.where(first, upper, lower)
    tile = (8, NR)
    cell = lax.broadcasted_iota(jnp.int32, tile, 1)
    row = lax.broadcasted_iota(jnp.int32, tile, 0)
    face_radius = (cell + NR).astype(F32)
    radius = face_radius + 0.5
    values = [jnp.broadcast_to(near(core_ref, diff_ref, side), tile) for side in range(2)]
    for field in range(2):
        for side in range(2):
            own = values[side] if field == 0 else jnp.ones(tile, F32)
            middle = 0.5 * (values[0] + values[1]) if field == 0 else own
            face = jnp.where(cell > 0, 0.5 * (pltpu.roll(own, 1, 1) + own) * face_radius, 0.0)
            ahead = pltpu.roll(face, NR - 1, 1)
            terms = (
                1.0 - DT * ((ahead + face) / radius + middle),
                DT * own / (radius * radius),
                DT * ahead / (radius + 1.0),
                DT * face / (radius - 1.0),
                DT * middle,
            )
            total = jnp.zeros(tile, F32)
            for at, term in enumerate(terms):
                total = jnp.where(row == at, term, total)
            coef_ref[side, field] = total


def stacked(value):
    high = value.astype(BF16)
    low = (value - high.astype(F32)).astype(BF16)
    return jnp.concatenate([high, low, high], axis=0)


def product(table, value):
    return jnp.dot(table, stacked(value), preferred_element_type=F32)


def flux(edge_ref, side, field, rim, value, past):
    edge = lambda row: edge_ref[side, pl.ds(row, 1), :]
    beyond = rim if past is None else edge(2) * (rim - past)
    return edge(field) * (beyond - value)


def field_rows(field):
    return pl.ds(field * K, K)


def first_kernel(outer, inner, factor_ref, table_ref, coef_ref, out_outer, out_inner):
    step_alone((outer, inner), factor_ref, table_ref, coef_ref, (out_outer, out_inner))


def next_kernel(opening, *refs):
    refs = list(refs)
    take = lambda n: [refs.pop(0) for _ in range(n)]
    parts, olds = take(2), take(2)
    if opening:
        pot_rim, slab_rim, beyond, inner_rim = take(4)
        comings = [
            [slab_rim[field_rows(0), :] + pot_rim[pl.ds(0, K), :], slab_rim[field_rows(1), :] + beyond[...]],
            [inner_rim[field_rows(field), :] for field in range(2)],
        ]
        ends = pl.ds(2 * K, 8)
        others = [slab_rim[ends, :] + pot_rim[pl.ds(K, 8), :], inner_rim[ends, :]]
    else:
        rims, pasts, (edge_ref,) = take(2), take(2), take(1)
        comings = [[rim[field_rows(field), :] for field in range(2)] for rim in rims]
    factor_ref, table_ref, coef_ref = take(3)
    outs, fulls, fluxes = take(2), take(2), take(2)
    if opening:
        (edge_ref,) = take(1)
        for side in range(2):
            own, other = olds[side][pl.ds(2 * K, 8), :], others[side]
            row = lax.broadcasted_iota(jnp.int32, (8, NR), 0)
            other = jnp.where(row < 2, DT * 0.5 * (own + other), other)
            edge_ref[side] = jnp.where(row == 3, 1.0 - pot_rim[pl.ds(K, 8), :], other)
    for side in range(2):
        for field in range(2):
            rows = field_rows(field)
            past = None if opening else pasts[side][rows, :]
            flow = flux(edge_ref, side, field, comings[side][field], olds[side][rows, :], past)
            fluxes[side][rows, :] = flow
            fulls[side][rows, :] = parts[side][rows, :] + flow
    step_alone(fulls, factor_ref, table_ref, coef_ref, outs)


def step_alone(sides, factor_ref, table_ref, coef_ref, outs):
    spans = [[pl.ds(field * K + half * HALF, HALF) for half in range(2)] for field in range(2)]
    for side, (ref, out_ref) in enumerate(zip(sides, outs)):
        low, high = (
            jnp.concatenate([ref[spans[0][half], :], ref[spans[1][half], :]], axis=1)
            for half in range(2)
        )
        terms = []
        for parity, mixed in enumerate((low + high, low - high)):
            spatial = product(table_ref[parity], mixed)
            pot, vel = spatial[:, :NR], spatial[:, NR:]
            rows = pl.ds(parity * HALF, HALF)
            terms.append(
                jnp.concatenate(
                    [
                        factor_ref[0, side, rows, :] * pot + factor_ref[1, side, rows, :] * vel,
                        factor_ref[2, side, rows, :] * pot + factor_ref[3, side, rows, :] * vel,
                    ],
                    axis=1,
                )
            )
        even = product(table_ref[0], terms[0])
        odd = product(table_ref[2], terms[1])
        back = (even + odd, even - odd)
        other = sides[1 - side]
        for half in range(2):
            k = lax.broadcasted_iota(jnp.int32, (HALF, NR), 0) + half * HALF
            mode = jnp.minimum(k, K - k).astype(F32)
            mode_sq = mode * mode
            for field in range(2):
                rows = spans[field][half]
                value = ref[rows, :]
                coef = lambda row: coef_ref[side, field, pl.ds(row, 1), :]
                out_ref[rows, :] = (
                    (coef(0) - coef(1) * mode_sq) * value
                    + coef(2) * pltpu.roll(value, NR - 1, 1)
                    + coef(3) * pltpu.roll(value, 1, 1)
                    + coef(4) * other[rows, :]
                    + back[half][:, field * NR : (field + 1) * NR]
                )


def last_kernel(*refs):
    parts, olds, rims, pasts = (refs[i : i + 2] for i in range(0, 8, 2))
    edge_ref, pot_rim, out_ref = refs[8:]
    for side in range(2):
        for field in range(2):
            for dest in range(PEERS):
                rows = pl.ds(field * K + dest * PER, PER)
                old, rim = olds[side][rows, :], rims[side][rows, :]
                if side == 0 and field == 0:
                    rim = rim + pot_rim[rows, :]
                flow = flux(edge_ref, side, field, rim, old, pasts[side][rows, :])
                if side == 0 and field == 1:
                    flow = edge_ref[0, pl.ds(3, 1), :] * flow
                    out_ref[dest, 4] = old
                out_ref[dest, 2 * side + field] = parts[side][rows, :] + flow


def swaps():
    spot = lambda g: (g % 16) * 16 + g // 16
    inner, outer = [], []
    for g in range(255):
        (inner if g % 2 == 0 else outer).extend([(spot(g), spot(g + 1)), (spot(g + 1), spot(g))])
    slab = [pair for pair in outer if pair[0] % 16 != pair[1] % 16]
    return inner, outer, slab


def on_device(pot, vel, diffusivity, *factors):
    shape = jax.ShapeDtypeStruct
    modes = lax.axis_index("modes").astype(jnp.int32)
    place = jnp.stack([modes % 2, 2 * modes])
    inner_pairs, outer_pairs, slab_pairs = swaps()
    table = jnp.asarray(tables())
    wide = shape((PEERS, 5, PER, NR), F32)
    plane = shape((2 * K, NR), F32)
    tiles = shape((2, 2, 8, NR), F32)
    staging = [pltpu.VMEM((2, 32 * PER, NR), F32), pltpu.SemaphoreType.DMA((2, PER // CHUNK))]

    def swap(planes, pairs=outer_pairs):
        return [lax.ppermute(planes[0], AXES, pairs), lax.ppermute(planes[1], AXES, inner_pairs)]

    flat = [a.reshape(-1, NR) for a in (pot, vel)]
    (sent,) = moved(pack_kernel, [wide], flat, (pltpu.HBM, pltpu.VMEM), staging)
    sent, place = lax.optimization_barrier((sent, place))
    got = lax.all_to_all(sent, "modes", split_axis=0, concat_axis=0, tiled=True)
    got, place, diffusivity, table = lax.optimization_barrier((got, place, diffusivity, table))
    *start, pot_rim, beyond = call(
        split_kernel,
        [shape((2 * K + rows, NR), F32) for rows in (8, 16)] + [shape((K + 8, NR), F32), shape((K, NR), F32)],
        [place, got, diffusivity],
        0,
        smem=1,
    )
    near_pairs = [pair for pair in outer_pairs if pair not in slab_pairs]
    rims = [
        lax.ppermute(pot_rim, AXES, near_pairs),
        lax.ppermute(start[0], AXES, slab_pairs),
        beyond,
        lax.ppermute(start[1], AXES, inner_pairs),
    ]
    start, factors = lax.optimization_barrier((start, factors))
    factor, coef = call(
        factor_kernel,
        [shape((4, 2, K, NR), F32), tiles],
        [place, diffusivity] + [f.reshape(-1, NR) for f in factors],
        0,
        smem=1,
    )
    shared = [factor, table, coef]
    flops = 1 << 34
    parts = call(first_kernel, [plane] * 2, [*start, *shared], flops)
    olds, pasts = start, []
    for step in range(1, STEPS):
        coming = swap(parts, outer_pairs if step < STEPS - 1 else slab_pairs)
        if step == STEPS - 1:
            pot_rim = lax.ppermute(parts[0][:K], AXES, near_pairs)
        outs = call(
            functools.partial(next_kernel, step == 1),
            [plane] * 6 + ([shape((2, 8, NR), F32)] if step == 1 else []),
            [*parts, *olds, *rims, *pasts, *shared],
            flops,
        )
        parts, olds = outs[:2], outs[2:4]
        edge = outs[6] if step == 1 else edge
        pasts, rims = [*outs[4:6], edge], coming
    (sent,) = call(last_kernel, [wide], [*parts, *olds, *rims, *pasts, pot_rim], 0)
    got = lax.all_to_all(sent, "modes", split_axis=0, concat_axis=0, tiled=True)
    outs = moved(unpack_kernel, [shape((32 * PER, NR), F32)] * 2, [got], (pltpu.VMEM, pltpu.HBM), staging)
    return tuple(a.reshape(PER, 32, NR) for a in outs)


def solution(mesh):
    whole = P(None, ("axial", "modes"), None)
    modal = P("modes", "axial", None)
    return jax.shard_map(
        on_device,
        mesh=mesh,
        in_specs=(modal, modal, P("axial", None), whole, whole, whole, whole),
        out_specs=(modal, modal),
        check_vma=False,
    )
```

```python
import functools
import math

import jax
import jax.numpy as jnp
import numpy as np
from jax import lax
from jax.experimental import pallas as pl
from jax.experimental.pallas import tpu as pltpu
from jax.sharding import PartitionSpec as P

K = 512
HALF = K // 2
NR = 128
STEPS = 4
DT = 0.1
PEERS = 16
PER = K // PEERS
CHUNK = 8
AXES = ("modes", "axial")
VMEM_BYTES = 24 * 1024 * 1024
F32 = jnp.float32
BF16 = jnp.bfloat16


def tables():
    idx = np.arange(HALF)

    def cas(rows):
        angle = 2.0 * np.pi / K * ((rows[:, None] * idx[None, :]) % K)
        return ((np.cos(angle) + np.sin(angle)) / math.sqrt(K)).astype(np.float32)

    def split(matrix):
        high = matrix.astype(jnp.bfloat16)
        low = (matrix - high.astype(np.float32)).astype(jnp.bfloat16)
        return np.concatenate([high, high, low], axis=1)

    even, odd = cas(2 * idx), cas(2 * idx + 1)
    return np.stack([split(even), split(odd), split(np.ascontiguousarray(odd.T))])


def call(body, out_shapes, args, flops, scratch=(), smem=0):
    space = [pl.BlockSpec(memory_space=pltpu.SMEM)] * smem
    space += [pl.BlockSpec(memory_space=pltpu.VMEM)] * (len(args) - smem)
    size = sum(math.prod(a.shape) * a.dtype.itemsize for a in list(args) + list(out_shapes))
    return pl.pallas_call(
        body,
        out_shape=out_shapes,
        in_specs=space,
        out_specs=[pl.BlockSpec(memory_space=pltpu.VMEM)] * len(out_shapes),
        scratch_shapes=scratch,
        compiler_params=pltpu.CompilerParams(vmem_limit_bytes=VMEM_BYTES),
        cost_estimate=pl.CostEstimate(flops=flops, bytes_accessed=size, transcendentals=0),
    )(*args)


def chunk_rows(chunk):
    return pl.ds(chunk * CHUNK * 32, CHUNK * 32)


def planes(sides):
    for peer in range(PEERS):
        order = (0, 1, -1) if peer % 2 == 0 else (1, 0, 2)
        for side in range(sides):
            plane = 2 * peer + order[side]
            yield peer, side, plane if 0 <= plane < 2 * PEERS else None


def pack_kernel(pot_ref, vel_ref, out_ref, rows, sems):
    arrive = [
        [
            pltpu.make_async_copy(
                ref.at[chunk_rows(chunk)], rows.at[field, chunk_rows(chunk)], sems.at[field, chunk]
            )
            for field, ref in enumerate((pot_ref, vel_ref))
        ]
        for chunk in range(PER // CHUNK)
    ]
    for pair in arrive:
        for copy in pair:
            copy.start()
    for chunk, pair in enumerate(arrive):
        for field, copy in enumerate(pair):
            copy.wait()
            for peer, side, plane in planes(2 + field):
                if plane is None:
                    piece = jnp.zeros((CHUNK, NR), F32)
                else:
                    piece = rows[field, pl.ds(chunk * CHUNK * 32 + plane, CHUNK, stride=32), :]
                out_ref[peer, 2 * side + field * (side < 2), pl.ds(chunk * CHUNK, CHUNK)] = piece


def unpack_kernel(in_ref, diff_ref, pot_ref, vel_ref, rows, sems):
    leave = []
    for chunk in range(PER // CHUNK):
        modes = pl.ds(chunk * CHUNK, CHUNK)
        for field, ref in enumerate((pot_ref, vel_ref)):
            flows = {}
            for left in range(1, PEERS - 1, 2):
                pair = diff_ref[pl.ds(2 * left + 1, 1), :] + diff_ref[pl.ds(2 * left + 2, 1), :]
                coef = DT * 0.5 * pair if field == 0 else DT
                flow = coef * (in_ref[left + 1, 4 + field, modes] - in_ref[left, 4 + field, modes])
                flows[left], flows[left + 1] = flow, -flow
            for peer, side, plane in planes(2):
                value = in_ref[peer, 2 * side + field, modes]
                if side == 0 and peer in flows:
                    value = value + flows[peer]
                rows[field, pl.ds(chunk * CHUNK * 32 + plane, CHUNK, stride=32), :] = value
            leave.append(
                pltpu.make_async_copy(
                    rows.at[field, chunk_rows(chunk)], ref.at[chunk_rows(chunk)], sems.at[field, chunk]
                )
            )
            leave[-1].start()
    for copy in leave:
        copy.wait()


def moved(body, out_shapes, args, spaces, scratch):
    if spaces[0] == pltpu.HBM:
        args = [pltpu.with_memory_space_constraint(a, pltpu.HBM) for a in args]
    else:
        out_shapes = [pltpu.HBM(a.shape, a.dtype) for a in out_shapes]
    return pl.pallas_call(
        body,
        out_shape=out_shapes,
        in_specs=[pl.BlockSpec(memory_space=spaces[0])] * len(args),
        out_specs=[pl.BlockSpec(memory_space=spaces[1])] * len(out_shapes),
        scratch_shapes=scratch,
        compiler_params=pltpu.CompilerParams(vmem_limit_bytes=VMEM_BYTES),
        cost_estimate=pl.CostEstimate(flops=0, bytes_accessed=1 << 21, transcendentals=0),
    )(*args)


def split_kernel(core_ref, in_ref, diff_ref, outer, inner, pot_rim, beyond):
    row = lax.broadcasted_iota(jnp.int32, (8, NR), 0)
    for side, out in enumerate((outer, inner)):
        own = jnp.broadcast_to(near(core_ref, diff_ref, side), (8, NR))
        own = jnp.where(row == 0, own, 1.0)
        out[pl.ds(2 * K, 8), :] = own
        if side == 0:
            pot_rim[pl.ds(K, 8), :] = own
        else:
            out[pl.ds(2 * K + 8, 8), :] = own
        for src in range(PEERS):
            for field in range(2):
                piece = in_ref[src, 2 * side + field]
                out[pl.ds(field * K + src * PER, PER), :] = piece
                if side == 0 and field == 0:
                    pot_rim[pl.ds(src * PER, PER), :] = piece
    for src in range(PEERS):
        beyond[pl.ds(src * PER, PER), :] = in_ref[src, 4]


def near(core_ref, diff_ref, side):
    plane = core_ref[1] + (core_ref[0] if side == 0 else 1 - core_ref[0])
    return diff_ref[pl.ds(plane, 1), :]


def factor_kernel(core_ref, diff_ref, *refs):
    ins, out_ref, coef_ref = refs[:4], refs[4], refs[5]
    core = core_ref[0]
    for which, ref in enumerate(ins):
        for parity in range(2):
            rows = pl.ds(parity * HALF, HALF)
            for side, plane in enumerate((core, 1 - core)):
                out_ref[which, side, rows, :] = ref[pl.ds(2 * parity + plane, HALF, stride=4), :] * DT
    tile = (8, NR)
    cell = lax.broadcasted_iota(jnp.int32, tile, 1)
    row = lax.broadcasted_iota(jnp.int32, tile, 0)
    face_radius = (cell + NR).astype(F32)
    radius = face_radius + 0.5
    values = [jnp.broadcast_to(near(core_ref, diff_ref, side), tile) for side in range(2)]
    for field in range(2):
        for side in range(2):
            own = values[side] if field == 0 else jnp.ones(tile, F32)
            middle = 0.5 * (values[0] + values[1]) if field == 0 else own
            face = jnp.where(cell > 0, 0.5 * (pltpu.roll(own, 1, 1) + own) * face_radius, 0.0)
            ahead = pltpu.roll(face, NR - 1, 1)
            terms = (
                1.0 - DT * ((ahead + face) / radius + middle),
                DT * own / (radius * radius),
                DT * ahead / (radius + 1.0),
                DT * face / (radius - 1.0),
                DT * middle,
            )
            total = jnp.zeros(tile, F32)
            for at, term in enumerate(terms):
                total = jnp.where(row == at, term, total)
            coef_ref[side, field] = total


def stacked(value):
    high = value.astype(BF16)
    low = (value - high.astype(F32)).astype(BF16)
    return jnp.concatenate([high, low, high], axis=0)


def product(table, value):
    return jnp.dot(table, stacked(value), preferred_element_type=F32)


def flux(edge_ref, side, field, rim, value, past):
    edge = lambda row: edge_ref[side, pl.ds(row, 1), :]
    beyond = rim if past is None else edge(2) * (rim - past)
    return edge(field) * (beyond - value)


def field_rows(field):
    return pl.ds(field * K, K)


def first_kernel(outer, inner, factor_ref, table_ref, coef_ref, out_outer, out_inner):
    step_alone((outer, inner), factor_ref, table_ref, coef_ref, (out_outer, out_inner))


def next_kernel(opening, *refs):
    refs = list(refs)
    take = lambda n: [refs.pop(0) for _ in range(n)]
    parts, olds = take(2), take(2)
    if opening:
        pot_rim, slab_rim, beyond, inner_rim = take(4)
        comings = [
            [slab_rim[field_rows(0), :] + pot_rim[pl.ds(0, K), :], slab_rim[field_rows(1), :] + beyond[...]],
            [inner_rim[field_rows(field), :] for field in range(2)],
        ]
        ends = pl.ds(2 * K, 8)
        others = [slab_rim[ends, :] + pot_rim[pl.ds(K, 8), :], inner_rim[ends, :]]
    else:
        rims, pasts, (edge_ref,) = take(2), take(2), take(1)
        comings = [[rim[field_rows(field), :] for field in range(2)] for rim in rims]
    factor_ref, table_ref, coef_ref = take(3)
    outs, fulls, fluxes = take(2), take(2), take(2)
    if opening:
        (edge_ref,) = take(1)
        for side in range(2):
            own, other = olds[side][pl.ds(2 * K, 8), :], others[side]
            row = lax.broadcasted_iota(jnp.int32, (8, NR), 0)
            other = jnp.where(row < 2, DT * 0.5 * (own + other), other)
            edge_ref[side] = jnp.where(row == 3, 1.0 - pot_rim[pl.ds(K, 8), :], other)
    for side in range(2):
        for field in range(2):
            rows = field_rows(field)
            past = None if opening else pasts[side][rows, :]
            flow = flux(edge_ref, side, field, comings[side][field], olds[side][rows, :], past)
            fluxes[side][rows, :] = flow
            fulls[side][rows, :] = parts[side][rows, :] + flow
    step_alone(fulls, factor_ref, table_ref, coef_ref, outs)


def step_alone(sides, factor_ref, table_ref, coef_ref, outs):
    spans = [[pl.ds(field * K + half * HALF, HALF) for half in range(2)] for field in range(2)]
    for side, (ref, out_ref) in enumerate(zip(sides, outs)):
        low, high = (
            jnp.concatenate([ref[spans[0][half], :], ref[spans[1][half], :]], axis=1)
            for half in range(2)
        )
        terms = []
        for parity, mixed in enumerate((low + high, low - high)):
            spatial = product(table_ref[parity], mixed)
            pot, vel = spatial[:, :NR], spatial[:, NR:]
            rows = pl.ds(parity * HALF, HALF)
            terms.append(
                jnp.concatenate(
                    [
                        factor_ref[0, side, rows, :] * pot + factor_ref[1, side, rows, :] * vel,
                        factor_ref[2, side, rows, :] * pot + factor_ref[3, side, rows, :] * vel,
                    ],
                    axis=1,
                )
            )
        even = product(table_ref[0], terms[0])
        odd = product(table_ref[2], terms[1])
        back = (even + odd, even - odd)
        other = sides[1 - side]
        for half in range(2):
            k = lax.broadcasted_iota(jnp.int32, (HALF, NR), 0) + half * HALF
            mode = jnp.minimum(k, K - k).astype(F32)
            mode_sq = mode * mode
            for field in range(2):
                rows = spans[field][half]
                value = ref[rows, :]
                coef = lambda row: coef_ref[side, field, pl.ds(row, 1), :]
                out_ref[rows, :] = (
                    (coef(0) - coef(1) * mode_sq) * value
                    + coef(2) * pltpu.roll(value, NR - 1, 1)
                    + coef(3) * pltpu.roll(value, 1, 1)
                    + coef(4) * other[rows, :]
                    + back[half][:, field * NR : (field + 1) * NR]
                )


def last_kernel(*refs):
    parts, olds, rims, pasts = (refs[i : i + 2] for i in range(0, 8, 2))
    edge_ref, out_ref = refs[8:]
    for side in range(2):
        for field in range(2):
            for dest in range(PEERS):
                rows = pl.ds(field * K + dest * PER, PER)
                old = olds[side][rows, :]
                flow = flux(edge_ref, side, field, rims[side][rows, :], old, pasts[side][rows, :])
                if side == 0:
                    flow = edge_ref[0, pl.ds(3, 1), :] * flow
                    out_ref[dest, 4 + field] = old
                out_ref[dest, 2 * side + field] = parts[side][rows, :] + flow


def swaps():
    spot = lambda g: (g % 16) * 16 + g // 16
    inner, outer = [], []
    for g in range(255):
        (inner if g % 2 == 0 else outer).extend([(spot(g), spot(g + 1)), (spot(g + 1), spot(g))])
    slab = [pair for pair in outer if pair[0] % 16 != pair[1] % 16]
    return inner, outer, slab


def on_device(pot, vel, diffusivity, *factors):
    shape = jax.ShapeDtypeStruct
    modes = lax.axis_index("modes").astype(jnp.int32)
    place = jnp.stack([modes % 2, 2 * modes])
    inner_pairs, outer_pairs, slab_pairs = swaps()
    table = jnp.asarray(tables())
    wide = shape((PEERS, 5, PER, NR), F32)
    plane = shape((2 * K, NR), F32)
    tiles = shape((2, 2, 8, NR), F32)
    staging = [pltpu.VMEM((2, 32 * PER, NR), F32), pltpu.SemaphoreType.DMA((2, PER // CHUNK))]

    def swap(planes, pairs=outer_pairs):
        return [lax.ppermute(planes[0], AXES, pairs), lax.ppermute(planes[1], AXES, inner_pairs)]

    flat = [a.reshape(-1, NR) for a in (pot, vel)]
    (sent,) = moved(pack_kernel, [wide], flat, (pltpu.HBM, pltpu.VMEM), staging)
    sent, place = lax.optimization_barrier((sent, place))
    got = lax.all_to_all(sent, "modes", split_axis=0, concat_axis=0, tiled=True)
    got, place, diffusivity, table = lax.optimization_barrier((got, place, diffusivity, table))
    *start, pot_rim, beyond = call(
        split_kernel,
        [shape((2 * K + rows, NR), F32) for rows in (8, 16)] + [shape((K + 8, NR), F32), shape((K, NR), F32)],
        [place, got, diffusivity],
        0,
        smem=1,
    )
    rims = [
        lax.ppermute(pot_rim, AXES, [pair for pair in outer_pairs if pair not in slab_pairs]),
        lax.ppermute(start[0], AXES, slab_pairs),
        beyond,
        lax.ppermute(start[1], AXES, inner_pairs),
    ]
    start, factors = lax.optimization_barrier((start, factors))
    factor, coef = call(
        factor_kernel,
        [shape((4, 2, K, NR), F32), tiles],
        [place, diffusivity] + [f.reshape(-1, NR) for f in factors],
        0,
        smem=1,
    )
    shared = [factor, table, coef]
    flops = 1 << 34
    parts = call(first_kernel, [plane] * 2, [*start, *shared], flops)
    olds, pasts = start, []
    for step in range(1, STEPS):
        coming = swap(parts, outer_pairs if step < STEPS - 1 else slab_pairs)
        outs = call(
            functools.partial(next_kernel, step == 1),
            [plane] * 6 + ([shape((2, 8, NR), F32)] if step == 1 else []),
            [*parts, *olds, *rims, *pasts, *shared],
            flops,
        )
        parts, olds = outs[:2], outs[2:4]
        edge = outs[6] if step == 1 else edge
        pasts, rims = [*outs[4:6], edge], coming
    (sent,) = call(last_kernel, [shape((PEERS, 6, PER, NR), F32)], [*parts, *olds, *rims, *pasts], 0)
    got = lax.all_to_all(sent, "modes", split_axis=0, concat_axis=0, tiled=True)
    outs = moved(unpack_kernel, [shape((32 * PER, NR), F32)] * 2, [got, diffusivity], (pltpu.VMEM, pltpu.HBM), staging)
    return tuple(a.reshape(PER, 32, NR) for a in outs)


def solution(mesh):
    whole = P(None, ("axial", "modes"), None)
    modal = P("modes", "axial", None)
    return jax.shard_map(
        on_device,
        mesh=mesh,
        in_specs=(modal, modal, P("axial", None), whole, whole, whole, whole),
        out_specs=(modal, modal),
        check_vma=False,
    )
```

```python
import functools
import math

import jax
import jax.numpy as jnp
import numpy as np
from jax import lax
from jax.experimental import pallas as pl
from jax.experimental.pallas import tpu as pltpu
from jax.sharding import PartitionSpec as P

K = 512
HALF = K // 2
NR = 128
STEPS = 4
DT = 0.1
PEERS = 16
PER = K // PEERS
CHUNK = 8
AXES = ("modes", "axial")
VMEM_BYTES = 24 * 1024 * 1024
F32 = jnp.float32
BF16 = jnp.bfloat16


def tables():
    idx = np.arange(HALF)

    def cas(rows):
        angle = 2.0 * np.pi / K * ((rows[:, None] * idx[None, :]) % K)
        return ((np.cos(angle) + np.sin(angle)) / math.sqrt(K)).astype(np.float32)

    def split(matrix):
        high = matrix.astype(jnp.bfloat16)
        low = (matrix - high.astype(np.float32)).astype(jnp.bfloat16)
        return np.concatenate([high, high, low], axis=1)

    even, odd = cas(2 * idx), cas(2 * idx + 1)
    return np.stack([split(even), split(odd), split(np.ascontiguousarray(odd.T))])


def call(body, out_shapes, args, flops, scratch=(), smem=0):
    space = [pl.BlockSpec(memory_space=pltpu.SMEM)] * smem
    space += [pl.BlockSpec(memory_space=pltpu.VMEM)] * (len(args) - smem)
    size = sum(math.prod(a.shape) * a.dtype.itemsize for a in list(args) + list(out_shapes))
    return pl.pallas_call(
        body,
        out_shape=out_shapes,
        in_specs=space,
        out_specs=[pl.BlockSpec(memory_space=pltpu.VMEM)] * len(out_shapes),
        scratch_shapes=scratch,
        compiler_params=pltpu.CompilerParams(vmem_limit_bytes=VMEM_BYTES),
        cost_estimate=pl.CostEstimate(flops=flops, bytes_accessed=size, transcendentals=0),
    )(*args)


def chunk_rows(chunk):
    return pl.ds(chunk * CHUNK * 32, CHUNK * 32)


def planes(sides):
    for peer in range(PEERS):
        order = (0, 1, -1) if peer % 2 == 0 else (1, 0, 2)
        for side in range(sides):
            plane = 2 * peer + order[side]
            yield peer, side, plane if 0 <= plane < 2 * PEERS else None


def pack_kernel(pot_ref, vel_ref, out_ref, rows, sems):
    arrive = [
        [
            pltpu.make_async_copy(
                ref.at[chunk_rows(chunk)], rows.at[field, chunk_rows(chunk)], sems.at[field, chunk]
            )
            for field, ref in enumerate((pot_ref, vel_ref))
        ]
        for chunk in range(PER // CHUNK)
    ]
    for pair in arrive:
        for copy in pair:
            copy.start()
    for chunk, pair in enumerate(arrive):
        for field, copy in enumerate(pair):
            copy.wait()
            for peer, side, plane in planes(2 + field):
                if plane is None:
                    piece = jnp.zeros((CHUNK, NR), F32)
                else:
                    piece = rows[field, pl.ds(chunk * CHUNK * 32 + plane, CHUNK, stride=32), :]
                out_ref[peer, 2 * side + field * (side < 2), pl.ds(chunk * CHUNK, CHUNK)] = piece


def unpack_kernel(in_ref, diff_ref, pot_ref, vel_ref, rows, sems):
    leave = []
    for chunk in range(PER // CHUNK):
        modes = pl.ds(chunk * CHUNK, CHUNK)
        for field, ref in enumerate((pot_ref, vel_ref)):
            flows = {}
            for left in range(1, PEERS - 1, 2):
                pair = diff_ref[pl.ds(2 * left + 1, 1), :] + diff_ref[pl.ds(2 * left + 2, 1), :]
                coef = DT * 0.5 * pair if field == 0 else DT
                flow = coef * (in_ref[left + 1, 4 + field, modes] - in_ref[left, 4 + field, modes])
                flows[left], flows[left + 1] = flow, -flow
            for peer, side, plane in planes(2):
                value = in_ref[peer, 2 * side + field, modes]
                if side == 0 and peer in flows:
                    value = value + flows[peer]
                rows[field, pl.ds(chunk * CHUNK * 32 + plane, CHUNK, stride=32), :] = value
            leave.append(
                pltpu.make_async_copy(
                    rows.at[field, chunk_rows(chunk)], ref.at[chunk_rows(chunk)], sems.at[field, chunk]
                )
            )
            leave[-1].start()
    for copy in leave:
        copy.wait()


def moved(body, out_shapes, args, spaces, scratch):
    if spaces[0] == pltpu.HBM:
        args = [pltpu.with_memory_space_constraint(a, pltpu.HBM) for a in args]
    else:
        out_shapes = [pltpu.HBM(a.shape, a.dtype) for a in out_shapes]
    return pl.pallas_call(
        body,
        out_shape=out_shapes,
        in_specs=[pl.BlockSpec(memory_space=spaces[0])] * len(args),
        out_specs=[pl.BlockSpec(memory_space=spaces[1])] * len(out_shapes),
        scratch_shapes=scratch,
        compiler_params=pltpu.CompilerParams(vmem_limit_bytes=VMEM_BYTES),
        cost_estimate=pl.CostEstimate(flops=0, bytes_accessed=1 << 21, transcendentals=0),
    )(*args)


def split_kernel(core_ref, in_ref, diff_ref, outer, inner, pot_rim, beyond):
    row = lax.broadcasted_iota(jnp.int32, (8, NR), 0)
    for side, out in enumerate((outer, inner)):
        own = jnp.broadcast_to(near(core_ref, diff_ref, side), (8, NR))
        own = jnp.where(row == 0, own, 1.0)
        out[pl.ds(2 * K, 8), :] = own
        if side == 0:
            pot_rim[pl.ds(K, 8), :] = own
            out[pl.ds(2 * K + 8, 8), :] = own
        for src in range(PEERS):
            for field in range(2):
                piece = in_ref[src, 2 * side + field]
                out[pl.ds(field * K + src * PER, PER), :] = piece
                if side == 0 and field == 0:
                    pot_rim[pl.ds(src * PER, PER), :] = piece
    for src in range(PEERS):
        beyond[pl.ds(src * PER, PER), :] = in_ref[src, 4]


def near(core_ref, diff_ref, side):
    plane = core_ref[1] + (core_ref[0] if side == 0 else 1 - core_ref[0])
    return diff_ref[pl.ds(plane, 1), :]


def factor_kernel(core_ref, diff_ref, *refs):
    ins, out_ref, coef_ref = refs[:4], refs[4], refs[5]
    core = core_ref[0]
    for which, ref in enumerate(ins):
        for parity in range(2):
            rows = pl.ds(parity * HALF, HALF)
            for side, plane in enumerate((core, 1 - core)):
                out_ref[which, side, rows, :] = ref[pl.ds(2 * parity + plane, HALF, stride=4), :] * DT
    tile = (8, NR)
    cell = lax.broadcasted_iota(jnp.int32, tile, 1)
    row = lax.broadcasted_iota(jnp.int32, tile, 0)
    face_radius = (cell + NR).astype(F32)
    radius = face_radius + 0.5
    values = [jnp.broadcast_to(near(core_ref, diff_ref, side), tile) for side in range(2)]
    for field in range(2):
        for side in range(2):
            own = values[side] if field == 0 else jnp.ones(tile, F32)
            middle = 0.5 * (values[0] + values[1]) if field == 0 else own
            face = jnp.where(cell > 0, 0.5 * (pltpu.roll(own, 1, 1) + own) * face_radius, 0.0)
            ahead = pltpu.roll(face, NR - 1, 1)
            terms = (
                1.0 - DT * ((ahead + face) / radius + middle),
                DT * own / (radius * radius),
                DT * ahead / (radius + 1.0),
                DT * face / (radius - 1.0),
                DT * middle,
            )
            total = jnp.zeros(tile, F32)
            for at, term in enumerate(terms):
                total = jnp.where(row == at, term, total)
            coef_ref[side, field] = total


def stacked(value):
    high = value.astype(BF16)
    low = (value - high.astype(F32)).astype(BF16)
    return jnp.concatenate([high, low, high], axis=0)


def product(table, value):
    return jnp.dot(table, stacked(value), preferred_element_type=F32)


def flux(edge_ref, side, field, rim, value, past):
    edge = lambda row: edge_ref[side, pl.ds(row, 1), :]
    beyond = rim if past is None else edge(2) * (rim - past)
    return edge(field) * (beyond - value)


def field_rows(field):
    return pl.ds(field * K, K)


def first_kernel(outer, inner, factor_ref, table_ref, coef_ref, out_outer, out_inner):
    step_alone((outer, inner), factor_ref, table_ref, coef_ref, (out_outer, out_inner))


def next_kernel(opening, *refs):
    refs = list(refs)
    take = lambda n: [refs.pop(0) for _ in range(n)]
    parts, olds = take(2), take(2)
    if opening:
        pot_rim, slab_rim, beyond, inner_rim = take(4)
        comings = [
            [slab_rim[field_rows(0), :] + pot_rim[pl.ds(0, K), :], slab_rim[field_rows(1), :] + beyond[...]],
            [inner_rim[field_rows(field), :] for field in range(2)],
        ]
        ends = pl.ds(2 * K, 8)
        others = [slab_rim[ends, :] + pot_rim[pl.ds(K, 8), :], inner_rim[ends, :]]
    else:
        rims, pasts, (edge_ref,) = take(2), take(2), take(1)
        comings = [[rim[field_rows(field), :] for field in range(2)] for rim in rims]
    factor_ref, table_ref, coef_ref = take(3)
    outs, fulls, fluxes = take(2), take(2), take(2)
    if opening:
        (edge_ref,) = take(1)
        for side in range(2):
            own, other = olds[side][pl.ds(2 * K, 8), :], others[side]
            row = lax.broadcasted_iota(jnp.int32, (8, NR), 0)
            other = jnp.where(row < 2, DT * 0.5 * (own + other), other)
            edge_ref[side] = jnp.where(row == 3, 1.0 - pot_rim[pl.ds(K, 8), :], other)
    for side in range(2):
        for field in range(2):
            rows = field_rows(field)
            past = None if opening else pasts[side][rows, :]
            flow = flux(edge_ref, side, field, comings[side][field], olds[side][rows, :], past)
            fluxes[side][rows, :] = flow
            fulls[side][rows, :] = parts[side][rows, :] + flow
    step_alone(fulls, factor_ref, table_ref, coef_ref, outs)


def step_alone(sides, factor_ref, table_ref, coef_ref, outs):
    spans = [[pl.ds(field * K + half * HALF, HALF) for half in range(2)] for field in range(2)]
    for side, (ref, out_ref) in enumerate(zip(sides, outs)):
        low, high = (
            jnp.concatenate([ref[spans[0][half], :], ref[spans[1][half], :]], axis=1)
            for half in range(2)
        )
        terms = []
        for parity, mixed in enumerate((low + high, low - high)):
            spatial = product(table_ref[parity], mixed)
            pot, vel = spatial[:, :NR], spatial[:, NR:]
            rows = pl.ds(parity * HALF, HALF)
            terms.append(
                jnp.concatenate(
                    [
                        factor_ref[0, side, rows, :] * pot + factor_ref[1, side, rows, :] * vel,
                        factor_ref[2, side, rows, :] * pot + factor_ref[3, side, rows, :] * vel,
                    ],
                    axis=1,
                )
            )
        even = product(table_ref[0], terms[0])
        odd = product(table_ref[2], terms[1])
        back = (even + odd, even - odd)
        other = sides[1 - side]
        for half in range(2):
            k = lax.broadcasted_iota(jnp.int32, (HALF, NR), 0) + half * HALF
            mode = jnp.minimum(k, K - k).astype(F32)
            mode_sq = mode * mode
            for field in range(2):
                rows = spans[field][half]
                value = ref[rows, :]
                coef = lambda row: coef_ref[side, field, pl.ds(row, 1), :]
                out_ref[rows, :] = (
                    (coef(0) - coef(1) * mode_sq) * value
                    + coef(2) * pltpu.roll(value, NR - 1, 1)
                    + coef(3) * pltpu.roll(value, 1, 1)
                    + coef(4) * other[rows, :]
                    + back[half][:, field * NR : (field + 1) * NR]
                )


def last_kernel(*refs):
    parts, olds, rims, pasts = (refs[i : i + 2] for i in range(0, 8, 2))
    edge_ref, out_ref = refs[8:]
    for side in range(2):
        for field in range(2):
            for dest in range(PEERS):
                rows = pl.ds(field * K + dest * PER, PER)
                old = olds[side][rows, :]
                flow = flux(edge_ref, side, field, rims[side][rows, :], old, pasts[side][rows, :])
                if side == 0:
                    flow = edge_ref[0, pl.ds(3, 1), :] * flow
                    out_ref[dest, 4 + field] = old
                out_ref[dest, 2 * side + field] = parts[side][rows, :] + flow


def swaps():
    spot = lambda g: (g % 16) * 16 + g // 16
    inner, outer = [], []
    for g in range(255):
        (inner if g % 2 == 0 else outer).extend([(spot(g), spot(g + 1)), (spot(g + 1), spot(g))])
    slab = [pair for pair in outer if pair[0] % 16 != pair[1] % 16]
    return inner, outer, slab


def on_device(pot, vel, diffusivity, *factors):
    shape = jax.ShapeDtypeStruct
    modes = lax.axis_index("modes").astype(jnp.int32)
    place = jnp.stack([modes % 2, 2 * modes])
    inner_pairs, outer_pairs, slab_pairs = swaps()
    table = jnp.asarray(tables())
    wide = shape((PEERS, 5, PER, NR), F32)
    plane = shape((2 * K, NR), F32)
    tiles = shape((2, 2, 8, NR), F32)
    staging = [pltpu.VMEM((2, 32 * PER, NR), F32), pltpu.SemaphoreType.DMA((2, PER // CHUNK))]

    def swap(planes, pairs=outer_pairs):
        return [lax.ppermute(planes[0], AXES, pairs), lax.ppermute(planes[1], AXES, inner_pairs)]

    flat = [a.reshape(-1, NR) for a in (pot, vel)]
    (sent,) = moved(pack_kernel, [wide], flat, (pltpu.HBM, pltpu.VMEM), staging)
    sent, place = lax.optimization_barrier((sent, place))
    got = lax.all_to_all(sent, "modes", split_axis=0, concat_axis=0, tiled=True)
    got, place, diffusivity, table = lax.optimization_barrier((got, place, diffusivity, table))
    *start, pot_rim, beyond = call(
        split_kernel,
        [shape((2 * K + rows, NR), F32) for rows in (16, 8)] + [shape((K + 8, NR), F32), shape((K, NR), F32)],
        [place, got, diffusivity],
        0,
        smem=1,
    )
    rims = [
        lax.ppermute(pot_rim, AXES, [pair for pair in outer_pairs if pair not in slab_pairs]),
        lax.ppermute(start[0], AXES, slab_pairs),
        beyond,
        lax.ppermute(start[1], AXES, inner_pairs),
    ]
    start, factors = lax.optimization_barrier((start, factors))
    factor, coef = call(
        factor_kernel,
        [shape((4, 2, K, NR), F32), tiles],
        [place, diffusivity] + [f.reshape(-1, NR) for f in factors],
        0,
        smem=1,
    )
    shared = [factor, table, coef]
    flops = 1 << 34
    parts = call(first_kernel, [plane] * 2, [*start, *shared], flops)
    olds, pasts = start, []
    for step in range(1, STEPS):
        coming = swap(parts, outer_pairs if step < STEPS - 1 else slab_pairs)
        outs = call(
            functools.partial(next_kernel, step == 1),
            [plane] * 6 + ([shape((2, 8, NR), F32)] if step == 1 else []),
            [*parts, *olds, *rims, *pasts, *shared],
            flops,
        )
        parts, olds = outs[:2], outs[2:4]
        edge = outs[6] if step == 1 else edge
        pasts, rims = [*outs[4:6], edge], coming
    (sent,) = call(last_kernel, [shape((PEERS, 6, PER, NR), F32)], [*parts, *olds, *rims, *pasts], 0)
    got = lax.all_to_all(sent, "modes", split_axis=0, concat_axis=0, tiled=True)
    outs = moved(unpack_kernel, [shape((32 * PER, NR), F32)] * 2, [got, diffusivity], (pltpu.VMEM, pltpu.HBM), staging)
    return tuple(a.reshape(PER, 32, NR) for a in outs)


def solution(mesh):
    whole = P(None, ("axial", "modes"), None)
    modal = P("modes", "axial", None)
    return jax.shard_map(
        on_device,
        mesh=mesh,
        in_specs=(modal, modal, P("axial", None), whole, whole, whole, whole),
        out_specs=(modal, modal),
        check_vma=False,
    )
```
